32 devices in a mesh: space: 16 (over z, y, x), sens: 2 (over core).
Axes of the slice: x: 2, y: 2, z: 4, core: 2. Of those that a mesh axis runs over, the one named last changes fastest.
Arguments:
- adjoint_end: float32 [16, 64, 64, 128], P('sens', 'space'), may hold values from -6 to 6
- checkpoints: float32 [8, 64, 64, 128], P('sens', 'space'), may hold values from 0.5 to 2
- dispersion: float32 [6, 64, 64, 128], P(None, 'space', 'sens'), as said below
- owner_steps: int32 [3], replicated, may hold values from 0 to 7, as said below
- sensor_cells: int32 [16], P('sens'), may hold values from 0 to 524287
- misfit: float32 [16, 3], P('sens'), may hold values from -6 to 6
- release_cells: int32 [128], replicated, may hold values from 0 to 524287
- release_steps: int32 [128], replicated, may hold values from 0 to 2
Outputs:
- adjoint: float32 [16, 64, 64, 128], P('sens', 'space')
- release_grad: float32 [16, 128], P('sens')
The draws below stay inside these ranges and needn't reach their ends.
Inputs may be any that keep to these rules, and one draw needn't show every extreme that they name: `owner_steps`: the entries are different stored states; the first and the last stored state are always among them. `sensor_cells`: flat cell indices. `release_cells`: flat cell indices. `dispersion`: zz, yy and xx components are positive.
All inputs are finite; a program needn't handle non-finite values.
Results may differ from the reference program's by a relative error of at most 0.00002.
Values sent between devices are 32-bit elements; how exact they have to be, the bound alone decides.
No kernel may reach another device: no remote copies, remote signals or barrier semaphores. Data moves between devices by JAX's collectives and lax.ppermute only.
A program may use at most 128 MiB of HBM per device.

```python
import math
import jax
import jax.numpy as jnp
from jax import lax

NY = 64
NX = 128
SENSORS = 16
STEPS = 3
RELEASES = 128
NZ = 64
CKPTS = 8


def draw_dispersion(key, part):
    key_diag = jax.random.fold_in(key, 11)
    key_cross = jax.random.fold_in(key, 12)
    diag = jnp.exp(jax.random.uniform(key_diag, (3, NZ, NY, NX), jnp.float32, math.log(0.5), math.log(1.5)))
    cross = jax.random.uniform(key_cross, (3, NZ, NY, NX), jnp.float32, -0.25, 0.25)
    return jnp.concatenate([diag, cross], 0)


def draw_owner_steps(key, part):
    inner = 1 + jax.random.permutation(jax.random.fold_in(key, 21), CKPTS - 2).astype(jnp.int32)
    ends = jnp.array([0, CKPTS - 1], jnp.int32)
    chosen = jnp.concatenate([ends, inner[:STEPS - 2]], 0)
    order = jax.random.permutation(jax.random.fold_in(key, 22), STEPS)
    return chosen[order].astype(jnp.int32)


def place_ends(values, own_key, least, top_value):
    extent = values.shape
    spot = [jax.random.randint(jax.random.fold_in(own_key, axis), (), 0, extent[axis]) for axis in range(len(extent))]
    values = values.at[tuple(spot)].set(least)
    longest = extent.index(max(extent))
    spot[longest] = (spot[longest] + 1) % extent[longest]
    return values.at[tuple(spot)].set(top_value)


def block_levels(own_key, extent, cuts, smallest, high):
    gain, own = 1.0, jax.random.fold_in(own_key, 6)
    for axis_at, blocks in cuts:
        heights = jnp.exp(jax.random.uniform(jax.random.fold_in(own, axis_at), (blocks,), jnp.float32, smallest / len(cuts), high / len(cuts)))
        gain = gain * jnp.repeat(heights, extent[axis_at] // blocks).reshape([-1 if axis == axis_at else 1 for axis in range(len(extent))])
    return gain


def bell_draw(stream_key, dims, scale, bound, split=(), kind=jnp.bfloat16):
    loudness = block_levels(stream_key, dims, split, -0.22, 0.18) if split else 1.0
    drawn = jax.random.normal(stream_key, dims, jnp.float32) * scale * loudness
    return jnp.minimum(jnp.maximum(drawn, -bound), bound).astype(kind)


def setup_inputs(seed: int = 0) -> dict:
    splits = jax.random.split(jax.random.key(seed), 9)
    return {
        "adjoint_end": bell_draw(splits[0], (SENSORS, NZ, NY, NX), 1.0, 6.0, ((0, 2), (1, 16)), jnp.float32),
        "checkpoints": jnp.clip(0.5 + 1.5 * jax.random.uniform(splits[1], (CKPTS, NZ, NY, NX), jnp.float32) ** block_levels(splits[1], (CKPTS, NZ, NY, NX), ((0, 2), (1, 16)), -0.2, 0.2), 0.5, 2.0),
        "dispersion": draw_dispersion(jax.random.fold_in(splits[8], 71), 0),
        "owner_steps": draw_owner_steps(jax.random.fold_in(splits[8], 71), 0),
        "sensor_cells": place_ends(jax.random.randint(splits[4], (SENSORS,), 0, NZ * NY * NX), jax.random.fold_in(splits[4], 1), 0, (NZ * NY * NX) - 1).astype(jnp.int32),
        "misfit": bell_draw(splits[5], (SENSORS, STEPS), 1.0, 6.0, ((0, 2),), jnp.float32),
        "release_cells": place_ends(jax.random.randint(splits[6], (RELEASES,), 0, NZ * NY * NX), jax.random.fold_in(splits[6], 1), 0, (NZ * NY * NX) - 1).astype(jnp.int32),
        "release_steps": place_ends(jax.random.randint(splits[7], (RELEASES,), 0, STEPS), jax.random.fold_in(splits[7], 1), 0, STEPS - 1).astype(jnp.int32),
    }


step_dt = 0.12


def retard_scale(conc):
    return step_dt / (1.0 + 0.5 * conc ** (-0.5))


def retard_slope(conc):
    retard = 1.0 + 0.5 * conc ** (-0.5)
    deriv = -0.25 * conc ** (-1.5)
    return -step_dt * deriv / (retard * retard)


def apply_op(field, tensor):
    depth = field.shape[1] - 2
    rows_y = field.shape[2]
    rows_x = field.shape[3]
    padded = jnp.pad(field, ((0, 0), (0, 0), (1, 1), (1, 1)))
    coeffs = jnp.pad(tensor, ((0, 0), (0, 0), (1, 1), (1, 1)))

    def at_shift(arr, shift):
        return arr[..., 1 + shift[0]:1 + shift[0] + depth, 1 + shift[1]:1 + shift[1] + rows_y, 1 + shift[2]:1 + shift[2] + rows_x]

    units = [(1, 0, 0), (0, 1, 0), (0, 0, 1)]
    centre = (0, 0, 0)
    total = jnp.zeros((field.shape[0], depth, rows_y, rows_x), jnp.float32)
    for axis_id in range(3):
        plus = units[axis_id]
        minus = tuple(-v for v in plus)
        diag = coeffs[axis_id]
        a_plus = 0.5 * (at_shift(diag, centre) + at_shift(diag, plus))
        a_minus = 0.5 * (at_shift(diag, centre) + at_shift(diag, minus))
        total = total + a_plus * (at_shift(padded, plus) - at_shift(padded, centre))
        total = total - a_minus * (at_shift(padded, centre) - at_shift(padded, minus))
    for first, second, comp in ((0, 1, 3), (0, 2, 4), (1, 2, 5)):
        for outer, inner in ((first, second), (second, first)):
            unit_o = units[outer]
            unit_i = units[inner]
            for sign in (1, -1):
                spot = tuple(sign * v for v in unit_o)
                up_spot = tuple(spot[t] + unit_i[t] for t in range(3))
                down_spot = tuple(spot[t] - unit_i[t] for t in range(3))
                flux = at_shift(coeffs[comp], spot) * (0.5 * (at_shift(padded, up_spot) - at_shift(padded, down_spot)))
                total = total + (0.5 * sign) * flux
    return total


def zpad(arr):
    return jnp.pad(arr, ((0, 0), (1, 1), (0, 0), (0, 0)))


def reference(adjoint_end, checkpoints, dispersion, owner_steps, sensor_cells, misfit, release_cells, release_steps):
    tensor = zpad(dispersion)
    lam = adjoint_end
    shape = lam.shape
    grad = jnp.zeros((SENSORS, RELEASES), jnp.float32)
    for step in reversed(range(STEPS)):
        conc = lax.dynamic_index_in_dim(checkpoints, owner_steps[step], 0, keepdims=False)
        flat = lam.reshape(SENSORS, -1)
        flat = flat.at[jnp.arange(SENSORS, dtype=jnp.int32), sensor_cells].add(misfit[:, step])
        mixed = flat.reshape(shape)
        scale = retard_scale(conc)
        conc_term = apply_op(zpad(conc[None]), tensor)[0]

        def one_sensor(single):
            return apply_op(zpad((scale * single)[None]), tensor)[0]

        spread = lax.map(one_sensor, mixed)
        lam = mixed + spread + retard_slope(conc) * conc_term * mixed
        values = lam.reshape(SENSORS, -1)[:, release_cells]
        grad = grad + jnp.where((release_steps == step)[None, :], values, 0.0)
    return lam, grad
```

```python
import functools

import jax
import jax.numpy as jnp
from jax import lax
from jax.experimental import pallas as pl
from jax.experimental.pallas import tpu as pltpu
from jax.sharding import PartitionSpec as P

STEPS = 3
DT = 0.12
PAD = 8
TILE = 8
CENTRE, ZP, ZM, YP, YM, ZPYP, ZPYM, ZMYP, ZMYM = range(9)
XP, XPZP, XPZM, XPYP, XPYM, XM, XMZP, XMZM, XMYP, XMYM = range(9, 19)
PLANES = 19
LOW = (ZM, ZMYP, ZMYM, XPZM, XMZM)
HIGH = (ZP, ZPYP, ZPYM, XPZP, XMZP)

VMEM = pl.BlockSpec(memory_space=pltpu.VMEM)
SMEM = pl.BlockSpec(memory_space=pltpu.SMEM)
ANY = pl.BlockSpec(memory_space=pl.ANY)


def f32(*shape):
    return jax.ShapeDtypeStruct(shape, jnp.float32)


def params(mib):
    return pltpu.CompilerParams(vmem_limit_bytes=mib * 1024 * 1024)


def cost(flops, moved):
    return pl.CostEstimate(flops=flops, bytes_accessed=moved, transcendentals=0)


def owned(owner_ref, slots):
    me = lax.axis_index("sens")
    o0, o1, o2 = (owner_ref[i] for i in range(3))
    own0 = lax.div(o0, slots) == me
    own1 = lax.div(o1, slots) == me
    first = jnp.where(own0, o0, jnp.where(own1, o1, o2))
    second = jnp.where(own0 & own1, o1, o2)
    return lax.rem(first, slots), lax.rem(second, slots)


def parity():
    return lax.rem(lax.axis_index("space"), 2)


def pack_kernel(owner, adj, ckpt, disp, lam_a, lam_b, small_a, small_b, states, sems):
    depth, rows_y = adj.shape[1], adj.shape[2]
    rows = disp.shape[2]
    even = parity() == 0
    z_a = jnp.where(even, depth - 1, 0)
    z_b = jnp.where(even, 0, depth - 1)
    held = owned(owner, ckpt.shape[0])
    moves = []
    for z, small in ((z_a, small_a), (z_b, small_b)):
        for j in range(2):
            moves.append((ckpt.at[held[j], z], small.at[pl.ds(j * rows_y, rows_y)]))
        for j, comp in enumerate((0, 3, 4)):
            moves.append((disp.at[comp, z], small.at[pl.ds(2 * rows_y + j * rows, rows)]))
    for j in range(2):
        moves.append((ckpt.at[held[j]], states.at[j]))
    moves.append((adj.at[:, z_a], lam_a))
    moves.append((adj.at[:, z_b], lam_b))
    copies = [pltpu.make_async_copy(s, d, sems.at[i]) for i, (s, d) in enumerate(moves)]
    for c in copies:
        c.start()
    for c in copies:
        c.wait()


def pack(owner, adj, ckpt, disp):
    own, depth, rows_y, rows_x = adj.shape
    rows = disp.shape[2]
    small = f32(2 * rows_y + 3 * rows, rows_x)
    return pl.pallas_call(
        pack_kernel,
        in_specs=[SMEM, ANY, ANY, ANY],
        out_specs=[ANY] * 5,
        out_shape=[f32(own, rows_y, rows_x)] * 2 + [small, small, f32(2, depth, rows_y, rows_x)],
        scratch_shapes=[pltpu.SemaphoreType.DMA((14,))],
        compiler_params=params(16),
        name="pack",
    )(owner, adj, ckpt, disp)


def lane_masks(shape):
    lanes = lax.broadcasted_iota(jnp.int32, shape, len(shape) - 1)
    return lanes >= 1, lanes < shape[-1] - 1


def before(value, keep):
    return jnp.where(keep, pltpu.roll(value, 1, axis=value.ndim - 1), 0.0)


def after(value, keep):
    return jnp.where(keep, pltpu.roll(value, value.shape[-1] - 1, axis=value.ndim - 1), 0.0)


def planes_at(window, keep_b, keep_a):
    def yy(dy):
        return window(1, 0, dy)

    c = [None] * PLANES
    zz, zzp, zzm = window(0, 0, 0), window(0, 1, 0), window(0, -1, 0)
    xx = window(2, 0, 0)
    c[ZP], c[ZM] = 0.5 * (zz + zzp), 0.5 * (zz + zzm)
    c[YP], c[YM] = 0.5 * (yy(0) + yy(1)), 0.5 * (yy(0) + yy(-1))
    xx_b, xx_a = before(xx, keep_b), after(xx, keep_a)
    c[XP] = jnp.where(keep_b, 0.5 * (xx_b + xx), 0.0)
    c[XM] = jnp.where(keep_a, 0.5 * (xx_a + xx), 0.0)
    c[CENTRE] = -(c[ZP] + c[ZM] + c[YP] + c[YM] + (xx + 0.5 * (xx_a + xx_b)))
    zp, zm, yp, ym = window(3, 1, 0), window(3, -1, 0), window(3, 0, 1), window(3, 0, -1)
    c[ZPYP], c[ZPYM] = 0.25 * (zp + yp), -0.25 * (zp + ym)
    c[ZMYP], c[ZMYM] = -0.25 * (zm + yp), 0.25 * (zm + ym)
    for comp, plus, minus, names in (
        (4, window(4, 1, 0), window(4, -1, 0), (XPZP, XPZM, XMZP, XMZM)),
        (5, window(5, 0, 1), window(5, 0, -1), (XPYP, XPYM, XMYP, XMYM)),
    ):
        here = window(comp, 0, 0)
        c[names[0]] = jnp.where(keep_b, 0.25 * (before(plus, keep_b) + here), 0.0)
        c[names[1]] = jnp.where(keep_b, -0.25 * (before(minus, keep_b) + here), 0.0)
        c[names[2]] = jnp.where(keep_a, -0.25 * (after(plus, keep_a) + here), 0.0)
        c[names[3]] = jnp.where(keep_a, 0.25 * (after(minus, keep_a) + here), 0.0)
    return c


def stencil(c, u):
    near = {(dz, dy): u(dz, dy) for dz in (-1, 0, 1) for dy in (-1, 0, 1)}
    here = c[CENTRE] * near[0, 0] + c[ZP] * near[1, 0] + c[ZM] * near[-1, 0]
    here += c[YP] * near[0, 1] + c[YM] * near[0, -1]
    here += c[ZPYP] * near[1, 1] + c[ZPYM] * near[1, -1]
    here += c[ZMYP] * near[-1, 1] + c[ZMYM] * near[-1, -1]
    right = c[XP] * near[0, 0] + c[XPZP] * near[1, 0] + c[XPZM] * near[-1, 0]
    right += c[XPYP] * near[0, 1] + c[XPYM] * near[0, -1]
    left = c[XM] * near[0, 0] + c[XMZP] * near[1, 0] + c[XMZM] * near[-1, 0]
    left += c[XMYP] * near[0, 1] + c[XMYM] * near[0, -1]
    width = here.shape[-1]
    return here + pltpu.roll(right, width - 1, axis=1) + pltpu.roll(left, 1, axis=1)


def scale_of(conc):
    root = jnp.sqrt(conc)
    return DT * root / (root + 0.5)


def slope_of(conc):
    root = jnp.sqrt(conc)
    return (0.25 * DT) / (root * (root + 0.5) * (root + 0.5))


def planes_kernel(count, slot_count, *refs):
    owner, cells = refs[:2]
    parts, states = refs[2 : 2 + count], refs[2 + count : 2 + 2 * count]
    small = refs[2 + 2 * count : 2 + 3 * count], refs[2 + 3 * count : 2 + 4 * count]
    coef, edge, gain, scale, rim, inside, full, conc = refs[2 + 4 * count :]
    depth, rows_y, rows_x = coef.shape[1:]
    rows = rows_y // count
    me = lax.axis_index("sens")
    even = parity() == 0
    z_a = jnp.where(even, depth + 1, 0)
    z_b = jnp.where(even, 0, depth + 1)
    inner = pl.ds(PAD, rows_y)

    blank = jnp.zeros((PAD, rows_x), jnp.float32)
    for ref in (full, conc):
        for i in range(ref.shape[0]):
            for z in range(depth + 2):
                ref[i, z, pl.ds(0, PAD)] = blank
                ref[i, z, pl.ds(PAD + rows_y, PAD)] = blank
    for side in range(2):
        for j in range(5):
            edge[side, j, pl.ds(0, PAD)] = blank
            edge[side, j, pl.ds(PAD + rows_y, PAD)] = blank
    for k in range(count):
        who = lax.rem(me - k + count, count)
        span = pl.ds(pl.multiple_of(PAD + who * rows, PAD), rows)
        for comp in range(6):
            for z in range(depth):
                full[comp, z + 1, span] = parts[k][comp, z]
        for j, comp in enumerate((0, 3, 4)):
            here = pl.ds(2 * rows_y + j * rows, rows)
            full[comp, z_a, span] = small[0][k][here]
            full[comp, z_b, span] = small[1][k][here]
    holders = [lax.div(owner[i], slot_count) for i in range(STEPS)]
    for i in range(STEPS):
        slot = jnp.int32(0)
        for j in range(i):
            slot += jnp.where(holders[j] == holders[i], 1, 0)
        slot = jnp.minimum(slot, 1)
        turn = lax.rem(me - holders[i] + count, count)
        for k in range(count):

            @pl.when(turn == k)
            def _(i=i, k=k, slot=slot):
                conc[i, pl.ds(1, depth), inner] = states[k][slot]
                span = pl.ds(pl.multiple_of(slot * rows_y, PAD), rows_y)
                conc[i, z_a, inner] = small[0][k][span]
                conc[i, z_b, inner] = small[1][k][span]

    plane = rows_y * rows_x
    start = lax.axis_index("space") * (depth * plane)

    def note(r, found):
        local = cells[r] - start

        @pl.when((local >= -plane) & (local < (depth + 1) * plane))
        def _():
            inside[found] = r

        return found + jnp.where((local >= -plane) & (local < (depth + 1) * plane), 1, 0)

    last = inside.shape[0] - 1
    inside[last] = lax.fori_loop(0, cells.shape[0], note, jnp.int32(0))

    keep_b, keep_a = lane_masks((TILE, rows_x))

    def layer(z, carry):
        for tile in range(rows_y // TILE):
            at = pl.ds(tile * TILE, TILE)

            def window(comp, dz, dy):
                return full[comp, z + 1 + dz, pl.ds(PAD + tile * TILE + dy, TILE)]

            c = planes_at(window, keep_b, keep_a)
            for j in range(PLANES):
                coef[j, z, at] = c[j]
            for i in range(STEPS):
                here = conc[i, z + 1, pl.ds(PAD + tile * TILE, TILE)]
                spread = stencil(
                    c, lambda dz, dy: conc[i, z + 1 + dz, pl.ds(PAD + tile * TILE + dy, TILE)]
                )
                scale[i, z, at] = scale_of(here)
                gain[i, z, at] = 1.0 + slope_of(here) * spread
        return carry

    lax.fori_loop(0, depth, layer, 0)
    for side, z, names in ((0, 0, LOW), (1, depth - 1, HIGH)):
        for j in range(5):
            edge[side, j, inner] = coef[names[j], z]
        rim[side] = scale_of(conc[STEPS - 1, side * (depth + 1), inner])


def planes(owner, cells, parts, states, small_a, small_b, slot_count):
    count = len(parts)
    depth, rows_y, rows_x = states[0].shape[1:]
    grown = rows_y + 2 * PAD
    return pl.pallas_call(
        functools.partial(planes_kernel, count, slot_count),
        in_specs=[SMEM, SMEM] + [VMEM] * (4 * count),
        out_specs=[VMEM] * 5 + [SMEM],
        out_shape=[
            f32(PLANES, depth, rows_y, rows_x),
            f32(2, 5, grown, rows_x),
            f32(STEPS, depth, rows_y, rows_x),
            f32(STEPS, depth, rows_y, rows_x),
            f32(2, rows_y, rows_x),
            jax.ShapeDtypeStruct((cells.shape[0] + 1,), jnp.int32),
        ],
        scratch_shapes=[
            pltpu.VMEM((6, depth + 2, grown, rows_x), jnp.float32),
            pltpu.VMEM((STEPS, depth + 2, grown, rows_x), jnp.float32),
        ],
        compiler_params=params(24),
        cost_estimate=cost(20_000_000, 6_000_000),
        name="planes",
    )(owner, cells, *parts, *states, *small_a, *small_b)


def spot(cell, start, rows_y, rows_x):
    local = cell - start
    lifted = local + rows_y * rows_x
    z = lax.div(lifted, rows_y * rows_x) - 1
    y = lax.div(lax.rem(lifted, rows_y * rows_x), rows_x)
    return lifted, z, y, lax.rem(lifted, rows_x)


def main_kernel(step, *refs):
    first, last = step == STEPS - 1, step == 0
    refs = list(refs)
    sensors, misfit = refs.pop(0), refs.pop(0)
    if not first:
        cells, steps, inside, grad_in = (refs.pop(0) for _ in range(4))
        lam_edges = refs.pop(0)
    lam, coef, gain, scale = (refs.pop(0) for _ in range(4))
    if last:
        planes_out = refs.pop(0)
    part, part_edges = refs.pop(0), refs.pop(0)
    if not first:
        grad = refs.pop(0)
    v, mu = refs.pop(0), refs.pop(0)
    if last:
        ghost, total = refs
    elif not first:
        total = grad
    own, depth, rows_y, rows_x = mu.shape
    plane = rows_y * rows_x
    start = lax.axis_index("space") * (depth * plane)
    lanes = lax.broadcasted_iota(jnp.int32, (1, rows_x), 1)

    for k in range(own):
        for z in range(depth):
            if first or 0 < z < depth - 1:
                mu[k, z] = lam[k, z]
            else:
                mu[k, z] = lam_edges[min(z, 1), k]

    def take(source, z, y, x, r):
        row = source(z, y)
        value = jnp.sum(jnp.where(lanes == x, row, 0.0), axis=-1, keepdims=True)
        slots = lax.broadcasted_iota(jnp.int32, (own, total.shape[1]), 1)
        total[...] += jnp.where(slots == r, value, 0.0)

    def collect(wanted, own_rows, ghost_rows):
        def visit(i, carry):
            r = inside[i]
            _, z, y, x = spot(cells[r], start, rows_y, rows_x)
            fits = steps[r] == wanted
            mine = (z >= 0) & (z < depth)

            @pl.when(fits & mine)
            def _():
                take(own_rows, z, y, x, r)

            if ghost_rows is not None:

                @pl.when(fits & jnp.logical_not(mine))
                def _():
                    take(ghost_rows, jnp.where(z < 0, 0, 1), y, x, r)

            return carry

        lax.fori_loop(0, inside[inside.shape[0] - 1], visit, 0)

    if not first:
        total[...] = grad_in[...]
        collect(step + 1, lambda z, y: mu[:, z, pl.ds(y, 1), :].reshape(own, rows_x), None)

    for k in range(own):
        lifted, z, y, x = spot(sensors[k], start, rows_y, rows_x)

        @pl.when((lifted >= plane) & (lifted < (depth + 1) * plane))
        def _(k=k, z=z, y=y, x=x):
            mu[k, z, pl.ds(y, 1), :] += jnp.where(lanes == x, misfit[k, step], 0.0)

    blank = jnp.zeros((PAD, rows_x), jnp.float32)
    void = jnp.zeros((rows_y + 2 * PAD, rows_x), jnp.float32)
    for k in range(own):
        v[k, 0] = void
        v[k, depth + 1] = void
        for z in range(depth):
            v[k, z + 1, pl.ds(0, PAD)] = blank
            v[k, z + 1, pl.ds(PAD + rows_y, PAD)] = blank
            v[k, z + 1, pl.ds(PAD, rows_y)] = scale[0, z] * mu[k, z]

    def layer(z, carry):
        for tile in range(rows_y // TILE):
            at = pl.ds(tile * TILE, TILE)
            c = [coef[j, z, at] for j in range(PLANES)]
            keep = gain[0, z, at]
            for k in range(own):
                spread = stencil(
                    c, lambda dz, dy: v[k, z + 1 + dz, pl.ds(PAD + tile * TILE + dy, TILE)]
                )
                part[k, z, at] = mu[k, z, at] * keep + spread
        return carry

    lax.fori_loop(0, depth, layer, 0)
    for k in range(own):
        part_edges[0, k] = part[k, 0]
        part_edges[1, k] = part[k, depth - 1]

    if last:
        def field(k, carry):
            for side in range(2):
                z = 1 + side * (depth - 1)
                for tile in range(rows_y // TILE):
                    base = PAD + tile * TILE
                    here = v[k, z, pl.ds(base, TILE)]
                    down, up = pl.ds(base - 1, TILE), pl.ds(base + 1, TILE)
                    mid = pl.ds(base, TILE)
                    value = planes_out[side, 0, mid] * here
                    value += planes_out[side, 1, down] * v[k, z, down]
                    value += planes_out[side, 2, up] * v[k, z, up]
                    value += planes_out[side, 3, mid] * pltpu.roll(here, 1, axis=1)
                    value += planes_out[side, 4, mid] * pltpu.roll(here, rows_x - 1, axis=1)
                    ghost[side, k, pl.ds(tile * TILE, TILE)] = value
            return carry

        lax.fori_loop(0, own, field, 0)
        collect(
            0,
            lambda z, y: part[:, z, pl.ds(y, 1), :].reshape(own, rows_x),
            lambda z, y: ghost[z, :, pl.ds(y, 1), :].reshape(own, rows_x),
        )
        for i in range(grad.shape[0]):
            grad[i] = total[...]


def main(step, sensors, misfit, lam, lam_edges, planes_all, release, copies):
    first, last = step == STEPS - 1, step == 0
    coef, edge, gain, scale = planes_all
    own, depth, rows_y, rows_x = lam.shape
    grown = rows_y + 2 * PAD
    one = pl.BlockSpec((1, depth, rows_y, rows_x), lambda i: (step, 0, 0, 0))

    def whole(x):
        return pl.BlockSpec(x.shape, lambda i: (0,) * len(x.shape))

    args, specs = [sensors, misfit], [SMEM, SMEM]
    if not first:
        cells, steps, inside, grad_in = release
        args += [cells, steps, inside, grad_in, lam_edges]
        specs += [SMEM, SMEM, SMEM, whole(grad_in), whole(lam_edges)]
    args += [lam, coef, gain, scale]
    specs += [whole(lam), whole(coef), one, one]
    outs = [f32(own, depth, rows_y, rows_x), f32(2, own, rows_y, rows_x)]
    scratch = [
        pltpu.VMEM((own, depth + 2, grown, rows_x), jnp.float32),
        pltpu.VMEM((own, depth, rows_y, rows_x), jnp.float32),
    ]
    if last:
        args.append(edge)
        specs.append(whole(edge))
        outs.append(f32(copies, *grad_in.shape))
        scratch.append(pltpu.VMEM((2, own, rows_y, rows_x), jnp.float32))
        scratch.append(pltpu.VMEM(grad_in.shape, jnp.float32))
    elif not first:
        outs.append(f32(*grad_in.shape))
    return pl.pallas_call(
        functools.partial(main_kernel, step),
        grid=(1,),
        in_specs=specs,
        out_specs=[whole(o) for o in outs],
        out_shape=outs,
        scratch_shapes=scratch,
        compiler_params=params(40),
        cost_estimate=cost(40_000_000, 6_000_000),
        name=f"step{step}",
    )(*args)


def rim_kernel(step, *refs):
    first, last = step == STEPS - 1, step == 0
    refs = list(refs)
    sensors, misfit = refs.pop(0), refs.pop(0)
    part_edges, got_a, got_b, edge = (refs.pop(0) for _ in range(4))
    if first:
        rim = refs.pop(0)
    if last:
        grads, _, out, grad, vh, lam, sems = refs
    else:
        scale, lam, send_a, send_b, vh, w = refs
    own, rows_y, rows_x = got_a.shape
    depth = scale.shape[1] if not last else out.shape[1]
    plane = rows_y * rows_x
    start = lax.axis_index("space") * (depth * plane)
    lanes = lax.broadcasted_iota(jnp.int32, (1, rows_x), 1)
    inner = pl.ds(PAD, rows_y)
    side_a = 1 - parity()
    side_b = parity()

    blank = jnp.zeros((PAD, rows_x), jnp.float32)
    for k in range(own):
        for side in range(2):
            vh[side, k, pl.ds(0, PAD)] = blank
            vh[side, k, pl.ds(PAD + rows_y, PAD)] = blank
        vh[side_a, k, inner] = got_a[k]
        vh[side_b, k, inner] = got_b[k]
    if first:
        for k in range(own):
            lifted, z, y, x = spot(sensors[k], start, rows_y, rows_x)
            below = (lifted >= 0) & (lifted < plane)
            above = (lifted >= (depth + 1) * plane) & (lifted < (depth + 2) * plane)

            @pl.when(below | above)
            def _(k=k, above=above, y=y, x=x):
                side = jnp.where(above, 1, 0)
                vh[side, k, pl.ds(PAD + y, 1), :] += jnp.where(lanes == x, misfit[k, step], 0.0)

        for side in range(2):
            for k in range(own):
                vh[side, k, inner] = vh[side, k, inner] * rim[side]

    for side in range(2):
        for tile in range(rows_y // TILE):
            at = pl.ds(tile * TILE, TILE)
            base = PAD + tile * TILE
            c = [edge[side, j, pl.ds(base, TILE)] for j in range(5)]
            if not last:
                z = side * (depth - 1)
                gain = scale[0, z, at]
            for k in range(own):
                here = vh[side, k, pl.ds(base, TILE)]
                value = part_edges[side, k, at] + c[0] * here
                value += c[1] * vh[side, k, pl.ds(base + 1, TILE)]
                value += c[2] * vh[side, k, pl.ds(base - 1, TILE)]
                value += pltpu.roll(c[3] * here, rows_x - 1, axis=1)
                value += pltpu.roll(c[4] * here, 1, axis=1)
                lam[side, k, at] = value
                if not last:
                    w[side, k, at] = gain * value
    if last:
        copies = [
            pltpu.make_async_copy(lam.at[side], out.at[:, side * (depth - 1)], sems.at[side])
            for side in range(2)
        ]
        for c in copies:
            c.start()
        total = grads[0]
        for i in range(1, grads.shape[0]):
            total += grads[i]
        grad[...] = total
        for c in copies:
            c.wait()
        return
    for k in range(own):
        lifted, z, y, x = spot(sensors[k], start, rows_y, rows_x)
        here = (lifted >= plane) & (lifted < (depth + 1) * plane)

        @pl.when(here & ((z == 0) | (z == depth - 1)))
        def _(k=k, z=z, y=y, x=x):
            side = jnp.where(z == 0, 0, 1)
            add = jnp.where(lanes == x, misfit[k, step - 1], 0.0)
            w[side, k, pl.ds(y, 1), :] += add * scale[0, z, pl.ds(y, 1), :]

    for k in range(own):
        send_a[k] = w[side_a, k]
        send_b[k] = w[side_b, k]


def rim_step(step, sensors, misfit, part, part_edges, got_a, got_b, planes_all, rim, grads):
    first, last = step == STEPS - 1, step == 0
    _, edge, _, scale = planes_all
    own, rows_y, rows_x = got_a.shape
    depth = part.shape[1]
    grown = rows_y + 2 * PAD

    def whole(x):
        return pl.BlockSpec(x.shape, lambda i: (0,) * len(x.shape))

    args = [sensors, misfit, part_edges, got_a, got_b, edge]
    specs = [SMEM, SMEM] + [whole(x) for x in args[2:]]
    if first:
        args.append(rim)
        specs.append(whole(rim))
    field = f32(own, rows_y, rows_x)
    halo = pltpu.VMEM((2, own, grown, rows_x), jnp.float32)
    both = pltpu.VMEM((2, own, rows_y, rows_x), jnp.float32)
    aliases = {}
    if last:
        aliases = {len(args) + 1: 0}
        args += [grads, part]
        specs += [whole(grads), ANY]
        outs = [f32(*part.shape), f32(*grads.shape[1:])]
        out_specs = [ANY, whole(outs[1])]
        scratch = [halo, both, pltpu.SemaphoreType.DMA((2,))]
    else:
        args.append(scale)
        specs.append(pl.BlockSpec((1, depth, rows_y, rows_x), lambda i: (step - 1, 0, 0, 0)))
        outs = [f32(2, own, rows_y, rows_x), field, field]
        out_specs = [whole(o) for o in outs]
        scratch = [halo, both]
    return pl.pallas_call(
        functools.partial(rim_kernel, step),
        grid=(1,),
        in_specs=specs,
        out_specs=out_specs,
        out_shape=outs,
        scratch_shapes=scratch,
        input_output_aliases=aliases,
        compiler_params=params(24),
        cost_estimate=cost(4_000_000, 3_000_000),
        name=f"rim{step}",
    )(*args)


def turned(array, axis):
    count = lax.axis_size(axis)
    return [array] + [
        lax.ppermute(array, axis, [(i, (i + k) % count) for i in range(count)])
        for k in range(1, count)
    ]


def body(
    adjoint_end,
    checkpoints,
    dispersion,
    owner_steps,
    sensor_cells,
    misfit,
    release_cells,
    release_steps,
):
    own, depth, rows_y, rows_x = adjoint_end.shape
    slabs = lax.axis_size("space")
    pairs_a = [(i, i ^ 1) for i in range(slabs)]
    pairs_b = [(i, ((i + 1) ^ 1) - 1) for i in range(1, slabs - 1)]

    def swap(a, b):
        return lax.ppermute(a, "space", pairs_a), lax.ppermute(b, "space", pairs_b)

    send_a, send_b, small_a, small_b, states = pack(
        owner_steps, adjoint_end, checkpoints, dispersion
    )
    small_a, small_b = swap(small_a, small_b)
    got_a, got_b = swap(send_a, send_b)
    parts = turned(dispersion, "sens")
    states = turned(states, "sens")
    small_a, small_b = turned(small_a, "sens"), turned(small_b, "sens")
    coef, edge, gain, scale, rim, inside = planes(
        owner_steps, release_cells, parts, states, small_a, small_b, checkpoints.shape[0]
    )
    planes_all = (coef, edge, gain, scale)
    part, part_edges = main(
        2, sensor_cells, misfit, adjoint_end, None, planes_all, None, slabs
    )
    edges, send_a, send_b = rim_step(
        2, sensor_cells, misfit, part, part_edges, got_a, got_b, planes_all, rim, None
    )
    grad = jnp.zeros((own, release_cells.shape[0]), jnp.float32)
    for step in (1, 0):
        got_a, got_b = swap(send_a, send_b)
        release = (release_cells, release_steps, inside, grad)
        part, part_edges, grad = main(
            step, sensor_cells, misfit, part, edges, planes_all, release, slabs
        )
        if step == 0:
            grad = lax.all_to_all(grad, "space", 0, 0, tiled=True)
        edges, *rest = rim_step(
            step, sensor_cells, misfit, part, part_edges, got_a, got_b, planes_all, rim, grad
        )
        if step:
            send_a, send_b = rest
    return edges, rest[0]


def solution(mesh):
    in_specs = (
        P("sens", "space", None, None),
        P("sens", "space", None, None),
        P(None, "space", "sens", None),
        P(),
        P("sens"),
        P("sens", None),
        P(),
        P(),
    )
    out_specs = (P("sens", "space", None, None), P("sens", None))
    return jax.shard_map(body, mesh=mesh, in_specs=in_specs, out_specs=out_specs, check_vma=False)
```

```python
import functools

import jax
import jax.numpy as jnp
from jax import lax
from jax.experimental import pallas as pl
from jax.experimental.pallas import tpu as pltpu
from jax.sharding import PartitionSpec as P

STEPS = 3
DT = 0.12
PAD = 8
TILE = 8
CENTRE, ZP, ZM, YP, YM, ZPYP, ZPYM, ZMYP, ZMYM = range(9)
XP, XPZP, XPZM, XPYP, XPYM, XM, XMZP, XMZM, XMYP, XMYM = range(9, 19)
PLANES = 19
LOW = (ZM, ZMYP, ZMYM, XPZM, XMZM)
HIGH = (ZP, ZPYP, ZPYM, XPZP, XMZP)

VMEM = pl.BlockSpec(memory_space=pltpu.VMEM)
SMEM = pl.BlockSpec(memory_space=pltpu.SMEM)
ANY = pl.BlockSpec(memory_space=pl.ANY)


def f32(*shape):
    return jax.ShapeDtypeStruct(shape, jnp.float32)


def params(mib):
    return pltpu.CompilerParams(vmem_limit_bytes=mib * 1024 * 1024)


def cost(flops, moved):
    return pl.CostEstimate(flops=flops, bytes_accessed=moved, transcendentals=0)


def owned(owner_ref, slots):
    me = lax.axis_index("sens")
    o0, o1, o2 = (owner_ref[i] for i in range(3))
    own0 = lax.div(o0, slots) == me
    own1 = lax.div(o1, slots) == me
    first = jnp.where(own0, o0, jnp.where(own1, o1, o2))
    second = jnp.where(own0 & own1, o1, o2)
    return lax.rem(first, slots), lax.rem(second, slots)


def parity():
    return lax.rem(lax.axis_index("space"), 2)


def spot(cell, start, rows_y, rows_x):
    local = cell - start
    lifted = local + rows_y * rows_x
    z = lax.div(lifted, rows_y * rows_x) - 1
    y = lax.div(lax.rem(lifted, rows_y * rows_x), rows_x)
    return lifted, z, y, lax.rem(lifted, rows_x)


def pack_kernel(
    owner, sensors, misfit, adj, ckpt, disp, lam_a, lam_b, small_a, small_b, sems
):
    own, depth, rows_y, rows_x = adj.shape
    rows = disp.shape[2]
    plane = rows_y * rows_x
    start = lax.axis_index("space") * (depth * plane)
    even = parity() == 0
    z_a = jnp.where(even, depth - 1, 0)
    z_b = jnp.where(even, 0, depth - 1)
    held = owned(owner, ckpt.shape[0])
    moves = [(adj.at[:, z_a], lam_a), (adj.at[:, z_b], lam_b)]
    for z, small in ((z_a, small_a), (z_b, small_b)):
        for j in range(2):
            moves.append((ckpt.at[held[j], z], small.at[pl.ds(j * rows_y, rows_y)]))
        for j, comp in enumerate((0, 3, 4)):
            moves.append((disp.at[comp, z], small.at[pl.ds(2 * rows_y + j * rows, rows)]))
    copies = [pltpu.make_async_copy(s, d, sems.at[i]) for i, (s, d) in enumerate(moves)]
    for c in copies:
        c.start()

    lanes = lax.broadcasted_iota(jnp.int32, (1, rows_x), 1)
    for c in copies[:2]:
        c.wait()
    for k in range(own):
        lifted, z, y, x = spot(sensors[k], start, rows_y, rows_x)
        mine = (lifted >= plane) & (lifted < (depth + 1) * plane)

        for edge, lam in ((z_a, lam_a), (z_b, lam_b)):

            @pl.when(mine & (z == edge))
            def _(k=k, y=y, x=x, lam=lam):
                lam[k, pl.ds(y, 1), :] += jnp.where(lanes == x, misfit[STEPS - 1, k], 0.0)

    for c in copies[2:]:
        c.wait()


def pack(owner, sensors, misfit, adj, ckpt, disp):
    own, depth, rows_y, rows_x = adj.shape
    rows = disp.shape[2]
    small = f32(2 * rows_y + 3 * rows, rows_x)
    return pl.pallas_call(
        pack_kernel,
        in_specs=[SMEM] * 3 + [ANY] * 3,
        out_specs=[VMEM] * 4,
        out_shape=[f32(own, rows_y, rows_x)] * 2 + [small, small],
        scratch_shapes=[pltpu.SemaphoreType.DMA((12,))],
        compiler_params=params(60),
        cost_estimate=cost(1000, 1000),
        name="pack",
    )(owner, sensors, misfit, adj, ckpt, disp)


def lane_masks(shape):
    lanes = lax.broadcasted_iota(jnp.int32, shape, len(shape) - 1)
    return lanes >= 1, lanes < shape[-1] - 1


def before(value, keep):
    return jnp.where(keep, pltpu.roll(value, 1, axis=value.ndim - 1), 0.0)


def after(value, keep):
    return jnp.where(keep, pltpu.roll(value, value.shape[-1] - 1, axis=value.ndim - 1), 0.0)


def planes_at(window, keep_b, keep_a):
    def yy(dy):
        return window(1, 0, dy)

    c = [None] * PLANES
    zz, zzp, zzm = window(0, 0, 0), window(0, 1, 0), window(0, -1, 0)
    xx = window(2, 0, 0)
    c[ZP], c[ZM] = 0.5 * (zz + zzp), 0.5 * (zz + zzm)
    c[YP], c[YM] = 0.5 * (yy(0) + yy(1)), 0.5 * (yy(0) + yy(-1))
    xx_b, xx_a = before(xx, keep_b), after(xx, keep_a)
    c[XP] = jnp.where(keep_b, 0.5 * (xx_b + xx), 0.0)
    c[XM] = jnp.where(keep_a, 0.5 * (xx_a + xx), 0.0)
    c[CENTRE] = -(c[ZP] + c[ZM] + c[YP] + c[YM] + (xx + 0.5 * (xx_a + xx_b)))
    zp, zm, yp, ym = window(3, 1, 0), window(3, -1, 0), window(3, 0, 1), window(3, 0, -1)
    c[ZPYP], c[ZPYM] = 0.25 * (zp + yp), -0.25 * (zp + ym)
    c[ZMYP], c[ZMYM] = -0.25 * (zm + yp), 0.25 * (zm + ym)
    for comp, plus, minus, names in (
        (4, window(4, 1, 0), window(4, -1, 0), (XPZP, XPZM, XMZP, XMZM)),
        (5, window(5, 0, 1), window(5, 0, -1), (XPYP, XPYM, XMYP, XMYM)),
    ):
        here = window(comp, 0, 0)
        c[names[0]] = jnp.where(keep_b, 0.25 * (before(plus, keep_b) + here), 0.0)
        c[names[1]] = jnp.where(keep_b, -0.25 * (before(minus, keep_b) + here), 0.0)
        c[names[2]] = jnp.where(keep_a, -0.25 * (after(plus, keep_a) + here), 0.0)
        c[names[3]] = jnp.where(keep_a, 0.25 * (after(minus, keep_a) + here), 0.0)
    return c


def stencil(c, u):
    near = {(dz, dy): u(dz, dy) for dz in (-1, 0, 1) for dy in (-1, 0, 1)}
    here = c[CENTRE] * near[0, 0] + c[ZP] * near[1, 0] + c[ZM] * near[-1, 0]
    here += c[YP] * near[0, 1] + c[YM] * near[0, -1]
    here += c[ZPYP] * near[1, 1] + c[ZPYM] * near[1, -1]
    here += c[ZMYP] * near[-1, 1] + c[ZMYM] * near[-1, -1]
    right = c[XP] * near[0, 0] + c[XPZP] * near[1, 0] + c[XPZM] * near[-1, 0]
    right += c[XPYP] * near[0, 1] + c[XPYM] * near[0, -1]
    left = c[XM] * near[0, 0] + c[XMZP] * near[1, 0] + c[XMZM] * near[-1, 0]
    left += c[XMYP] * near[0, 1] + c[XMYM] * near[0, -1]
    width = here.shape[-1]
    return here + pltpu.roll(right, width - 1, axis=1) + pltpu.roll(left, 1, axis=1)


def scale_of(conc):
    root = jnp.sqrt(conc)
    return DT * root / (root + 0.5)


def slope_of(conc):
    root = jnp.sqrt(conc)
    return (0.25 * DT) / (root * (root + 0.5) * (root + 0.5))


def planes_kernel(count, *refs):
    owner = refs[0]
    parts, states = refs[1 : 1 + count], refs[1 + count : 1 + 2 * count]
    coef, gain, scale, ends, full, conc = refs[1 + 2 * count :]
    depth, rows_y, rows_x = coef.shape[1:]
    rows = rows_y // count
    slots = states[0].shape[0]
    me = lax.axis_index("sens")
    inner = pl.ds(PAD, rows_y)

    blank = jnp.zeros((PAD, rows_x), jnp.float32)
    void = jnp.zeros((rows_y + 2 * PAD, rows_x), jnp.float32)
    for ref in (full, conc):
        for i in range(ref.shape[0]):
            ref[i, 0] = void
            ref[i, depth + 1] = void
            for z in range(depth):
                ref[i, z + 1, pl.ds(0, PAD)] = blank
                ref[i, z + 1, pl.ds(PAD + rows_y, PAD)] = blank
    for k in range(count):
        who = lax.rem(me - k + count, count)
        span = pl.ds(pl.multiple_of(PAD + who * rows, PAD), rows)
        for comp in range(6):
            for z in range(depth):
                full[comp, z + 1, span] = parts[k][comp, z]
    for i in range(STEPS):
        turn = lax.rem(me - lax.div(owner[i], slots) + count, count)
        slot = lax.rem(owner[i], slots)
        for k in range(count):

            @pl.when(turn == k)
            def _(i=i, k=k, slot=slot):
                conc[i, pl.ds(1, depth), inner] = states[k][slot]

        for side in range(2):
            ends[i, side] = conc[i, 1 + side * (depth - 1), inner]

    keep_b, keep_a = lane_masks((TILE, rows_x))

    def layer(z, carry):
        for tile in range(rows_y // TILE):
            at = pl.ds(tile * TILE, TILE)

            def window(comp, dz, dy):
                return full[comp, z + 1 + dz, pl.ds(PAD + tile * TILE + dy, TILE)]

            c = planes_at(window, keep_b, keep_a)
            for j in range(PLANES):
                coef[j, z, at] = c[j]
            for i in range(STEPS):
                here = conc[i, z + 1, pl.ds(PAD + tile * TILE, TILE)]
                spread = stencil(
                    c, lambda dz, dy: conc[i, z + 1 + dz, pl.ds(PAD + tile * TILE + dy, TILE)]
                )
                scale[i, z, at] = scale_of(here)
                gain[i, z, at] = 1.0 + slope_of(here) * spread
        return carry

    lax.fori_loop(0, depth, layer, 0)


def planes(owner, parts, states):
    count = len(parts)
    depth, rows_y, rows_x = states[0].shape[1:]
    grown = rows_y + 2 * PAD
    return pl.pallas_call(
        functools.partial(planes_kernel, count),
        in_specs=[SMEM] + [VMEM] * (2 * count),
        out_specs=[VMEM] * 4,
        out_shape=[
            f32(PLANES, depth, rows_y, rows_x),
            f32(STEPS, depth, rows_y, rows_x),
            f32(STEPS, depth, rows_y, rows_x),
            f32(STEPS, 2, rows_y, rows_x),
        ],
        scratch_shapes=[
            pltpu.VMEM((6, depth + 2, grown, rows_x), jnp.float32),
            pltpu.VMEM((STEPS, depth + 2, grown, rows_x), jnp.float32),
        ],
        compiler_params=params(24),
        cost_estimate=cost(2_000_000_000, 60_000_000),
        name="planes",
    )(owner, *parts, *states)


def ends_kernel(count, slots, *refs):
    owner, coef, ends = refs[:3]
    small = refs[3 : 3 + count], refs[3 + count : 3 + 2 * count]
    edge, edge_raw, corr, tensor, conc = refs[3 + 2 * count :]
    depth, rows_y, rows_x = coef.shape[1:]
    rows = rows_y // count
    me = lax.axis_index("sens")
    side_a = 1 - parity()
    inner = pl.ds(PAD, rows_y)
    blank = jnp.zeros((PAD, rows_x), jnp.float32)
    for side in range(2):
        for i in range(STEPS):
            conc[side, i, pl.ds(0, PAD)] = blank
            conc[side, i, pl.ds(PAD + rows_y, PAD)] = blank
    for k in range(count):
        who = lax.rem(me - k + count, count)
        span = pl.ds(pl.multiple_of(who * rows, PAD), rows)
        for j in range(3):
            here = pl.ds(2 * rows_y + j * rows, rows)
            tensor[side_a, j, span] = small[0][k][here]
            tensor[1 - side_a, j, span] = small[1][k][here]
    holders = [lax.div(owner[i], slots) for i in range(STEPS)]
    for i in range(STEPS):
        slot = jnp.int32(0)
        for j in range(i):
            slot += jnp.where(holders[j] == holders[i], 1, 0)
        slot = jnp.minimum(slot, 1)
        turn = lax.rem(me - holders[i] + count, count)
        for k in range(count):

            @pl.when(turn == k)
            def _(i=i, k=k, slot=slot):
                span = pl.ds(pl.multiple_of(slot * rows_y, PAD), rows_y)
                conc[side_a, i, inner] = small[0][k][span]
                conc[1 - side_a, i, inner] = small[1][k][span]

    keep_b, keep_a = lane_masks((TILE, rows_x))
    ys = lax.broadcasted_iota(jnp.int32, (TILE, rows_x), 0)
    for side, z, names in ((0, 0, LOW), (1, depth - 1, HIGH)):
        sign = 2 * side - 1
        for tile in range(rows_y // TILE):
            at = pl.ds(tile * TILE, TILE)
            zz, zy, zx = (tensor[side, j, at] for j in range(3))
            e = [coef[names[j], z, at] for j in range(5)]
            e[0] += 0.5 * zz
            e[1] += (0.25 * sign) * zy
            e[2] -= (0.25 * sign) * zy
            e[3] += (0.25 * sign) * before(zx, keep_b)
            e[4] -= (0.25 * sign) * after(zx, keep_a)
            if tile == rows_y // TILE - 1:
                e[1] = jnp.where(ys < TILE - 1, e[1], 0.0)
            if tile == 0:
                e[2] = jnp.where(ys > 0, e[2], 0.0)
            near = [
                [conc[side, i, pl.ds(PAD + tile * TILE + d, TILE)] for d in (0, 1, -1)]
                for i in range(STEPS)
            ]
            for j in range(5):
                edge[side, j, at] = e[j]
                edge_raw[side, j, at] = e[j] * scale_of(near[STEPS - 1][(0, 1, 2, 0, 0)[j]])
            for i in range(STEPS):
                here, up, down = near[i]
                own = ends[i, side, at]
                spread = e[0] * here + e[1] * up + e[2] * down - 0.5 * zz * own
                spread += pltpu.roll(e[3] * here, rows_x - 1, axis=1)
                spread += pltpu.roll(e[4] * here, 1, axis=1)
                gain, scale = slope_of(own) * spread, scale_of(own)
                if i == STEPS - 1:
                    corr[i, side, at] = gain - 0.5 * zz * scale
                else:
                    corr[i, side, at] = gain / scale - 0.5 * zz


def ends_call(owner, coef, ends, small_a, small_b, slots):
    count = len(small_a)
    _, _, rows_y, rows_x = coef.shape
    return pl.pallas_call(
        functools.partial(ends_kernel, count, slots),
        in_specs=[SMEM] + [VMEM] * (2 + 2 * count),
        out_specs=[VMEM] * 3,
        out_shape=[
            f32(2, 5, rows_y, rows_x),
            f32(2, 5, rows_y, rows_x),
            f32(STEPS, 2, rows_y, rows_x),
        ],
        scratch_shapes=[
            pltpu.VMEM((2, 3, rows_y, rows_x), jnp.float32),
            pltpu.VMEM((2, STEPS, rows_y + 2 * PAD, rows_x), jnp.float32),
        ],
        compiler_params=params(16),
        cost_estimate=cost(1_000_000, 1_000_000),
        name="ends",
    )(owner, coef, ends, *small_a, *small_b)


def gather_field(first, lam, lam_a, lam_b, mu):
    own, depth = mu.shape[:2]
    for k in range(own):
        for z in range(depth):
            if first or 0 < z < depth - 1:
                mu[k, z] = lam[k, z]
    if not first:
        z_a = jnp.where(parity() == 0, depth - 1, 0)
        for k in range(own):
            mu[k, z_a] = lam_a[k]
            mu[k, depth - 1 - z_a] = lam_b[k]


def add_misfit(step, sensors, misfit, mu):
    own, depth, rows_y, rows_x = mu.shape
    plane = rows_y * rows_x
    start = lax.axis_index("space") * (depth * plane)
    lanes = lax.broadcasted_iota(jnp.int32, (1, rows_x), 1)
    for k in range(own):
        lifted, z, y, x = spot(sensors[k], start, rows_y, rows_x)

        @pl.when((lifted >= plane) & (lifted < (depth + 1) * plane))
        def _(k=k, z=z, y=y, x=x):
            mu[k, z, pl.ds(y, 1), :] += jnp.where(lanes == x, misfit[step, k], 0.0)


def scale_field(scale, step, mu, v):
    own, depth, rows_y, rows_x = mu.shape
    blank = jnp.zeros((PAD, rows_x), jnp.float32)
    void = jnp.zeros((rows_y + 2 * PAD, rows_x), jnp.float32)
    for k in range(own):
        v[k, 0] = void
        v[k, depth + 1] = void
        for z in range(depth):
            v[k, z + 1, pl.ds(0, PAD)] = blank
            v[k, z + 1, pl.ds(PAD + rows_y, PAD)] = blank
            v[k, z + 1, pl.ds(PAD, rows_y)] = scale[step, z] * mu[k, z]


def spread_field(coef, gain, step, mu, v, part, part_edges=None):
    own, depth, rows_y, rows_x = mu.shape

    def layer(z, carry):
        for tile in range(rows_y // TILE):
            at = pl.ds(tile * TILE, TILE)
            c = [coef[j, z, at] for j in range(PLANES)]
            keep = gain[step, z, at]
            for k in range(own):
                spread = stencil(
                    c, lambda dz, dy: v[k, z + 1 + dz, pl.ds(PAD + tile * TILE + dy, TILE)]
                )
                part[k, z, at] = mu[k, z, at] * keep + spread
        return carry

    lax.fori_loop(0, depth, layer, 0)
    if part_edges is not None:
        for k in range(own):
            part_edges[0, k] = part[k, 0]
            part_edges[1, k] = part[k, depth - 1]


def collect(wanted, release, shape, total, own_row, near_row=None):
    cells, steps, inside = release
    own, depth, rows_y, rows_x = shape
    start = lax.axis_index("space") * (depth * rows_y * rows_x)
    lanes = lax.broadcasted_iota(jnp.int32, (1, rows_x), 1)
    slots = lax.broadcasted_iota(jnp.int32, (own, total.shape[1]), 1)

    def take(r, x, row):
        value = jnp.sum(jnp.where(lanes == x, row, 0.0), axis=-1, keepdims=True)
        total[...] += jnp.where(slots == r, value, 0.0)

    def visit(i, carry):
        r = inside[i]
        _, z, y, x = spot(cells[r], start, rows_y, rows_x)
        fits = steps[r] == wanted
        mine = (z >= 0) & (z < depth)

        @pl.when(fits & mine)
        def _():
            take(r, x, own_row(z, y))

        if near_row is not None:

            @pl.when(fits & jnp.logical_not(mine))
            def _():
                take(r, x, near_row(jnp.where(z < 0, 0, 1), y))

        return carry

    lax.fori_loop(0, inside[inside.shape[0] - 1], visit, 0)


def list_releases(cells, shape, inside):
    own, depth, rows_y, rows_x = shape
    plane = rows_y * rows_x
    start = lax.axis_index("space") * (depth * plane)

    def note(r, found):
        local = cells[r] - start
        near = (local >= -plane) & (local < (depth + 1) * plane)

        @pl.when(near)
        def _():
            inside[found] = r

        return found + jnp.where(near, 1, 0)

    inside[inside.shape[0] - 1] = lax.fori_loop(0, cells.shape[0], note, jnp.int32(0))


def rows_of(ref, *index):
    row = ref[(slice(None), *index, slice(None))]
    return row.reshape(row.shape[0], row.shape[-1])


def first_kernel(sensors, misfit, lam, coef, gain, scale, part, part_edges, v, mu):
    gather_field(True, lam, None, None, mu)
    add_misfit(STEPS - 1, sensors, misfit, mu)
    scale_field(scale, STEPS - 1, mu, v)
    spread_field(coef, gain, STEPS - 1, mu, v, part, part_edges)


def middle_kernel(
    step, sensors, misfit, cells, steps, lam, lam_a, lam_b, coef, gain, scale, part, part_edges, grad, inside, v, mu
):
    gather_field(False, lam, lam_a, lam_b, mu)
    grad[...] = jnp.zeros_like(grad)
    list_releases(cells, mu.shape, inside)
    collect(
        step + 1, (cells, steps, inside), mu.shape, grad, lambda z, y: rows_of(mu, z, pl.ds(y, 1))
    )
    add_misfit(step, sensors, misfit, mu)
    scale_field(scale, step, mu, v)
    spread_field(coef, gain, step, mu, v, part, part_edges)


def front_kernel(
    sensors, misfit, cells, steps, inside, grad_in, lam, lam_a, lam_b, coef, edge, corr, gain, scale, grads, mu, v, total
):
    own, depth, rows_y, rows_x = mu.shape
    gather_field(False, lam, lam_a, lam_b, mu)
    total[...] = grad_in[...]
    release = (cells, steps, inside)
    collect(1, release, mu.shape, total, lambda z, y: rows_of(mu, z, pl.ds(y, 1)))
    add_misfit(0, sensors, misfit, mu)
    scale_field(scale, 0, mu, v)

    def own_row(z, y):
        at = pl.ds(y, 1)
        c = [coef[j, z, at] for j in range(PLANES)]
        spread = stencil(c, lambda dz, dy: rows_of(v, z + 1 + dz, pl.ds(PAD + y + dy, 1)))
        at_edge = (z == 0) | (z == depth - 1)
        miss = jnp.where(at_edge, corr[0, jnp.where(z == 0, 0, 1), at], 0.0)
        return rows_of(mu, z, at) * gain[0, z, at] + spread + miss * rows_of(v, z + 1, pl.ds(PAD + y, 1))

    def near_row(side, y):
        z = 1 + side * (depth - 1)
        here, down, up = (rows_of(v, z, pl.ds(PAD + y + d, 1)) for d in (0, -1, 1))
        at = pl.ds(y, 1)
        value = edge[side, 0, at] * here
        value += edge[side, 1, pl.ds(jnp.maximum(y - 1, 0), 1)] * down
        value += edge[side, 2, pl.ds(jnp.minimum(y + 1, rows_y - 1), 1)] * up
        value += edge[side, 3, at] * pltpu.roll(here, 1, axis=1)
        value += edge[side, 4, at] * pltpu.roll(here, rows_x - 1, axis=1)
        return value

    collect(0, release, mu.shape, total, own_row, near_row)
    for i in range(grads.shape[0]):
        grads[i] = total[...]


def field_call(kernel, name, args, specs, outs, scratch, flops, listed=0):
    return pl.pallas_call(
        kernel,
        in_specs=specs,
        out_specs=[VMEM] * len(outs) + [SMEM] * (listed > 0),
        out_shape=outs + [jax.ShapeDtypeStruct((listed,), jnp.int32)] * (listed > 0),
        scratch_shapes=[pltpu.VMEM(o.shape, jnp.float32) for o in scratch],
        compiler_params=params(32),
        cost_estimate=cost(flops, 4_000_000),
        name=name,
    )(*args)


def met(got, k, tile, tiles):
    here = got[k, pl.ds(tile * TILE, TILE)]
    if tile == tiles - 1:
        up = pltpu.roll(here, TILE - 1, axis=0)
    else:
        up = got[k, pl.ds(tile * TILE + 1, TILE)]
    if tile == 0:
        down = pltpu.roll(here, 1, axis=0)
    else:
        down = got[k, pl.ds(tile * TILE - 1, TILE)]
    return here, up, down


def from_met(c, here, up, down):
    width = here.shape[-1]
    value = c[0] * here + c[1] * up + c[2] * down
    value += pltpu.roll(c[3] * here, width - 1, axis=1)
    return value + pltpu.roll(c[4] * here, 1, axis=1)


def rim_kernel(step, late, sensors, misfit, part_edges, got, sent, edge, corr, scale, lam, send):
    depth = scale.shape[1]
    own, rows_y, rows_x = got.shape
    tiles = rows_y // TILE
    side = parity() if late else 1 - parity()
    z = side * (depth - 1)
    for tile in range(tiles):
        at = pl.ds(tile * TILE, TILE)
        c = [edge[side, j, at] for j in range(5)]
        miss = corr[step, side, at]
        gain = scale[step - 1, z, at]
        for k in range(own):
            value = part_edges[side, k, at] + miss * sent[k, at]
            value += from_met(c, *met(got, k, tile, tiles))
            lam[k, at] = value
            send[k, at] = gain * value
    plane = rows_y * rows_x
    start = lax.axis_index("space") * (depth * plane)
    lanes = lax.broadcasted_iota(jnp.int32, (1, rows_x), 1)
    for k in range(own):
        lifted, at_z, y, x = spot(sensors[k], start, rows_y, rows_x)
        here = (lifted >= plane) & (lifted < (depth + 1) * plane)

        @pl.when(here & (at_z == z))
        def _(k=k, y=y, x=x):
            add = jnp.where(lanes == x, misfit[step - 1, k], 0.0)
            send[k, pl.ds(y, 1), :] += add * scale[step - 1, z, pl.ds(y, 1), :]


def rim(step, late, sensors, misfit, part_edges, got, sent, edge, corr, scale):
    return pl.pallas_call(
        functools.partial(rim_kernel, step, late),
        in_specs=[SMEM] * 2 + [VMEM] * 6,
        out_specs=[VMEM] * 2,
        out_shape=[f32(*got.shape)] * 2,
        compiler_params=params(16),
        cost_estimate=cost(2_000_000, 1_500_000),
        name=f"rim{step}{'b' if late else 'a'}",
    )(sensors, misfit, part_edges, got, sent, edge, corr, scale)


def last_kernel(mu, v, coef, gain, got_a, got_b, edge, corr, grads, out, grad, part, sems):
    own, depth, rows_y, rows_x = mu.shape
    tiles = rows_y // TILE
    spread_field(coef, gain, 0, mu, v, part)
    copies = [
        pltpu.make_async_copy(part.at[:, z], out.at[:, z], sems.at[z]) for z in range(depth)
    ]
    for c in copies[1:-1]:
        c.start()
    total = grads[0]
    for i in range(1, grads.shape[0]):
        total += grads[i]
    grad[...] = total
    side_a = 1 - parity()
    for got, side in ((got_a, side_a), (got_b, 1 - side_a)):
        z = side * (depth - 1)
        for tile in range(tiles):
            at = pl.ds(tile * TILE, TILE)
            c = [edge[side, j, at] for j in range(5)]
            miss = corr[0, side, at]
            for k in range(own):
                value = part[k, z, at] + miss * v[k, z + 1, pl.ds(PAD + tile * TILE, TILE)]
                part[k, z, at] = value + from_met(c, *met(got, k, tile, tiles))
    for c in (copies[0], copies[-1]):
        c.start()
    for c in copies:
        c.wait()


def last_call(mu, v, coef, gain, got_a, got_b, edge, corr, grads):
    return pl.pallas_call(
        last_kernel,
        in_specs=[VMEM] * 9,
        out_specs=[ANY, VMEM],
        out_shape=[f32(*mu.shape), f32(*grads.shape[1:])],
        scratch_shapes=[
            pltpu.VMEM(mu.shape, jnp.float32),
            pltpu.SemaphoreType.DMA((mu.shape[1],)),
        ],
        compiler_params=params(16),
        cost_estimate=cost(40_000_000, 6_000_000),
        name="step0",
    )(mu, v, coef, gain, got_a, got_b, edge, corr, grads)


def turned(array, axis):
    count = lax.axis_size(axis)
    return [array] + [
        lax.ppermute(array, axis, [(i, (i + k) % count) for i in range(count)])
        for k in range(1, count)
    ]


def body(
    adjoint_end,
    checkpoints,
    dispersion,
    owner_steps,
    sensor_cells,
    misfit,
    release_cells,
    release_steps,
):
    own, depth, rows_y, rows_x = adjoint_end.shape
    slabs = lax.axis_size("space")
    pairs_a = [(i, i ^ 1) for i in range(slabs)]
    pairs_b = [(i, ((i + 1) ^ 1) - 1) for i in range(1, slabs - 1)]
    misfit = misfit.T

    def swap_a(x):
        return lax.ppermute(x, "space", pairs_a)

    def swap_b(x):
        return lax.ppermute(x, "space", pairs_b)

    parts, states = turned(dispersion, "sens"), turned(checkpoints, "sens")
    sent_a, sent_b, small_a, small_b = pack(
        owner_steps, sensor_cells, misfit, adjoint_end, checkpoints, dispersion
    )
    small_a, small_b = swap_a(small_a), swap_b(small_b)
    parts, states, sent_a, sent_b = lax.optimization_barrier((parts, states, sent_a, sent_b))
    got_a, got_b = swap_a(sent_a), swap_b(sent_b)
    small_a, small_b, parts = lax.optimization_barrier((small_a, small_b, parts))
    small_a, small_b = turned(small_a, "sens"), turned(small_b, "sens")
    coef, gain, scale, ends = planes(owner_steps, parts, states)

    field = f32(own, depth, rows_y, rows_x)
    edges = f32(2, own, rows_y, rows_x)
    tall = f32(own, depth + 2, rows_y + 2 * PAD, rows_x)
    kept = f32(own, release_cells.shape[0])
    sensors = (sensor_cells, misfit)
    release = (release_cells, release_steps)

    part, part_edges = field_call(
        first_kernel,
        "step2",
        (*sensors, adjoint_end, coef, gain, scale),
        [SMEM] * 2 + [VMEM, VMEM, VMEM, VMEM],
        [field, edges],
        [tall, field],
        40_000_000,
    )
    small_a, small_b, part_edges = lax.optimization_barrier((small_a, small_b, part_edges))
    edge, edge_raw, corr = ends_call(
        owner_steps, coef, ends, small_a, small_b, checkpoints.shape[0]
    )
    lam_b, send_b = rim(2, True, *sensors, part_edges, got_b, sent_b, edge_raw, corr, scale)
    got_b = swap_b(send_b)
    lam_a, send_a = rim(2, False, *sensors, part_edges, got_a, sent_a, edge_raw, corr, scale)
    got_a = swap_a(send_a)
    part, part_edges, grad, inside = field_call(
        functools.partial(middle_kernel, 1),
        "step1",
        (*sensors, *release, part, lam_a, lam_b, coef, gain, scale),
        [SMEM] * 4 + [VMEM] * 6,
        [field, edges, kept],
        [tall, field],
        40_000_000,
        release_cells.shape[0] + 1,
    )
    sent_a, sent_b = send_a, send_b
    lam_b, send_b = rim(1, True, *sensors, part_edges, got_b, sent_b, edge, corr, scale)
    got_b = swap_b(send_b)
    lam_a, send_a = rim(1, False, *sensors, part_edges, got_a, sent_a, edge, corr, scale)
    got_a = swap_a(send_a)
    grads, mu, v = field_call(
        front_kernel,
        "front0",
        (*sensors, *release, inside, grad, part, lam_a, lam_b, coef, edge, corr, gain, scale),
        [SMEM] * 5 + [VMEM] * 9,
        [f32(slabs, *kept.shape), field, tall],
        [kept],
        10_000_000,
    )
    grads = lax.all_to_all(grads, "space", 0, 0, tiled=True)
    grads, mu, v = lax.optimization_barrier((grads, mu, v))
    return tuple(last_call(mu, v, coef, gain, got_a, got_b, edge, corr, grads))


def solution(mesh):
    in_specs = (
        P("sens", "space", None, None),
        P("sens", "space", None, None),
        P(None, "space", "sens", None),
        P(),
        P("sens"),
        P("sens", None),
        P(),
        P(),
    )
    out_specs = (P("sens", "space", None, None), P("sens", None))
    return jax.shard_map(body, mesh=mesh, in_specs=in_specs, out_specs=out_specs, check_vma=False)
```

```python
import functools

import jax
import jax.numpy as jnp
from jax import lax
from jax.experimental import pallas as pl
from jax.experimental.pallas import tpu as pltpu
from jax.sharding import PartitionSpec as P

STEPS = 3
DT = 0.12
PAD = 8
TILE = 8
CENTRE, ZP, ZM, YP, YM, ZPYP, ZPYM, ZMYP, ZMYM = range(9)
XP, XPZP, XPZM, XPYP, XPYM, XM, XMZP, XMZM, XMYP, XMYM = range(9, 19)
PLANES = 19
LOW = (ZM, ZMYP, ZMYM, XPZM, XMZM)
HIGH = (ZP, ZPYP, ZPYM, XPZP, XMZP)
IN_LAYER = (CENTRE, YP, YM, XP, XPYP, XPYM, XM, XMYP, XMYM)

VMEM = pl.BlockSpec(memory_space=pltpu.VMEM)
SMEM = pl.BlockSpec(memory_space=pltpu.SMEM)
ANY = pl.BlockSpec(memory_space=pl.ANY)


def f32(*shape):
    return jax.ShapeDtypeStruct(shape, jnp.float32)


def params(mib):
    return pltpu.CompilerParams(vmem_limit_bytes=mib * 1024 * 1024)


def cost(flops, moved):
    return pl.CostEstimate(flops=flops, bytes_accessed=moved, transcendentals=0)


def owned(owner_ref, slots):
    me = lax.axis_index("sens")
    o0, o1, o2 = (owner_ref[i] for i in range(3))
    own0 = lax.div(o0, slots) == me
    own1 = lax.div(o1, slots) == me
    first = jnp.where(own0, o0, jnp.where(own1, o1, o2))
    second = jnp.where(own0 & own1, o1, o2)
    return lax.rem(first, slots), lax.rem(second, slots)


def parity():
    return lax.rem(lax.axis_index("space"), 2)


def spot(cell, start, rows_y, rows_x):
    local = cell - start
    lifted = local + rows_y * rows_x
    z = lax.div(lifted, rows_y * rows_x) - 1
    y = lax.div(lax.rem(lifted, rows_y * rows_x), rows_x)
    return lifted, z, y, lax.rem(lifted, rows_x)


def pack_kernel(
    owner, sensors, misfit, adj, ckpt, disp, lam_a, lam_b, small_a, small_b, sems
):
    own, depth, rows_y, rows_x = adj.shape
    rows = disp.shape[2]
    plane = rows_y * rows_x
    start = lax.axis_index("space") * (depth * plane)
    even = parity() == 0
    z_a = jnp.where(even, depth - 1, 0)
    z_b = jnp.where(even, 0, depth - 1)
    held = owned(owner, ckpt.shape[0])
    moves = [(adj.at[:, z_a], lam_a), (adj.at[:, z_b], lam_b)]
    for z, small in ((z_a, small_a), (z_b, small_b)):
        for j in range(2):
            moves.append((ckpt.at[held[j], z], small.at[pl.ds(j * rows_y, rows_y)]))
        for j, comp in enumerate((0, 3, 4)):
            moves.append((disp.at[comp, z], small.at[pl.ds(2 * rows_y + j * rows, rows)]))
    copies = [pltpu.make_async_copy(s, d, sems.at[i]) for i, (s, d) in enumerate(moves)]
    for c in copies:
        c.start()

    lanes = lax.broadcasted_iota(jnp.int32, (1, rows_x), 1)
    for c in copies[:2]:
        c.wait()
    for k in range(own):
        lifted, z, y, x = spot(sensors[k], start, rows_y, rows_x)
        mine = (lifted >= plane) & (lifted < (depth + 1) * plane)

        for edge, lam in ((z_a, lam_a), (z_b, lam_b)):

            @pl.when(mine & (z == edge))
            def _(k=k, y=y, x=x, lam=lam):
                lam[k, pl.ds(y, 1), :] += jnp.where(lanes == x, misfit[STEPS - 1, k], 0.0)

    for c in copies[2:]:
        c.wait()


def pack(owner, sensors, misfit, adj, ckpt, disp):
    own, depth, rows_y, rows_x = adj.shape
    rows = disp.shape[2]
    small = f32(2 * rows_y + 3 * rows, rows_x)
    return pl.pallas_call(
        pack_kernel,
        in_specs=[SMEM] * 3 + [ANY] * 3,
        out_specs=[VMEM] * 4,
        out_shape=[f32(own, rows_y, rows_x)] * 2 + [small, small],
        scratch_shapes=[pltpu.SemaphoreType.DMA((12,))],
        compiler_params=params(60),
        cost_estimate=cost(20_000_000_000, 60_000_000),
        name="pack",
    )(owner, sensors, misfit, adj, ckpt, disp)


def lane_masks(shape):
    lanes = lax.broadcasted_iota(jnp.int32, shape, len(shape) - 1)
    return lanes >= 1, lanes < shape[-1] - 1


def before(value, keep):
    return jnp.where(keep, pltpu.roll(value, 1, axis=value.ndim - 1), 0.0)


def after(value, keep):
    return jnp.where(keep, pltpu.roll(value, value.shape[-1] - 1, axis=value.ndim - 1), 0.0)


def planes_at(window, keep_b, keep_a):
    def yy(dy):
        return window(1, 0, dy)

    c = [None] * PLANES
    zz, zzp, zzm = window(0, 0, 0), window(0, 1, 0), window(0, -1, 0)
    xx = window(2, 0, 0)
    c[ZP], c[ZM] = 0.5 * (zz + zzp), 0.5 * (zz + zzm)
    c[YP], c[YM] = 0.5 * (yy(0) + yy(1)), 0.5 * (yy(0) + yy(-1))
    xx_b, xx_a = before(xx, keep_b), after(xx, keep_a)
    c[XP] = jnp.where(keep_b, 0.5 * (xx_b + xx), 0.0)
    c[XM] = jnp.where(keep_a, 0.5 * (xx_a + xx), 0.0)
    c[CENTRE] = -(c[ZP] + c[ZM] + c[YP] + c[YM] + (xx + 0.5 * (xx_a + xx_b)))
    zp, zm, yp, ym = window(3, 1, 0), window(3, -1, 0), window(3, 0, 1), window(3, 0, -1)
    c[ZPYP], c[ZPYM] = 0.25 * (zp + yp), -0.25 * (zp + ym)
    c[ZMYP], c[ZMYM] = -0.25 * (zm + yp), 0.25 * (zm + ym)
    for comp, plus, minus, names in (
        (4, window(4, 1, 0), window(4, -1, 0), (XPZP, XPZM, XMZP, XMZM)),
        (5, window(5, 0, 1), window(5, 0, -1), (XPYP, XPYM, XMYP, XMYM)),
    ):
        here = window(comp, 0, 0)
        c[names[0]] = jnp.where(keep_b, 0.25 * (before(plus, keep_b) + here), 0.0)
        c[names[1]] = jnp.where(keep_b, -0.25 * (before(minus, keep_b) + here), 0.0)
        c[names[2]] = jnp.where(keep_a, -0.25 * (after(plus, keep_a) + here), 0.0)
        c[names[3]] = jnp.where(keep_a, 0.25 * (after(minus, keep_a) + here), 0.0)
    return c


def stencil(c, u):
    near = {(dz, dy): u(dz, dy) for dz in (-1, 0, 1) for dy in (-1, 0, 1)}
    here = c[CENTRE] * near[0, 0] + c[ZP] * near[1, 0] + c[ZM] * near[-1, 0]
    here += c[YP] * near[0, 1] + c[YM] * near[0, -1]
    here += c[ZPYP] * near[1, 1] + c[ZPYM] * near[1, -1]
    here += c[ZMYP] * near[-1, 1] + c[ZMYM] * near[-1, -1]
    right = c[XP] * near[0, 0] + c[XPZP] * near[1, 0] + c[XPZM] * near[-1, 0]
    right += c[XPYP] * near[0, 1] + c[XPYM] * near[0, -1]
    left = c[XM] * near[0, 0] + c[XMZP] * near[1, 0] + c[XMZM] * near[-1, 0]
    left += c[XMYP] * near[0, 1] + c[XMYM] * near[0, -1]
    width = here.shape[-1]
    return here + pltpu.roll(right, width - 1, axis=1) + pltpu.roll(left, 1, axis=1)


def scale_of(conc):
    root = jnp.sqrt(conc)
    return DT * root / (root + 0.5)


def slope_of(conc):
    root = jnp.sqrt(conc)
    return (0.25 * DT) / (root * (root + 0.5) * (root + 0.5))


def planes_kernel(count, *refs):
    owner = refs[0]
    parts, states = refs[1 : 1 + count], refs[1 + count : 1 + 2 * count]
    coef, gain, scale, ends, full, conc = refs[1 + 2 * count :]
    depth, rows_y, rows_x = coef.shape[1:]
    rows = rows_y // count
    slots = states[0].shape[0]
    me = lax.axis_index("sens")
    inner = pl.ds(PAD, rows_y)

    blank = jnp.zeros((PAD, rows_x), jnp.float32)
    void = jnp.zeros((rows_y + 2 * PAD, rows_x), jnp.float32)
    for ref in (full, conc):
        for i in range(ref.shape[0]):
            ref[i, 0] = void
            ref[i, depth + 1] = void
            for z in range(depth):
                ref[i, z + 1, pl.ds(0, PAD)] = blank
                ref[i, z + 1, pl.ds(PAD + rows_y, PAD)] = blank
    for k in range(count):
        who = lax.rem(me - k + count, count)
        span = pl.ds(pl.multiple_of(PAD + who * rows, PAD), rows)
        for comp in range(6):
            for z in range(depth):
                full[comp, z + 1, span] = parts[k][comp, z]
    for i in range(STEPS):
        turn = lax.rem(me - lax.div(owner[i], slots) + count, count)
        slot = lax.rem(owner[i], slots)
        for k in range(count):

            @pl.when(turn == k)
            def _(i=i, k=k, slot=slot):
                conc[i, pl.ds(1, depth), inner] = states[k][slot]

        for side in range(2):
            ends[i, side] = conc[i, 1 + side * (depth - 1), inner]

    keep_b, keep_a = lane_masks((TILE, rows_x))

    def layer(z, carry):
        for tile in range(rows_y // TILE):
            at = pl.ds(tile * TILE, TILE)

            def window(comp, dz, dy):
                return full[comp, z + 1 + dz, pl.ds(PAD + tile * TILE + dy, TILE)]

            c = planes_at(window, keep_b, keep_a)
            for j in range(PLANES):
                coef[j, z, at] = c[j]
            for i in range(STEPS):
                here = conc[i, z + 1, pl.ds(PAD + tile * TILE, TILE)]
                spread = stencil(
                    c, lambda dz, dy: conc[i, z + 1 + dz, pl.ds(PAD + tile * TILE + dy, TILE)]
                )
                scale[i, z, at] = scale_of(here)
                gain[i, z, at] = 1.0 + slope_of(here) * spread
        return carry

    lax.fori_loop(0, depth, layer, 0)


def planes(owner, parts, states):
    count = len(parts)
    depth, rows_y, rows_x = states[0].shape[1:]
    grown = rows_y + 2 * PAD
    return pl.pallas_call(
        functools.partial(planes_kernel, count),
        in_specs=[SMEM] + [VMEM] * (2 * count),
        out_specs=[VMEM] * 4,
        out_shape=[
            f32(PLANES, depth, rows_y, rows_x),
            f32(STEPS, depth, rows_y, rows_x),
            f32(STEPS, depth, rows_y, rows_x),
            f32(STEPS, 2, rows_y, rows_x),
        ],
        scratch_shapes=[
            pltpu.VMEM((6, depth + 2, grown, rows_x), jnp.float32),
            pltpu.VMEM((STEPS, depth + 2, grown, rows_x), jnp.float32),
        ],
        compiler_params=params(24),
        cost_estimate=cost(2_000_000_000, 60_000_000),
        name="planes",
    )(owner, *parts, *states)


def ends_kernel(count, slots, *refs):
    owner, coef, ends = refs[:3]
    small = refs[3 : 3 + count], refs[3 + count : 3 + 2 * count]
    edge, edge_raw, corr, tensor, conc = refs[3 + 2 * count :]
    depth, rows_y, rows_x = coef.shape[1:]
    rows = rows_y // count
    me = lax.axis_index("sens")
    side_a = 1 - parity()
    inner = pl.ds(PAD, rows_y)
    blank = jnp.zeros((PAD, rows_x), jnp.float32)
    for side in range(2):
        for i in range(STEPS):
            conc[side, i, pl.ds(0, PAD)] = blank
            conc[side, i, pl.ds(PAD + rows_y, PAD)] = blank
    for k in range(count):
        who = lax.rem(me - k + count, count)
        span = pl.ds(pl.multiple_of(who * rows, PAD), rows)
        for j in range(3):
            here = pl.ds(2 * rows_y + j * rows, rows)
            tensor[side_a, j, span] = small[0][k][here]
            tensor[1 - side_a, j, span] = small[1][k][here]
    holders = [lax.div(owner[i], slots) for i in range(STEPS)]
    for i in range(STEPS):
        slot = jnp.int32(0)
        for j in range(i):
            slot += jnp.where(holders[j] == holders[i], 1, 0)
        slot = jnp.minimum(slot, 1)
        turn = lax.rem(me - holders[i] + count, count)
        for k in range(count):

            @pl.when(turn == k)
            def _(i=i, k=k, slot=slot):
                span = pl.ds(pl.multiple_of(slot * rows_y, PAD), rows_y)
                conc[side_a, i, inner] = small[0][k][span]
                conc[1 - side_a, i, inner] = small[1][k][span]

    keep_b, keep_a = lane_masks((TILE, rows_x))
    ys = lax.broadcasted_iota(jnp.int32, (TILE, rows_x), 0)
    for side, z, names in ((0, 0, LOW), (1, depth - 1, HIGH)):
        sign = 2 * side - 1
        for tile in range(rows_y // TILE):
            at = pl.ds(tile * TILE, TILE)
            zz, zy, zx = (tensor[side, j, at] for j in range(3))
            e = [coef[names[j], z, at] for j in range(5)]
            e[0] += 0.5 * zz
            e[1] += (0.25 * sign) * zy
            e[2] -= (0.25 * sign) * zy
            e[3] += (0.25 * sign) * before(zx, keep_b)
            e[4] -= (0.25 * sign) * after(zx, keep_a)
            if tile == rows_y // TILE - 1:
                e[1] = jnp.where(ys < TILE - 1, e[1], 0.0)
            if tile == 0:
                e[2] = jnp.where(ys > 0, e[2], 0.0)
            near = [
                [conc[side, i, pl.ds(PAD + tile * TILE + d, TILE)] for d in (0, 1, -1)]
                for i in range(STEPS)
            ]
            for j in range(5):
                edge[side, j, at] = e[j]
                edge_raw[side, j, at] = e[j] * scale_of(near[STEPS - 1][(0, 1, 2, 0, 0)[j]])
            for i in range(STEPS):
                here, up, down = near[i]
                own = ends[i, side, at]
                spread = e[0] * here + e[1] * up + e[2] * down - 0.5 * zz * own
                spread += pltpu.roll(e[3] * here, rows_x - 1, axis=1)
                spread += pltpu.roll(e[4] * here, 1, axis=1)
                gain, scale = slope_of(own) * spread, scale_of(own)
                if i == STEPS - 1:
                    corr[i, side, at] = gain - 0.5 * zz * scale
                else:
                    corr[i, side, at] = gain / scale - 0.5 * zz


def ends_call(owner, coef, ends, small_a, small_b, slots):
    count = len(small_a)
    _, _, rows_y, rows_x = coef.shape
    return pl.pallas_call(
        functools.partial(ends_kernel, count, slots),
        in_specs=[SMEM] + [VMEM] * (2 + 2 * count),
        out_specs=[VMEM] * 3,
        out_shape=[
            f32(2, 5, rows_y, rows_x),
            f32(2, 5, rows_y, rows_x),
            f32(STEPS, 2, rows_y, rows_x),
        ],
        scratch_shapes=[
            pltpu.VMEM((2, 3, rows_y, rows_x), jnp.float32),
            pltpu.VMEM((2, STEPS, rows_y + 2 * PAD, rows_x), jnp.float32),
        ],
        compiler_params=params(16),
        cost_estimate=cost(1_000_000, 1_000_000),
        name="ends",
    )(owner, coef, ends, *small_a, *small_b)


def gather_field(first, lam, lam_a, lam_b, mu):
    own, depth = mu.shape[:2]
    for k in range(own):
        for z in range(depth):
            if first or 0 < z < depth - 1:
                mu[k, z] = lam[k, z]
    if not first:
        z_a = jnp.where(parity() == 0, depth - 1, 0)
        for k in range(own):
            mu[k, z_a] = lam_a[k]
            mu[k, depth - 1 - z_a] = lam_b[k]


def add_misfit(step, sensors, misfit, mu, skip=0):
    own, depth, rows_y, rows_x = mu.shape
    plane = rows_y * rows_x
    start = lax.axis_index("space") * (depth * plane)
    lanes = lax.broadcasted_iota(jnp.int32, (1, rows_x), 1)
    for k in range(own):
        lifted, z, y, x = spot(sensors[k], start, rows_y, rows_x)

        @pl.when((lifted >= (1 + skip) * plane) & (lifted < (depth + 1 - skip) * plane))
        def _(k=k, z=z, y=y, x=x):
            mu[k, z, pl.ds(y, 1), :] += jnp.where(lanes == x, misfit[step, k], 0.0)


def scale_field(scale, step, mu, v):
    own, depth, rows_y, rows_x = mu.shape
    blank = jnp.zeros((PAD, rows_x), jnp.float32)
    void = jnp.zeros((rows_y + 2 * PAD, rows_x), jnp.float32)
    for k in range(own):
        v[k, 0] = void
        v[k, depth + 1] = void
        for z in range(depth):
            v[k, z + 1, pl.ds(0, PAD)] = blank
            v[k, z + 1, pl.ds(PAD + rows_y, PAD)] = blank
            v[k, z + 1, pl.ds(PAD, rows_y)] = scale[step, z] * mu[k, z]


def spread_field(coef, gain, step, mu, v, part, part_edges=None):
    own, depth, rows_y, rows_x = mu.shape

    def layer(z, carry):
        for tile in range(rows_y // TILE):
            at = pl.ds(tile * TILE, TILE)
            c = [coef[j, z, at] for j in range(PLANES)]
            keep = gain[step, z, at]
            for k in range(own):
                spread = stencil(
                    c, lambda dz, dy: v[k, z + 1 + dz, pl.ds(PAD + tile * TILE + dy, TILE)]
                )
                part[k, z, at] = mu[k, z, at] * keep + spread
        return carry

    lax.fori_loop(0, depth, layer, 0)
    if part_edges is not None:
        for k in range(own):
            part_edges[0, k] = part[k, 0]
            part_edges[1, k] = part[k, depth - 1]


def taker(total, own, rows_x):
    lanes = lax.broadcasted_iota(jnp.int32, (1, rows_x), 1)
    slots = lax.broadcasted_iota(jnp.int32, (own, total.shape[1]), 1)

    def take(r, x, row):
        value = jnp.sum(jnp.where(lanes == x, row, 0.0), axis=-1, keepdims=True)
        total[...] += jnp.where(slots == r, value, 0.0)

    return take


def collect(wanted, release, shape, total, own_row):
    cells, steps, inside = release
    own, depth, rows_y, rows_x = shape
    start = lax.axis_index("space") * (depth * rows_y * rows_x)
    take = taker(total, own, rows_x)

    def visit(i, carry):
        r = inside[i]
        _, z, y, x = spot(cells[r], start, rows_y, rows_x)

        @pl.when((steps[r] == wanted) & (z >= 0) & (z < depth))
        def _():
            take(r, x, own_row(z, y))

        return carry

    lax.fori_loop(0, inside[inside.shape[0] - 1], visit, 0)


def list_releases(cells, shape, inside):
    own, depth, rows_y, rows_x = shape
    plane = rows_y * rows_x
    start = lax.axis_index("space") * (depth * plane)

    def note(r, found):
        local = cells[r] - start
        inside[found] = r
        return found + jnp.where((local >= -plane) & (local < (depth + 1) * plane), 1, 0)

    inside[inside.shape[0] - 1] = lax.fori_loop(0, cells.shape[0], note, jnp.int32(0))


def rows_of(ref, *index):
    row = ref[(slice(None), *index, slice(None))]
    return row.reshape(row.shape[0], row.shape[-1])


def first_kernel(sensors, misfit, lam, coef, gain, scale, part, part_edges, v, mu):
    gather_field(True, lam, None, None, mu)
    add_misfit(STEPS - 1, sensors, misfit, mu)
    scale_field(scale, STEPS - 1, mu, v)
    spread_field(coef, gain, STEPS - 1, mu, v, part, part_edges)


def middle_kernel(
    sensors, misfit, cells, steps, lam, lam_a, lam_b, coef, gain, scale, base, part_edges, grad, inside, v, mu, part
):
    own, depth, rows_y, rows_x = mu.shape
    gather_field(False, lam, lam_a, lam_b, mu)
    grad[...] = jnp.zeros_like(grad)
    list_releases(cells, mu.shape, inside)
    release = (cells, steps, inside)
    collect(2, release, mu.shape, grad, lambda z, y: rows_of(mu, z, pl.ds(y, 1)))
    add_misfit(1, sensors, misfit, mu)
    scale_field(scale, 1, mu, v)
    spread_field(coef, gain, 1, mu, v, part, part_edges)

    void = jnp.zeros((rows_y, rows_x), jnp.float32)
    for k in range(own):
        mu[k, 0] = void
        mu[k, depth - 1] = void
        for z in range(1, depth - 1):
            mu[k, z] = part[k, z]
    collect(1, release, mu.shape, grad, lambda z, y: rows_of(mu, z, pl.ds(y, 1)))
    add_misfit(0, sensors, misfit, mu, 1)
    scale_field(scale, 0, mu, v)
    spread_field(coef, gain, 0, mu, v, base)

    def own_row(z, y):
        at = pl.ds(y, 1)
        c = [coef[j, z, at] for j in range(PLANES)]
        spread = stencil(c, lambda dz, dy: rows_of(v, z + 1 + dz, pl.ds(PAD + y + dy, 1)))
        return rows_of(mu, z, at) * gain[0, z, at] + spread

    collect(0, release, mu.shape, grad, own_row)


def in_layer(c, here, up, down):
    width = here.shape[-1]
    value = c[0] * here + c[1] * up + c[2] * down
    right = c[3] * here + c[4] * up + c[5] * down
    left = c[6] * here + c[7] * up + c[8] * down
    return value + pltpu.roll(right, width - 1, axis=1) + pltpu.roll(left, 1, axis=1)


def front_kernel(
    cells, steps, inside, grad_in, lam_a, lam_b, sent_a, sent_b, coef, edge, corr, gain, scale, grads, ve, total
):
    own, rows_y, rows_x = lam_a.shape
    depth = coef.shape[1]
    start = lax.axis_index("space") * (depth * rows_y * rows_x)
    side_a = 1 - parity()
    blank = jnp.zeros((PAD, rows_x), jnp.float32)
    for k in range(own):
        for side in range(2):
            ve[side, k, pl.ds(0, PAD)] = blank
            ve[side, k, pl.ds(PAD + rows_y, PAD)] = blank
        ve[side_a, k, pl.ds(PAD, rows_y)] = sent_a[k]
        ve[1 - side_a, k, pl.ds(PAD, rows_y)] = sent_b[k]
    total[...] = grad_in[...]
    take = taker(total, own, rows_x)

    def visit(i, carry):
        r = inside[i]
        _, z, y, x = spot(cells[r], start, rows_y, rows_x)
        step = steps[r]
        at = pl.ds(y, 1)
        for lam, side in ((lam_a, side_a), (lam_b, 1 - side_a)):

            @pl.when((step == 1) & (z == side * (depth - 1)))
            def _(lam=lam):
                take(r, x, rows_of(lam, at))

        for side, names in ((0, LOW), (1, HIGH)):
            out = 2 * side - 1
            end = side * (depth - 1)

            def near(side=side):
                return [rows_of(ve.at[side], pl.ds(PAD + y + d, 1)) for d in (0, 1, -1)]

            @pl.when((step == 0) & (z == end))
            def _(side=side, end=end, near=near):
                here, up, down = near()
                value = in_layer([coef[j, end, at] for j in IN_LAYER], here, up, down)
                keep = gain[0, end, at] / scale[0, end, at] + corr[0, side, at]
                take(r, x, value + keep * here)

            @pl.when((step == 0) & (z == end - out))
            def _(end=end, out=out, names=names, near=near):
                take(r, x, from_met([coef[j, end - out, at] for j in names], *near()))

            @pl.when((step == 0) & (z == end + out))
            def _(side=side, near=near):
                here, up, down = near()
                value = edge[side, 0, at] * here
                value += edge[side, 1, pl.ds(jnp.maximum(y - 1, 0), 1)] * down
                value += edge[side, 2, pl.ds(jnp.minimum(y + 1, rows_y - 1), 1)] * up
                value += edge[side, 3, at] * pltpu.roll(here, 1, axis=1)
                value += edge[side, 4, at] * pltpu.roll(here, rows_x - 1, axis=1)
                take(r, x, value)

        return carry

    lax.fori_loop(0, inside[inside.shape[0] - 1], visit, 0)
    for i in range(grads.shape[0]):
        grads[i] = total[...]


def field_call(kernel, name, args, specs, outs, scratch, flops, listed=0):
    return pl.pallas_call(
        kernel,
        in_specs=specs,
        out_specs=[VMEM] * len(outs) + [SMEM] * (listed > 0),
        out_shape=outs + [jax.ShapeDtypeStruct((listed,), jnp.int32)] * (listed > 0),
        scratch_shapes=[pltpu.VMEM(o.shape, jnp.float32) for o in scratch],
        compiler_params=params(32),
        cost_estimate=cost(flops, 4_000_000),
        name=name,
    )(*args)


def met(got, k, tile, tiles):
    here = got[k, pl.ds(tile * TILE, TILE)]
    if tile == tiles - 1:
        up = pltpu.roll(here, TILE - 1, axis=0)
    else:
        up = got[k, pl.ds(tile * TILE + 1, TILE)]
    if tile == 0:
        down = pltpu.roll(here, 1, axis=0)
    else:
        down = got[k, pl.ds(tile * TILE - 1, TILE)]
    return here, up, down


def from_met(c, here, up, down):
    width = here.shape[-1]
    value = c[0] * here + c[1] * up + c[2] * down
    value += pltpu.roll(c[3] * here, width - 1, axis=1)
    return value + pltpu.roll(c[4] * here, 1, axis=1)


def rim_kernel(step, late, sensors, misfit, part_edges, got, sent, edge, corr, scale, lam, send):
    depth = scale.shape[1]
    own, rows_y, rows_x = got.shape
    tiles = rows_y // TILE
    side = parity() if late else 1 - parity()
    z = side * (depth - 1)
    for tile in range(tiles):
        at = pl.ds(tile * TILE, TILE)
        c = [edge[side, j, at] for j in range(5)]
        miss = corr[step, side, at]
        gain = scale[step - 1, z, at]
        for k in range(own):
            value = part_edges[side, k, at] + miss * sent[k, at]
            value += from_met(c, *met(got, k, tile, tiles))
            lam[k, at] = value
            send[k, at] = gain * value
    plane = rows_y * rows_x
    start = lax.axis_index("space") * (depth * plane)
    lanes = lax.broadcasted_iota(jnp.int32, (1, rows_x), 1)
    for k in range(own):
        lifted, at_z, y, x = spot(sensors[k], start, rows_y, rows_x)
        here = (lifted >= plane) & (lifted < (depth + 1) * plane)

        @pl.when(here & (at_z == z))
        def _(k=k, y=y, x=x):
            add = jnp.where(lanes == x, misfit[step - 1, k], 0.0)
            send[k, pl.ds(y, 1), :] += add * scale[step - 1, z, pl.ds(y, 1), :]


def rim(step, late, sensors, misfit, part_edges, got, sent, edge, corr, scale):
    return pl.pallas_call(
        functools.partial(rim_kernel, step, late),
        in_specs=[SMEM] * 2 + [VMEM] * 6,
        out_specs=[VMEM] * 2,
        out_shape=[f32(*got.shape)] * 2,
        compiler_params=params(16),
        cost_estimate=cost(2_000_000, 1_500_000),
        name=f"rim{step}{'b' if late else 'a'}",
    )(sensors, misfit, part_edges, got, sent, edge, corr, scale)


def last_kernel(base, ve, coef, gain, scale, got_a, got_b, edge, corr, grads, out, grad, part, sems):
    own, depth, rows_y, rows_x = base.shape
    tiles = rows_y // TILE
    copies = [
        pltpu.make_async_copy(base.at[:, z], out.at[:, z], sems.at[z]) for z in range(2, depth - 2)
    ]
    for c in copies:
        c.start()
    side_a = 1 - parity()
    for turn, (got, side) in enumerate(((got_b, 1 - side_a), (got_a, side_a))):
        end = side * (depth - 1)
        inner = end + 1 - 2 * side
        for tile in range(tiles):
            at = pl.ds(tile * TILE, TILE)
            ce = [coef[j, end, at] for j in IN_LAYER]
            ci = [coef[jnp.where(side == 0, low, high), inner, at] for low, high in zip(LOW, HIGH)]
            cm = [edge[side, j, at] for j in range(5)]
            keep = gain[0, end, at] / scale[0, end, at] + corr[0, side, at]
            for k in range(own):
                here, up, down = (
                    ve[side, k, pl.ds(PAD + tile * TILE + d, TILE)] for d in (0, 1, -1)
                )
                value = base[k, end, at] + keep * here + in_layer(ce, here, up, down)
                part[k, end, at] = value + from_met(cm, *met(got, k, tile, tiles))
                part[k, inner, at] = base[k, inner, at] + from_met(ci, here, up, down)
        for z, sem in ((end, turn), (inner, depth - 1 - turn)):
            copies.append(pltpu.make_async_copy(part.at[:, z], out.at[:, z], sems.at[sem]))
            copies[-1].start()
    total = grads[0]
    for i in range(1, grads.shape[0]):
        total += grads[i]
    grad[...] = total
    for c in copies:
        c.wait()


def last_call(base, ve, coef, gain, scale, got_a, got_b, edge, corr, grads):
    return pl.pallas_call(
        last_kernel,
        in_specs=[VMEM] * 10,
        out_specs=[ANY, VMEM],
        out_shape=[f32(*base.shape), f32(*grads.shape[1:])],
        scratch_shapes=[
            pltpu.VMEM(base.shape, jnp.float32),
            pltpu.SemaphoreType.DMA((base.shape[1],)),
        ],
        compiler_params=params(16),
        cost_estimate=cost(10_000_000, 6_000_000),
        name="step0",
    )(base, ve, coef, gain, scale, got_a, got_b, edge, corr, grads)


def turned(array, axis):
    count = lax.axis_size(axis)
    return [array] + [
        lax.ppermute(array, axis, [(i, (i + k) % count) for i in range(count)])
        for k in range(1, count)
    ]


def body(
    adjoint_end,
    checkpoints,
    dispersion,
    owner_steps,
    sensor_cells,
    misfit,
    release_cells,
    release_steps,
):
    own, depth, rows_y, rows_x = adjoint_end.shape
    slabs = lax.axis_size("space")
    pairs_a = [(i, i ^ 1) for i in range(slabs)]
    pairs_b = [(i, ((i + 1) ^ 1) - 1) for i in range(1, slabs - 1)]
    misfit = misfit.T

    def swap_a(x):
        return lax.ppermute(x, "space", pairs_a)

    def swap_b(x):
        return lax.ppermute(x, "space", pairs_b)

    parts, states = turned(dispersion, "sens"), turned(checkpoints, "sens")
    sent_a, sent_b, small_a, small_b = pack(
        owner_steps, sensor_cells, misfit, adjoint_end, checkpoints, dispersion
    )
    small_a, small_b = swap_a(small_a), swap_b(small_b)
    parts, states, sent_a, sent_b = lax.optimization_barrier((parts, states, sent_a, sent_b))
    got_a, got_b = swap_a(sent_a), swap_b(sent_b)
    small_a, small_b, parts = lax.optimization_barrier((small_a, small_b, parts))
    small_a, small_b = turned(small_a, "sens"), turned(small_b, "sens")
    coef, gain, scale, ends = planes(owner_steps, parts, states)

    field = f32(own, depth, rows_y, rows_x)
    edges = f32(2, own, rows_y, rows_x)
    tall = f32(own, depth + 2, rows_y + 2 * PAD, rows_x)
    kept = f32(own, release_cells.shape[0])
    sensors = (sensor_cells, misfit)
    release = (release_cells, release_steps)

    part, part_edges = field_call(
        first_kernel,
        "step2",
        (*sensors, adjoint_end, coef, gain, scale),
        [SMEM] * 2 + [VMEM, VMEM, VMEM, VMEM],
        [field, edges],
        [tall, field],
        40_000_000,
    )
    small_a, small_b, part_edges = lax.optimization_barrier((small_a, small_b, part_edges))
    edge, edge_raw, corr = ends_call(
        owner_steps, coef, ends, small_a, small_b, checkpoints.shape[0]
    )
    lam_b, send_b = rim(2, True, *sensors, part_edges, got_b, sent_b, edge_raw, corr, scale)
    got_b = swap_b(send_b)
    lam_a, send_a = rim(2, False, *sensors, part_edges, got_a, sent_a, edge_raw, corr, scale)
    got_a = swap_a(send_a)
    base, part_edges, grad, inside = field_call(
        middle_kernel,
        "step1",
        (*sensors, *release, part, lam_a, lam_b, coef, gain, scale),
        [SMEM] * 4 + [VMEM] * 6,
        [field, edges, kept],
        [tall, field, field],
        40_000_000,
        release_cells.shape[0] + 1,
    )
    sent_a, sent_b = send_a, send_b
    lam_b, send_b = rim(1, True, *sensors, part_edges, got_b, sent_b, edge, corr, scale)
    got_b = swap_b(send_b)
    lam_a, send_a = rim(1, False, *sensors, part_edges, got_a, sent_a, edge, corr, scale)
    got_a = swap_a(send_a)
    halo = f32(2, own, rows_y + 2 * PAD, rows_x)
    grads, ve = field_call(
        front_kernel,
        "front0",
        (*release, inside, grad, lam_a, lam_b, send_a, send_b, coef, edge, corr, gain, scale),
        [SMEM] * 3 + [VMEM] * 10,
        [f32(slabs, *kept.shape), halo],
        [kept],
        10_000_000,
    )
    grads = lax.all_to_all(grads, "space", 0, 0, tiled=True)
    grads, ve = lax.optimization_barrier((grads, ve))
    return tuple(last_call(base, ve, coef, gain, scale, got_a, got_b, edge, corr, grads))


def solution(mesh):
    in_specs = (
        P("sens", "space", None, None),
        P("sens", "space", None, None),
        P(None, "space", "sens", None),
        P(),
        P("sens"),
        P("sens", None),
        P(),
        P(),
    )
    out_specs = (P("sens", "space", None, None), P("sens", None))
    return jax.shard_map(body, mesh=mesh, in_specs=in_specs, out_specs=out_specs, check_vma=False)
```

```python
import functools

import jax
import jax.numpy as jnp
from jax import lax
from jax.experimental import pallas as pl
from jax.experimental.pallas import tpu as pltpu
from jax.sharding import PartitionSpec as P

STEPS = 3
DT = 0.12
PAD = 8
TILE = 8
CENTRE, ZP, ZM, YP, YM, ZPYP, ZPYM, ZMYP, ZMYM = range(9)
XP, XPZP, XPZM, XPYP, XPYM, XM, XMZP, XMZM, XMYP, XMYM = range(9, 19)
PLANES = 19
LOW = (ZM, ZMYP, ZMYM, XPZM, XMZM)
HIGH = (ZP, ZPYP, ZPYM, XPZP, XMZP)
GROUPS = (
    (
        (CENTRE, 0, 0),
        (ZP, 1, 0),
        (ZM, -1, 0),
        (YP, 0, 1),
        (YM, 0, -1),
        (ZPYP, 1, 1),
        (ZPYM, 1, -1),
        (ZMYP, -1, 1),
        (ZMYM, -1, -1),
    ),
    ((XP, 0, 0), (XPZP, 1, 0), (XPZM, -1, 0), (XPYP, 0, 1), (XPYM, 0, -1)),
    ((XM, 0, 0), (XMZP, 1, 0), (XMZM, -1, 0), (XMYP, 0, 1), (XMYM, 0, -1)),
)
IN_LAYER = (CENTRE, YP, YM, XP, XPYP, XPYM, XM, XMYP, XMYM)

VMEM = pl.BlockSpec(memory_space=pltpu.VMEM)
SMEM = pl.BlockSpec(memory_space=pltpu.SMEM)
ANY = pl.BlockSpec(memory_space=pl.ANY)


def f32(*shape):
    return jax.ShapeDtypeStruct(shape, jnp.float32)


def params(mib):
    return pltpu.CompilerParams(vmem_limit_bytes=mib * 1024 * 1024)


def cost(flops, moved):
    return pl.CostEstimate(flops=flops, bytes_accessed=moved, transcendentals=0)


def owned(owner_ref, slots):
    me = lax.axis_index("sens")
    o0, o1, o2 = (owner_ref[i] for i in range(3))
    own0 = lax.div(o0, slots) == me
    own1 = lax.div(o1, slots) == me
    first = jnp.where(own0, o0, jnp.where(own1, o1, o2))
    second = jnp.where(own0 & own1, o1, o2)
    return lax.rem(first, slots), lax.rem(second, slots)


def parity():
    return lax.rem(lax.axis_index("space"), 2)


def spot(cell, start, rows_y, rows_x):
    local = cell - start
    lifted = local + rows_y * rows_x
    z = lax.div(lifted, rows_y * rows_x) - 1
    y = lax.div(lax.rem(lifted, rows_y * rows_x), rows_x)
    return lifted, z, y, lax.rem(lifted, rows_x)


def pack_kernel(
    owner, sensors, misfit, adj, ckpt, disp, lam_a, lam_b, small_a, small_b, sems
):
    own, depth, rows_y, rows_x = adj.shape
    rows = disp.shape[2]
    plane = rows_y * rows_x
    start = lax.axis_index("space") * (depth * plane)
    even = parity() == 0
    z_a = jnp.where(even, depth - 1, 0)
    z_b = jnp.where(even, 0, depth - 1)
    held = owned(owner, ckpt.shape[0])
    moves = [(adj.at[:, z_a], lam_a), (adj.at[:, z_b], lam_b)]
    for z, small in ((z_a, small_a), (z_b, small_b)):
        for j in range(2):
            moves.append((ckpt.at[held[j], z], small.at[pl.ds(j * rows_y, rows_y)]))
        for j, comp in enumerate((0, 3, 4)):
            moves.append((disp.at[comp, z], small.at[pl.ds(2 * rows_y + j * rows, rows)]))
    copies = [pltpu.make_async_copy(s, d, sems.at[i]) for i, (s, d) in enumerate(moves)]
    for c in copies:
        c.start()

    lanes = lax.broadcasted_iota(jnp.int32, (1, rows_x), 1)
    for c in copies[:2]:
        c.wait()
    for k in range(own):
        lifted, z, y, x = spot(sensors[k], start, rows_y, rows_x)
        mine = (lifted >= plane) & (lifted < (depth + 1) * plane)

        for edge, lam in ((z_a, lam_a), (z_b, lam_b)):

            @pl.when(mine & (z == edge))
            def _(k=k, y=y, x=x, lam=lam):
                lam[k, pl.ds(y, 1), :] += jnp.where(lanes == x, misfit[STEPS - 1, k], 0.0)

    for c in copies[2:]:
        c.wait()


def pack(owner, sensors, misfit, adj, ckpt, disp):
    own, depth, rows_y, rows_x = adj.shape
    rows = disp.shape[2]
    small = f32(2 * rows_y + 3 * rows, rows_x)
    return pl.pallas_call(
        pack_kernel,
        in_specs=[SMEM] * 3 + [ANY] * 3,
        out_specs=[VMEM] * 4,
        out_shape=[f32(own, rows_y, rows_x)] * 2 + [small, small],
        scratch_shapes=[pltpu.SemaphoreType.DMA((12,))],
        compiler_params=params(60),
        cost_estimate=cost(20_000_000_000, 60_000_000),
        name="pack",
    )(owner, sensors, misfit, adj, ckpt, disp)


def lane_masks(shape):
    lanes = lax.broadcasted_iota(jnp.int32, shape, len(shape) - 1)
    return lanes >= 1, lanes < shape[-1] - 1


def before(value, keep):
    return jnp.where(keep, pltpu.roll(value, 1, axis=value.ndim - 1), 0.0)


def after(value, keep):
    return jnp.where(keep, pltpu.roll(value, value.shape[-1] - 1, axis=value.ndim - 1), 0.0)


def planes_at(window, keep_b, keep_a):
    def yy(dy):
        return window(1, 0, dy)

    c = [None] * PLANES
    zz, zzp, zzm = window(0, 0, 0), window(0, 1, 0), window(0, -1, 0)
    xx = window(2, 0, 0)
    c[ZP], c[ZM] = 0.5 * (zz + zzp), 0.5 * (zz + zzm)
    c[YP], c[YM] = 0.5 * (yy(0) + yy(1)), 0.5 * (yy(0) + yy(-1))
    xx_b, xx_a = before(xx, keep_b), after(xx, keep_a)
    c[XP] = jnp.where(keep_b, 0.5 * (xx_b + xx), 0.0)
    c[XM] = jnp.where(keep_a, 0.5 * (xx_a + xx), 0.0)
    c[CENTRE] = -(c[ZP] + c[ZM] + c[YP] + c[YM] + (xx + 0.5 * (xx_a + xx_b)))
    zp, zm, yp, ym = window(3, 1, 0), window(3, -1, 0), window(3, 0, 1), window(3, 0, -1)
    c[ZPYP], c[ZPYM] = 0.25 * (zp + yp), -0.25 * (zp + ym)
    c[ZMYP], c[ZMYM] = -0.25 * (zm + yp), 0.25 * (zm + ym)
    for comp, plus, minus, names in (
        (4, window(4, 1, 0), window(4, -1, 0), (XPZP, XPZM, XMZP, XMZM)),
        (5, window(5, 0, 1), window(5, 0, -1), (XPYP, XPYM, XMYP, XMYM)),
    ):
        here = window(comp, 0, 0)
        c[names[0]] = jnp.where(keep_b, 0.25 * (before(plus, keep_b) + here), 0.0)
        c[names[1]] = jnp.where(keep_b, -0.25 * (before(minus, keep_b) + here), 0.0)
        c[names[2]] = jnp.where(keep_a, -0.25 * (after(plus, keep_a) + here), 0.0)
        c[names[3]] = jnp.where(keep_a, 0.25 * (after(minus, keep_a) + here), 0.0)
    return c


def stencil(c, u, reach=(-1, 0, 1)):
    near = {(dz, dy): u(dz, dy) for dz in reach for dy in (-1, 0, 1)}
    sums = []
    for group in GROUPS:
        value = None
        for j, dz, dy in group:
            if dz in reach:
                term = c[j] * near[dz, dy]
                value = term if value is None else value + term
        sums.append(value)
    here, right, left = sums
    width = here.shape[-1]
    return here + pltpu.roll(right, width - 1, axis=1) + pltpu.roll(left, 1, axis=1)


def scale_of(conc):
    root = jnp.sqrt(conc)
    return DT * root / (root + 0.5)


def slope_of(conc):
    root = jnp.sqrt(conc)
    return (0.25 * DT) / (root * (root + 0.5) * (root + 0.5))


def planes_kernel(count, *refs):
    owner = refs[0]
    parts, states = refs[1 : 1 + count], refs[1 + count : 1 + 2 * count]
    coef, gain, scale, ends, full, conc = refs[1 + 2 * count :]
    depth, rows_y, rows_x = coef.shape[1:]
    rows = rows_y // count
    slots = states[0].shape[0]
    me = lax.axis_index("sens")
    inner = pl.ds(PAD, rows_y)

    blank = jnp.zeros((PAD, rows_x), jnp.float32)
    void = jnp.zeros((rows_y + 2 * PAD, rows_x), jnp.float32)
    for ref in (full, conc):
        for i in range(ref.shape[0]):
            ref[i, 0] = void
            ref[i, depth + 1] = void
            for z in range(depth):
                ref[i, z + 1, pl.ds(0, PAD)] = blank
                ref[i, z + 1, pl.ds(PAD + rows_y, PAD)] = blank
    for k in range(count):
        who = lax.rem(me - k + count, count)
        span = pl.ds(pl.multiple_of(PAD + who * rows, PAD), rows)
        for comp in range(6):
            for z in range(depth):
                full[comp, z + 1, span] = parts[k][comp, z]
    for i in range(STEPS):
        turn = lax.rem(me - lax.div(owner[i], slots) + count, count)
        slot = lax.rem(owner[i], slots)
        for k in range(count):

            @pl.when(turn == k)
            def _(i=i, k=k, slot=slot):
                conc[i, pl.ds(1, depth), inner] = states[k][slot]

        for side in range(2):
            ends[i, side] = conc[i, 1 + side * (depth - 1), inner]

    keep_b, keep_a = lane_masks((TILE, rows_x))

    def layer(z, carry):
        for tile in range(rows_y // TILE):
            at = pl.ds(tile * TILE, TILE)

            def window(comp, dz, dy):
                return full[comp, z + 1 + dz, pl.ds(PAD + tile * TILE + dy, TILE)]

            c = planes_at(window, keep_b, keep_a)
            for j in range(PLANES):
                coef[j, z, at] = c[j]
            for i in range(STEPS):
                here = conc[i, z + 1, pl.ds(PAD + tile * TILE, TILE)]
                spread = stencil(
                    c, lambda dz, dy: conc[i, z + 1 + dz, pl.ds(PAD + tile * TILE + dy, TILE)]
                )
                scale[i, z, at] = scale_of(here)
                gain[i, z, at] = 1.0 + slope_of(here) * spread
        return carry

    lax.fori_loop(0, depth, layer, 0)


def planes(owner, parts, states):
    count = len(parts)
    depth, rows_y, rows_x = states[0].shape[1:]
    grown = rows_y + 2 * PAD
    return pl.pallas_call(
        functools.partial(planes_kernel, count),
        in_specs=[SMEM] + [VMEM] * (2 * count),
        out_specs=[VMEM] * 4,
        out_shape=[
            f32(PLANES, depth, rows_y, rows_x),
            f32(STEPS, depth, rows_y, rows_x),
            f32(STEPS, depth, rows_y, rows_x),
            f32(STEPS, 2, rows_y, rows_x),
        ],
        scratch_shapes=[
            pltpu.VMEM((6, depth + 2, grown, rows_x), jnp.float32),
            pltpu.VMEM((STEPS, depth + 2, grown, rows_x), jnp.float32),
        ],
        compiler_params=params(24),
        cost_estimate=cost(2_000_000_000, 60_000_000),
        name="planes",
    )(owner, *parts, *states)


def ends_kernel(count, slots, *refs):
    owner, coef, ends = refs[:3]
    small = refs[3 : 3 + count], refs[3 + count : 3 + 2 * count]
    edge, edge_raw, corr, tensor, conc = refs[3 + 2 * count :]
    depth, rows_y, rows_x = coef.shape[1:]
    rows = rows_y // count
    me = lax.axis_index("sens")
    side_a = 1 - parity()
    inner = pl.ds(PAD, rows_y)
    blank = jnp.zeros((PAD, rows_x), jnp.float32)
    for side in range(2):
        for i in range(STEPS):
            conc[side, i, pl.ds(0, PAD)] = blank
            conc[side, i, pl.ds(PAD + rows_y, PAD)] = blank
    for k in range(count):
        who = lax.rem(me - k + count, count)
        span = pl.ds(pl.multiple_of(who * rows, PAD), rows)
        for j in range(3):
            here = pl.ds(2 * rows_y + j * rows, rows)
            tensor[side_a, j, span] = small[0][k][here]
            tensor[1 - side_a, j, span] = small[1][k][here]
    holders = [lax.div(owner[i], slots) for i in range(STEPS)]
    for i in range(STEPS):
        slot = jnp.int32(0)
        for j in range(i):
            slot += jnp.where(holders[j] == holders[i], 1, 0)
        slot = jnp.minimum(slot, 1)
        turn = lax.rem(me - holders[i] + count, count)
        for k in range(count):

            @pl.when(turn == k)
            def _(i=i, k=k, slot=slot):
                span = pl.ds(pl.multiple_of(slot * rows_y, PAD), rows_y)
                conc[side_a, i, inner] = small[0][k][span]
                conc[1 - side_a, i, inner] = small[1][k][span]

    keep_b, keep_a = lane_masks((TILE, rows_x))
    ys = lax.broadcasted_iota(jnp.int32, (TILE, rows_x), 0)
    for side, z, names in ((0, 0, LOW), (1, depth - 1, HIGH)):
        sign = 2 * side - 1
        for tile in range(rows_y // TILE):
            at = pl.ds(tile * TILE, TILE)
            zz, zy, zx = (tensor[side, j, at] for j in range(3))
            e = [coef[names[j], z, at] for j in range(5)]
            e[0] += 0.5 * zz
            e[1] += (0.25 * sign) * zy
            e[2] -= (0.25 * sign) * zy
            e[3] += (0.25 * sign) * before(zx, keep_b)
            e[4] -= (0.25 * sign) * after(zx, keep_a)
            if tile == rows_y // TILE - 1:
                e[1] = jnp.where(ys < TILE - 1, e[1], 0.0)
            if tile == 0:
                e[2] = jnp.where(ys > 0, e[2], 0.0)
            near = [
                [conc[side, i, pl.ds(PAD + tile * TILE + d, TILE)] for d in (0, 1, -1)]
                for i in range(STEPS)
            ]
            for j in range(5):
                edge[side, j, at] = e[j]
                edge_raw[side, j, at] = e[j] * scale_of(near[STEPS - 1][(0, 1, 2, 0, 0)[j]])
            for i in range(STEPS):
                here, up, down = near[i]
                own = ends[i, side, at]
                spread = e[0] * here + e[1] * up + e[2] * down - 0.5 * zz * own
                spread += pltpu.roll(e[3] * here, rows_x - 1, axis=1)
                spread += pltpu.roll(e[4] * here, 1, axis=1)
                gain, scale = slope_of(own) * spread, scale_of(own)
                if i == STEPS - 1:
                    corr[i, side, at] = gain - 0.5 * zz * scale
                else:
                    corr[i, side, at] = gain / scale - 0.5 * zz


def ends_call(owner, coef, ends, small_a, small_b, slots):
    count = len(small_a)
    _, _, rows_y, rows_x = coef.shape
    return pl.pallas_call(
        functools.partial(ends_kernel, count, slots),
        in_specs=[SMEM] + [VMEM] * (2 + 2 * count),
        out_specs=[VMEM] * 3,
        out_shape=[
            f32(2, 5, rows_y, rows_x),
            f32(2, 5, rows_y, rows_x),
            f32(STEPS, 2, rows_y, rows_x),
        ],
        scratch_shapes=[
            pltpu.VMEM((2, 3, rows_y, rows_x), jnp.float32),
            pltpu.VMEM((2, STEPS, rows_y + 2 * PAD, rows_x), jnp.float32),
        ],
        compiler_params=params(16),
        cost_estimate=cost(1_000_000, 1_000_000),
        name="ends",
    )(owner, coef, ends, *small_a, *small_b)


def gather_field(first, lam, lam_a, lam_b, mu):
    own, depth = mu.shape[:2]
    for k in range(own):
        for z in range(depth):
            if first or 0 < z < depth - 1:
                mu[k, z] = lam[k, z]
    if not first:
        z_a = jnp.where(parity() == 0, depth - 1, 0)
        for k in range(own):
            mu[k, z_a] = lam_a[k]
            mu[k, depth - 1 - z_a] = lam_b[k]


def add_misfit(step, sensors, misfit, mu, skip=0):
    own, depth, rows_y, rows_x = mu.shape
    plane = rows_y * rows_x
    start = lax.axis_index("space") * (depth * plane)
    lanes = lax.broadcasted_iota(jnp.int32, (1, rows_x), 1)
    for k in range(own):
        lifted, z, y, x = spot(sensors[k], start, rows_y, rows_x)

        @pl.when((lifted >= (1 + skip) * plane) & (lifted < (depth + 1 - skip) * plane))
        def _(k=k, z=z, y=y, x=x):
            mu[k, z, pl.ds(y, 1), :] += jnp.where(lanes == x, misfit[step, k], 0.0)


def scale_field(scale, step, mu, v):
    own, depth, rows_y, rows_x = mu.shape
    blank = jnp.zeros((PAD, rows_x), jnp.float32)
    void = jnp.zeros((rows_y + 2 * PAD, rows_x), jnp.float32)
    for k in range(own):
        v[k, 0] = void
        v[k, depth + 1] = void
        for z in range(depth):
            v[k, z + 1, pl.ds(0, PAD)] = blank
            v[k, z + 1, pl.ds(PAD + rows_y, PAD)] = blank
            v[k, z + 1, pl.ds(PAD, rows_y)] = scale[step, z] * mu[k, z]


def spread_field(coef, gain, step, mu, v, part, part_edges=None, skip=0):
    own, depth, rows_y, rows_x = mu.shape
    for z in range(depth):
        reach = [dz for dz in (-1, 0, 1) if skip <= z + dz < depth - skip]
        used = {j for group in GROUPS for j, dz, _ in group if dz in reach}
        for tile in range(rows_y // TILE):
            at = pl.ds(tile * TILE, TILE)
            c = {j: coef[j, z, at] for j in sorted(used)}
            keep = gain[step, z, at]
            for k in range(own):
                value = stencil(
                    c, lambda dz, dy: v[k, z + 1 + dz, pl.ds(PAD + tile * TILE + dy, TILE)], reach
                )
                if 0 in reach:
                    value += mu[k, z, at] * keep
                part[k, z, at] = value
    if part_edges is not None:
        for k in range(own):
            part_edges[0, k] = part[k, 0]
            part_edges[1, k] = part[k, depth - 1]


def taker(total, own, rows_x):
    lanes = lax.broadcasted_iota(jnp.int32, (1, rows_x), 1)
    slots = lax.broadcasted_iota(jnp.int32, (own, total.shape[1]), 1)

    def take(r, x, row):
        value = jnp.sum(jnp.where(lanes == x, row, 0.0), axis=-1, keepdims=True)
        total[...] += jnp.where(slots == r, value, 0.0)

    return take


def collect(wanted, release, shape, total, own_row):
    cells, steps, inside = release
    own, depth, rows_y, rows_x = shape
    start = lax.axis_index("space") * (depth * rows_y * rows_x)
    take = taker(total, own, rows_x)

    def visit(i, carry):
        r = inside[i]
        _, z, y, x = spot(cells[r], start, rows_y, rows_x)

        @pl.when((steps[r] == wanted) & (z >= 0) & (z < depth))
        def _():
            take(r, x, own_row(z, y))

        return carry

    lax.fori_loop(0, inside[inside.shape[0] - 1], visit, 0)


def list_releases(cells, shape, inside):
    own, depth, rows_y, rows_x = shape
    plane = rows_y * rows_x
    start = lax.axis_index("space") * (depth * plane)

    def note(r, found):
        local = cells[r] - start
        inside[found] = r
        return found + jnp.where((local >= -plane) & (local < (depth + 1) * plane), 1, 0)

    inside[inside.shape[0] - 1] = lax.fori_loop(0, cells.shape[0], note, jnp.int32(0))


def rows_of(ref, *index):
    row = ref[(slice(None), *index, slice(None))]
    return row.reshape(row.shape[0], row.shape[-1])


def first_kernel(sensors, misfit, lam, coef, gain, scale, part, part_edges, v, mu):
    gather_field(True, lam, None, None, mu)
    add_misfit(STEPS - 1, sensors, misfit, mu)
    scale_field(scale, STEPS - 1, mu, v)
    spread_field(coef, gain, STEPS - 1, mu, v, part, part_edges)


def middle_kernel(
    sensors, misfit, cells, steps, lam, lam_a, lam_b, coef, gain, scale, base, part_edges, grad, inside, v, mu, part
):
    own, depth, rows_y, rows_x = mu.shape
    gather_field(False, lam, lam_a, lam_b, mu)
    grad[...] = jnp.zeros_like(grad)
    list_releases(cells, mu.shape, inside)
    release = (cells, steps, inside)
    collect(2, release, mu.shape, grad, lambda z, y: rows_of(mu, z, pl.ds(y, 1)))
    add_misfit(1, sensors, misfit, mu)
    scale_field(scale, 1, mu, v)
    spread_field(coef, gain, 1, mu, v, part, part_edges)

    void = jnp.zeros((rows_y, rows_x), jnp.float32)
    for k in range(own):
        mu[k, 0] = void
        mu[k, depth - 1] = void
        for z in range(1, depth - 1):
            mu[k, z] = part[k, z]
    collect(1, release, mu.shape, grad, lambda z, y: rows_of(mu, z, pl.ds(y, 1)))
    add_misfit(0, sensors, misfit, mu, 1)
    scale_field(scale, 0, mu, v)
    spread_field(coef, gain, 0, mu, v, base, skip=1)

    def own_row(z, y):
        at = pl.ds(y, 1)
        c = [coef[j, z, at] for j in range(PLANES)]
        spread = stencil(c, lambda dz, dy: rows_of(v, z + 1 + dz, pl.ds(PAD + y + dy, 1)))
        return rows_of(mu, z, at) * gain[0, z, at] + spread

    collect(0, release, mu.shape, grad, own_row)


def in_layer(c, here, up, down):
    width = here.shape[-1]
    value = c[0] * here + c[1] * up + c[2] * down
    right = c[3] * here + c[4] * up + c[5] * down
    left = c[6] * here + c[7] * up + c[8] * down
    return value + pltpu.roll(right, width - 1, axis=1) + pltpu.roll(left, 1, axis=1)


def front_kernel(
    cells, steps, inside, grad_in, lam_a, lam_b, sent_a, sent_b, coef, edge, corr, gain, scale, grads, ve, total
):
    own, rows_y, rows_x = lam_a.shape
    depth = coef.shape[1]
    start = lax.axis_index("space") * (depth * rows_y * rows_x)
    side_a = 1 - parity()
    blank = jnp.zeros((PAD, rows_x), jnp.float32)
    for k in range(own):
        for side in range(2):
            ve[side, k, pl.ds(0, PAD)] = blank
            ve[side, k, pl.ds(PAD + rows_y, PAD)] = blank
        ve[side_a, k, pl.ds(PAD, rows_y)] = sent_a[k]
        ve[1 - side_a, k, pl.ds(PAD, rows_y)] = sent_b[k]
    total[...] = grad_in[...]
    take = taker(total, own, rows_x)

    def visit(i, carry):
        r = inside[i]
        _, z, y, x = spot(cells[r], start, rows_y, rows_x)
        step = steps[r]
        at = pl.ds(y, 1)
        for lam, side in ((lam_a, side_a), (lam_b, 1 - side_a)):

            @pl.when((step == 1) & (z == side * (depth - 1)))
            def _(lam=lam):
                take(r, x, rows_of(lam, at))

        for side, names in ((0, LOW), (1, HIGH)):
            out = 2 * side - 1
            end = side * (depth - 1)

            def near(side=side):
                return [rows_of(ve.at[side], pl.ds(PAD + y + d, 1)) for d in (0, 1, -1)]

            @pl.when((step == 0) & (z == end))
            def _(side=side, end=end, near=near):
                here, up, down = near()
                value = in_layer([coef[j, end, at] for j in IN_LAYER], here, up, down)
                keep = gain[0, end, at] / scale[0, end, at] + corr[0, side, at]
                take(r, x, value + keep * here)

            @pl.when((step == 0) & (z == end - out))
            def _(end=end, out=out, names=names, near=near):
                take(r, x, from_met([coef[j, end - out, at] for j in names], *near()))

            @pl.when((step == 0) & (z == end + out))
            def _(side=side, near=near):
                here, up, down = near()
                value = edge[side, 0, at] * here
                value += edge[side, 1, pl.ds(jnp.maximum(y - 1, 0), 1)] * down
                value += edge[side, 2, pl.ds(jnp.minimum(y + 1, rows_y - 1), 1)] * up
                value += edge[side, 3, at] * pltpu.roll(here, 1, axis=1)
                value += edge[side, 4, at] * pltpu.roll(here, rows_x - 1, axis=1)
                take(r, x, value)

        return carry

    lax.fori_loop(0, inside[inside.shape[0] - 1], visit, 0)
    for i in range(grads.shape[0]):
        grads[i] = total[...]


def field_call(kernel, name, args, specs, outs, scratch, flops, listed=0):
    return pl.pallas_call(
        kernel,
        in_specs=specs,
        out_specs=[VMEM] * len(outs) + [SMEM] * (listed > 0),
        out_shape=outs + [jax.ShapeDtypeStruct((listed,), jnp.int32)] * (listed > 0),
        scratch_shapes=[pltpu.VMEM(o.shape, jnp.float32) for o in scratch],
        compiler_params=params(32),
        cost_estimate=cost(flops, 4_000_000),
        name=name,
    )(*args)


def met(got, k, tile, tiles):
    here = got[k, pl.ds(tile * TILE, TILE)]
    if tile == tiles - 1:
        up = pltpu.roll(here, TILE - 1, axis=0)
    else:
        up = got[k, pl.ds(tile * TILE + 1, TILE)]
    if tile == 0:
        down = pltpu.roll(here, 1, axis=0)
    else:
        down = got[k, pl.ds(tile * TILE - 1, TILE)]
    return here, up, down


def from_met(c, here, up, down):
    width = here.shape[-1]
    value = c[0] * here + c[1] * up + c[2] * down
    value += pltpu.roll(c[3] * here, width - 1, axis=1)
    return value + pltpu.roll(c[4] * here, 1, axis=1)


def rim_kernel(step, late, sensors, misfit, part_edges, got, sent, edge, corr, scale, lam, send):
    depth = scale.shape[1]
    own, rows_y, rows_x = got.shape
    tiles = rows_y // TILE
    side = parity() if late else 1 - parity()
    z = side * (depth - 1)
    for tile in range(tiles):
        at = pl.ds(tile * TILE, TILE)
        c = [edge[side, j, at] for j in range(5)]
        miss = corr[step, side, at]
        gain = scale[step - 1, z, at]
        for k in range(own):
            value = part_edges[side, k, at] + miss * sent[k, at]
            value += from_met(c, *met(got, k, tile, tiles))
            lam[k, at] = value
            send[k, at] = gain * value
    plane = rows_y * rows_x
    first = (lax.axis_index("space") * depth + z) * plane
    lanes = lax.broadcasted_iota(jnp.int32, (1, rows_x), 1)
    for k in range(own):
        local = sensors[k] - first

        @pl.when((local >= 0) & (local < plane))
        def _(k=k, local=local):
            y, x = lax.div(local, rows_x), lax.rem(local, rows_x)
            add = jnp.where(lanes == x, misfit[step - 1, k], 0.0)
            send[k, pl.ds(y, 1), :] += add * scale[step - 1, z, pl.ds(y, 1), :]


def rim(step, late, sensors, misfit, part_edges, got, sent, edge, corr, scale):
    return pl.pallas_call(
        functools.partial(rim_kernel, step, late),
        in_specs=[SMEM] * 2 + [VMEM] * 6,
        out_specs=[VMEM] * 2,
        out_shape=[f32(*got.shape)] * 2,
        compiler_params=params(16),
        cost_estimate=cost(2_000_000, 1_500_000),
        name=f"rim{step}{'b' if late else 'a'}",
    )(sensors, misfit, part_edges, got, sent, edge, corr, scale)


def last_kernel(base, ve, coef, gain, scale, got_a, got_b, edge, corr, grads, out, grad, part, sems):
    own, depth, rows_y, rows_x = base.shape
    tiles = rows_y // TILE
    copies = [
        pltpu.make_async_copy(base.at[:, z], out.at[:, z], sems.at[z]) for z in range(2, depth - 2)
    ]
    for c in copies:
        c.start()
    side_a = 1 - parity()
    for turn, (got, side) in enumerate(((got_b, 1 - side_a), (got_a, side_a))):
        end = side * (depth - 1)
        inner = end + 1 - 2 * side
        for tile in range(tiles):
            at = pl.ds(tile * TILE, TILE)
            ce = [coef[j, end, at] for j in IN_LAYER]
            ci = [coef[jnp.where(side == 0, low, high), inner, at] for low, high in zip(LOW, HIGH)]
            cm = [edge[side, j, at] for j in range(5)]
            keep = gain[0, end, at] / scale[0, end, at] + corr[0, side, at]
            for k in range(own):
                here, up, down = (
                    ve[side, k, pl.ds(PAD + tile * TILE + d, TILE)] for d in (0, 1, -1)
                )
                value = base[k, end, at] + keep * here + in_layer(ce, here, up, down)
                part[k, end, at] = value + from_met(cm, *met(got, k, tile, tiles))
                part[k, inner, at] = base[k, inner, at] + from_met(ci, here, up, down)
        for z, sem in ((end, turn), (inner, depth - 1 - turn)):
            copies.append(pltpu.make_async_copy(part.at[:, z], out.at[:, z], sems.at[sem]))
            copies[-1].start()
    total = grads[0]
    for i in range(1, grads.shape[0]):
        total += grads[i]
    grad[...] = total
    for c in copies:
        c.wait()


def last_call(base, ve, coef, gain, scale, got_a, got_b, edge, corr, grads):
    return pl.pallas_call(
        last_kernel,
        in_specs=[VMEM] * 10,
        out_specs=[ANY, VMEM],
        out_shape=[f32(*base.shape), f32(*grads.shape[1:])],
        scratch_shapes=[
            pltpu.VMEM(base.shape, jnp.float32),
            pltpu.SemaphoreType.DMA((base.shape[1],)),
        ],
        compiler_params=params(16),
        cost_estimate=cost(10_000_000, 6_000_000),
        name="step0",
    )(base, ve, coef, gain, scale, got_a, got_b, edge, corr, grads)


def turned(array, axis):
    count = lax.axis_size(axis)
    return [array] + [
        lax.ppermute(array, axis, [(i, (i + k) % count) for i in range(count)])
        for k in range(1, count)
    ]


def body(
    adjoint_end,
    checkpoints,
    dispersion,
    owner_steps,
    sensor_cells,
    misfit,
    release_cells,
    release_steps,
):
    own, depth, rows_y, rows_x = adjoint_end.shape
    slabs = lax.axis_size("space")
    pairs_a = [(i, i ^ 1) for i in range(slabs)]
    pairs_b = [(i, ((i + 1) ^ 1) - 1) for i in range(1, slabs - 1)]
    misfit = misfit.T

    def swap_a(x):
        return lax.ppermute(x, "space", pairs_a)

    def swap_b(x):
        return lax.ppermute(x, "space", pairs_b)

    parts, states = turned(dispersion, "sens"), turned(checkpoints, "sens")
    sent_a, sent_b, small_a, small_b = pack(
        owner_steps, sensor_cells, misfit, adjoint_end, checkpoints, dispersion
    )
    small_a, small_b = swap_a(small_a), swap_b(small_b)
    parts, states, sent_a, sent_b = lax.optimization_barrier((parts, states, sent_a, sent_b))
    got_a, got_b = swap_a(sent_a), swap_b(sent_b)
    small_a, small_b, parts = lax.optimization_barrier((small_a, small_b, parts))
    small_a, small_b = turned(small_a, "sens"), turned(small_b, "sens")
    coef, gain, scale, ends = planes(owner_steps, parts, states)

    field = f32(own, depth, rows_y, rows_x)
    edges = f32(2, own, rows_y, rows_x)
    tall = f32(own, depth + 2, rows_y + 2 * PAD, rows_x)
    kept = f32(own, release_cells.shape[0])
    sensors = (sensor_cells, misfit)
    release = (release_cells, release_steps)

    part, part_edges = field_call(
        first_kernel,
        "step2",
        (*sensors, adjoint_end, coef, gain, scale),
        [SMEM] * 2 + [VMEM, VMEM, VMEM, VMEM],
        [field, edges],
        [tall, field],
        40_000_000,
    )
    small_a, small_b, part_edges = lax.optimization_barrier((small_a, small_b, part_edges))
    edge, edge_raw, corr = ends_call(
        owner_steps, coef, ends, small_a, small_b, checkpoints.shape[0]
    )
    lam_b, send_b = rim(2, True, *sensors, part_edges, got_b, sent_b, edge_raw, corr, scale)
    got_b = swap_b(send_b)
    lam_a, send_a = rim(2, False, *sensors, part_edges, got_a, sent_a, edge_raw, corr, scale)
    got_a = swap_a(send_a)
    base, part_edges, grad, inside = field_call(
        middle_kernel,
        "step1",
        (*sensors, *release, part, lam_a, lam_b, coef, gain, scale),
        [SMEM] * 4 + [VMEM] * 6,
        [field, edges, kept],
        [tall, field, field],
        40_000_000,
        release_cells.shape[0] + 1,
    )
    sent_a, sent_b = send_a, send_b
    lam_b, send_b = rim(1, True, *sensors, part_edges, got_b, sent_b, edge, corr, scale)
    got_b = swap_b(send_b)
    lam_a, send_a = rim(1, False, *sensors, part_edges, got_a, sent_a, edge, corr, scale)
    got_a = swap_a(send_a)
    halo = f32(2, own, rows_y + 2 * PAD, rows_x)
    grads, ve = field_call(
        front_kernel,
        "front0",
        (*release, inside, grad, lam_a, lam_b, send_a, send_b, coef, edge, corr, gain, scale),
        [SMEM] * 3 + [VMEM] * 10,
        [f32(slabs, *kept.shape), halo],
        [kept],
        10_000_000,
    )
    grads = lax.all_to_all(grads, "space", 0, 0, tiled=True)
    grads, ve = lax.optimization_barrier((grads, ve))
    return tuple(last_call(base, ve, coef, gain, scale, got_a, got_b, edge, corr, grads))


def solution(mesh):
    in_specs = (
        P("sens", "space", None, None),
        P("sens", "space", None, None),
        P(None, "space", "sens", None),
        P(),
        P("sens"),
        P("sens", None),
        P(),
        P(),
    )
    out_specs = (P("sens", "space", None, None), P("sens", None))
    return jax.shard_map(body, mesh=mesh, in_specs=in_specs, out_specs=out_specs, check_vma=False)
```

```python
import functools

import jax
import jax.numpy as jnp
from jax import lax
from jax.experimental import pallas as pl
from jax.experimental.pallas import tpu as pltpu
from jax.sharding import PartitionSpec as P

STEPS = 3
DT = 0.12
PAD = 8
TILE = 8
CENTRE, ZP, ZM, YP, YM, ZPYP, ZPYM, ZMYP, ZMYM = range(9)
XP, XPZP, XPZM, XPYP, XPYM, XM, XMZP, XMZM, XMYP, XMYM = range(9, 19)
PLANES = 19
LOW = (ZM, ZMYP, ZMYM, XPZM, XMZM)
HIGH = (ZP, ZPYP, ZPYM, XPZP, XMZP)
GROUPS = (
    (
        (CENTRE, 0, 0),
        (ZP, 1, 0),
        (ZM, -1, 0),
        (YP, 0, 1),
        (YM, 0, -1),
        (ZPYP, 1, 1),
        (ZPYM, 1, -1),
        (ZMYP, -1, 1),
        (ZMYM, -1, -1),
    ),
    ((XP, 0, 0), (XPZP, 1, 0), (XPZM, -1, 0), (XPYP, 0, 1), (XPYM, 0, -1)),
    ((XM, 0, 0), (XMZP, 1, 0), (XMZM, -1, 0), (XMYP, 0, 1), (XMYM, 0, -1)),
)
IN_LAYER = (CENTRE, YP, YM, XP, XPYP, XPYM, XM, XMYP, XMYM)

VMEM = pl.BlockSpec(memory_space=pltpu.VMEM)
SMEM = pl.BlockSpec(memory_space=pltpu.SMEM)
ANY = pl.BlockSpec(memory_space=pl.ANY)


def f32(*shape):
    return jax.ShapeDtypeStruct(shape, jnp.float32)


def params(mib):
    return pltpu.CompilerParams(vmem_limit_bytes=mib * 1024 * 1024)


def cost(flops, moved):
    return pl.CostEstimate(flops=flops, bytes_accessed=moved, transcendentals=0)


def owned(owner_ref, slots):
    me = lax.axis_index("sens")
    o0, o1, o2 = (owner_ref[i] for i in range(3))
    own0 = lax.div(o0, slots) == me
    own1 = lax.div(o1, slots) == me
    first = jnp.where(own0, o0, jnp.where(own1, o1, o2))
    second = jnp.where(own0 & own1, o1, o2)
    return lax.rem(first, slots), lax.rem(second, slots)


def parity():
    return lax.rem(lax.axis_index("space"), 2)


def spot(cell, start, rows_y, rows_x):
    local = cell - start
    lifted = local + rows_y * rows_x
    z = lax.div(lifted, rows_y * rows_x) - 1
    y = lax.div(lax.rem(lifted, rows_y * rows_x), rows_x)
    return lifted, z, y, lax.rem(lifted, rows_x)


def pack_kernel(
    owner, sensors, misfit, adj, ckpt, disp, lam_a, lam_b, small_a, small_b, sems
):
    own, depth, rows_y, rows_x = adj.shape
    rows = disp.shape[2]
    plane = rows_y * rows_x
    start = lax.axis_index("space") * (depth * plane)
    even = parity() == 0
    z_a = jnp.where(even, depth - 1, 0)
    z_b = jnp.where(even, 0, depth - 1)
    held = owned(owner, ckpt.shape[0])
    moves = [(adj.at[:, z_a], lam_a), (adj.at[:, z_b], lam_b)]
    for z, small in ((z_a, small_a), (z_b, small_b)):
        for j in range(2):
            moves.append((ckpt.at[held[j], z], small.at[pl.ds(j * rows_y, rows_y)]))
        for j, comp in enumerate((0, 3, 4)):
            moves.append((disp.at[comp, z], small.at[pl.ds(2 * rows_y + j * rows, rows)]))
    copies = [pltpu.make_async_copy(s, d, sems.at[i]) for i, (s, d) in enumerate(moves)]
    for c in copies:
        c.start()

    lanes = lax.broadcasted_iota(jnp.int32, (1, rows_x), 1)
    for c in copies[:2]:
        c.wait()
    for k in range(own):
        lifted, z, y, x = spot(sensors[k], start, rows_y, rows_x)
        mine = (lifted >= plane) & (lifted < (depth + 1) * plane)

        for edge, lam in ((z_a, lam_a), (z_b, lam_b)):

            @pl.when(mine & (z == edge))
            def _(k=k, y=y, x=x, lam=lam):
                lam[k, pl.ds(y, 1), :] += jnp.where(lanes == x, misfit[STEPS - 1, k], 0.0)

    for c in copies[2:]:
        c.wait()


def pack(owner, sensors, misfit, adj, ckpt, disp):
    own, depth, rows_y, rows_x = adj.shape
    rows = disp.shape[2]
    small = f32(2 * rows_y + 3 * rows, rows_x)
    return pl.pallas_call(
        pack_kernel,
        in_specs=[SMEM] * 3 + [ANY] * 3,
        out_specs=[VMEM] * 4,
        out_shape=[f32(own, rows_y, rows_x)] * 2 + [small, small],
        scratch_shapes=[pltpu.SemaphoreType.DMA((12,))],
        compiler_params=params(56),
        cost_estimate=cost(20_000_000_000, 60_000_000),
        name="pack",
    )(owner, sensors, misfit, adj, ckpt, disp)


def lane_masks(shape):
    lanes = lax.broadcasted_iota(jnp.int32, shape, len(shape) - 1)
    return lanes >= 1, lanes < shape[-1] - 1


def before(value, keep):
    return jnp.where(keep, pltpu.roll(value, 1, axis=value.ndim - 1), 0.0)


def after(value, keep):
    return jnp.where(keep, pltpu.roll(value, value.shape[-1] - 1, axis=value.ndim - 1), 0.0)


def planes_at(window, keep_b, keep_a):
    def yy(dy):
        return window(1, 0, dy)

    c = [None] * PLANES
    zz, zzp, zzm = window(0, 0, 0), window(0, 1, 0), window(0, -1, 0)
    xx = window(2, 0, 0)
    c[ZP], c[ZM] = 0.5 * (zz + zzp), 0.5 * (zz + zzm)
    c[YP], c[YM] = 0.5 * (yy(0) + yy(1)), 0.5 * (yy(0) + yy(-1))
    xx_b, xx_a = before(xx, keep_b), after(xx, keep_a)
    c[XP] = jnp.where(keep_b, 0.5 * (xx_b + xx), 0.0)
    c[XM] = jnp.where(keep_a, 0.5 * (xx_a + xx), 0.0)
    c[CENTRE] = -(c[ZP] + c[ZM] + c[YP] + c[YM] + (xx + 0.5 * (xx_a + xx_b)))
    zp, zm, yp, ym = window(3, 1, 0), window(3, -1, 0), window(3, 0, 1), window(3, 0, -1)
    c[ZPYP], c[ZPYM] = 0.25 * (zp + yp), -0.25 * (zp + ym)
    c[ZMYP], c[ZMYM] = -0.25 * (zm + yp), 0.25 * (zm + ym)
    for comp, plus, minus, names in (
        (4, window(4, 1, 0), window(4, -1, 0), (XPZP, XPZM, XMZP, XMZM)),
        (5, window(5, 0, 1), window(5, 0, -1), (XPYP, XPYM, XMYP, XMYM)),
    ):
        here = window(comp, 0, 0)
        c[names[0]] = jnp.where(keep_b, 0.25 * (before(plus, keep_b) + here), 0.0)
        c[names[1]] = jnp.where(keep_b, -0.25 * (before(minus, keep_b) + here), 0.0)
        c[names[2]] = jnp.where(keep_a, -0.25 * (after(plus, keep_a) + here), 0.0)
        c[names[3]] = jnp.where(keep_a, 0.25 * (after(minus, keep_a) + here), 0.0)
    return c


def stencil(c, u, reach=(-1, 0, 1)):
    near = {(dz, dy): u(dz, dy) for dz in reach for dy in (-1, 0, 1)}
    sums = []
    for group in GROUPS:
        value = None
        for j, dz, dy in group:
            if dz in reach:
                term = c[j] * near[dz, dy]
                value = term if value is None else value + term
        sums.append(value)
    here, right, left = sums
    width = here.shape[-1]
    return here + pltpu.roll(right, width - 1, axis=1) + pltpu.roll(left, 1, axis=1)


def scale_of(conc):
    root = jnp.sqrt(conc)
    return DT * root / (root + 0.5)


def slope_of(conc):
    root = jnp.sqrt(conc)
    return (0.25 * DT) / (root * (root + 0.5) * (root + 0.5))


def planes_kernel(count, *refs):
    owner = refs[0]
    parts, states = refs[1 : 1 + count], refs[1 + count : 1 + 2 * count]
    coef, gain, scale, ends, full, conc = refs[1 + 2 * count :]
    depth, rows_y, rows_x = coef.shape[1:]
    rows = rows_y // count
    slots = states[0].shape[0]
    me = lax.axis_index("sens")
    inner = pl.ds(PAD, rows_y)

    blank = jnp.zeros((PAD, rows_x), jnp.float32)
    void = jnp.zeros((rows_y + 2 * PAD, rows_x), jnp.float32)
    for ref in (full, conc):
        for i in range(ref.shape[0]):
            ref[i, 0] = void
            ref[i, depth + 1] = void
            for z in range(depth):
                ref[i, z + 1, pl.ds(0, PAD)] = blank
                ref[i, z + 1, pl.ds(PAD + rows_y, PAD)] = blank
    for k in range(count):
        who = lax.rem(me - k + count, count)
        span = pl.ds(pl.multiple_of(PAD + who * rows, PAD), rows)
        for comp in range(6):
            for z in range(depth):
                full[comp, z + 1, span] = parts[k][comp, z]
    for i in range(STEPS):
        turn = lax.rem(me - lax.div(owner[i], slots) + count, count)
        slot = lax.rem(owner[i], slots)
        for k in range(count):

            @pl.when(turn == k)
            def _(i=i, k=k, slot=slot):
                conc[i, pl.ds(1, depth), inner] = states[k][slot]

        for side in range(2):
            ends[i, side] = conc[i, 1 + side * (depth - 1), inner]

    keep_b, keep_a = lane_masks((TILE, rows_x))

    def layer(z, carry):
        for tile in range(rows_y // TILE):
            at = pl.ds(tile * TILE, TILE)

            def window(comp, dz, dy):
                return full[comp, z + 1 + dz, pl.ds(PAD + tile * TILE + dy, TILE)]

            c = planes_at(window, keep_b, keep_a)
            for j in range(PLANES):
                coef[j, z, at] = c[j]
            for i in range(STEPS):
                here = conc[i, z + 1, pl.ds(PAD + tile * TILE, TILE)]
                spread = stencil(
                    c, lambda dz, dy: conc[i, z + 1 + dz, pl.ds(PAD + tile * TILE + dy, TILE)]
                )
                scale[i, z, at] = scale_of(here)
                gain[i, z, at] = 1.0 + slope_of(here) * spread
        return carry

    lax.fori_loop(0, depth, layer, 0)


def planes(owner, parts, states):
    count = len(parts)
    depth, rows_y, rows_x = states[0].shape[1:]
    grown = rows_y + 2 * PAD
    return pl.pallas_call(
        functools.partial(planes_kernel, count),
        in_specs=[SMEM] + [VMEM] * (2 * count),
        out_specs=[VMEM] * 4,
        out_shape=[
            f32(PLANES, depth, rows_y, rows_x),
            f32(STEPS, depth, rows_y, rows_x),
            f32(STEPS, depth, rows_y, rows_x),
            f32(STEPS, 2, rows_y, rows_x),
        ],
        scratch_shapes=[
            pltpu.VMEM((6, depth + 2, grown, rows_x), jnp.float32),
            pltpu.VMEM((STEPS, depth + 2, grown, rows_x), jnp.float32),
        ],
        compiler_params=params(24),
        cost_estimate=cost(2_000_000_000, 60_000_000),
        name="planes",
    )(owner, *parts, *states)


def ends_kernel(count, slots, *refs):
    owner, coef, gains, scales, ends = refs[:5]
    small = refs[5 : 5 + count], refs[5 + count : 5 + 2 * count]
    edge, edge_raw, corr, tail, tensor, conc = refs[5 + 2 * count :]
    depth, rows_y, rows_x = coef.shape[1:]
    rows = rows_y // count
    me = lax.axis_index("sens")
    side_a = 1 - parity()
    inner = pl.ds(PAD, rows_y)
    blank = jnp.zeros((PAD, rows_x), jnp.float32)
    for side in range(2):
        for i in range(STEPS):
            conc[side, i, pl.ds(0, PAD)] = blank
            conc[side, i, pl.ds(PAD + rows_y, PAD)] = blank
    for k in range(count):
        who = lax.rem(me - k + count, count)
        span = pl.ds(pl.multiple_of(who * rows, PAD), rows)
        for j in range(3):
            here = pl.ds(2 * rows_y + j * rows, rows)
            tensor[side_a, j, span] = small[0][k][here]
            tensor[1 - side_a, j, span] = small[1][k][here]
    holders = [lax.div(owner[i], slots) for i in range(STEPS)]
    for i in range(STEPS):
        slot = jnp.int32(0)
        for j in range(i):
            slot += jnp.where(holders[j] == holders[i], 1, 0)
        slot = jnp.minimum(slot, 1)
        turn = lax.rem(me - holders[i] + count, count)
        for k in range(count):

            @pl.when(turn == k)
            def _(i=i, k=k, slot=slot):
                span = pl.ds(pl.multiple_of(slot * rows_y, PAD), rows_y)
                conc[side_a, i, inner] = small[0][k][span]
                conc[1 - side_a, i, inner] = small[1][k][span]

    keep_b, keep_a = lane_masks((TILE, rows_x))
    ys = lax.broadcasted_iota(jnp.int32, (TILE, rows_x), 0)
    for side, z, names in ((0, 0, LOW), (1, depth - 1, HIGH)):
        sign = 2 * side - 1
        for tile in range(rows_y // TILE):
            at = pl.ds(tile * TILE, TILE)
            zz, zy, zx = (tensor[side, j, at] for j in range(3))
            e = [coef[names[j], z, at] for j in range(5)]
            e[0] += 0.5 * zz
            e[1] += (0.25 * sign) * zy
            e[2] -= (0.25 * sign) * zy
            e[3] += (0.25 * sign) * before(zx, keep_b)
            e[4] -= (0.25 * sign) * after(zx, keep_a)
            if tile == rows_y // TILE - 1:
                e[1] = jnp.where(ys < TILE - 1, e[1], 0.0)
            if tile == 0:
                e[2] = jnp.where(ys > 0, e[2], 0.0)
            near = [
                [conc[side, i, pl.ds(PAD + tile * TILE + d, TILE)] for d in (0, 1, -1)]
                for i in range(STEPS)
            ]
            for j in range(5):
                edge[side, j, at] = e[j]
                edge_raw[side, j, at] = e[j] * scale_of(near[STEPS - 1][(0, 1, 2, 0, 0)[j]])
            for i in range(STEPS):
                here, up, down = near[i]
                own = ends[i, side, at]
                spread = e[0] * here + e[1] * up + e[2] * down - 0.5 * zz * own
                spread += pltpu.roll(e[3] * here, rows_x - 1, axis=1)
                spread += pltpu.roll(e[4] * here, 1, axis=1)
                gain, scale = slope_of(own) * spread, scale_of(own)
                if i == STEPS - 1:
                    corr[i, side, at] = gain - 0.5 * zz * scale
                else:
                    corr[i, side, at] = gain / scale - 0.5 * zz
                    if i == 0:
                        keep = gains[0, z, at] / scales[0, z, at]
                        tail[side, 14, at] = keep + (gain / scale - 0.5 * zz)
            rows_in = [(name, z) for name in IN_LAYER] + [(name, z - sign) for name in names]
            for j, (name, layer) in enumerate(rows_in):
                value = coef[name, layer, at]
                if tile == rows_y // TILE - 1 and j in (1, 4, 7, 10):
                    value = jnp.where(ys < TILE - 1, value, 0.0)
                if tile == 0 and j in (2, 5, 8, 11):
                    value = jnp.where(ys > 0, value, 0.0)
                tail[side, j, at] = value


def ends_call(owner, coef, gain, scale, ends, small_a, small_b, slots):
    count = len(small_a)
    _, _, rows_y, rows_x = coef.shape
    return pl.pallas_call(
        functools.partial(ends_kernel, count, slots),
        in_specs=[SMEM] + [VMEM] * (4 + 2 * count),
        out_specs=[VMEM] * 4,
        out_shape=[
            f32(2, 5, rows_y, rows_x),
            f32(2, 5, rows_y, rows_x),
            f32(STEPS, 2, rows_y, rows_x),
            f32(2, 15, rows_y, rows_x),
        ],
        scratch_shapes=[
            pltpu.VMEM((2, 3, rows_y, rows_x), jnp.float32),
            pltpu.VMEM((2, STEPS, rows_y + 2 * PAD, rows_x), jnp.float32),
        ],
        compiler_params=params(16),
        cost_estimate=cost(1_000_000, 1_000_000),
        name="ends",
    )(owner, coef, gain, scale, ends, *small_a, *small_b)


def gather_field(first, lam, lam_a, lam_b, mu):
    own, depth = mu.shape[:2]
    for k in range(own):
        for z in range(depth):
            if first or 0 < z < depth - 1:
                mu[k, z] = lam[k, z]
    if not first:
        z_a = jnp.where(parity() == 0, depth - 1, 0)
        for k in range(own):
            mu[k, z_a] = lam_a[k]
            mu[k, depth - 1 - z_a] = lam_b[k]


def add_misfit(step, sensors, misfit, mu, skip=0):
    own, depth, rows_y, rows_x = mu.shape
    plane = rows_y * rows_x
    start = lax.axis_index("space") * (depth * plane)
    lanes = lax.broadcasted_iota(jnp.int32, (1, rows_x), 1)
    for k in range(own):
        lifted, z, y, x = spot(sensors[k], start, rows_y, rows_x)

        @pl.when((lifted >= (1 + skip) * plane) & (lifted < (depth + 1 - skip) * plane))
        def _(k=k, z=z, y=y, x=x):
            mu[k, z, pl.ds(y, 1), :] += jnp.where(lanes == x, misfit[step, k], 0.0)


def scale_field(scale, step, mu, v):
    own, depth, rows_y, rows_x = mu.shape
    blank = jnp.zeros((PAD, rows_x), jnp.float32)
    void = jnp.zeros((rows_y + 2 * PAD, rows_x), jnp.float32)
    for k in range(own):
        v[k, 0] = void
        v[k, depth + 1] = void
        for z in range(depth):
            v[k, z + 1, pl.ds(0, PAD)] = blank
            v[k, z + 1, pl.ds(PAD + rows_y, PAD)] = blank
            v[k, z + 1, pl.ds(PAD, rows_y)] = scale[step, z] * mu[k, z]


def spread_field(coef, gain, step, mu, v, part, part_edges=None, skip=0):
    own, depth, rows_y, rows_x = mu.shape
    for z in range(depth):
        reach = [dz for dz in (-1, 0, 1) if skip <= z + dz < depth - skip]
        used = {j for group in GROUPS for j, dz, _ in group if dz in reach}
        for tile in range(rows_y // TILE):
            at = pl.ds(tile * TILE, TILE)
            c = {j: coef[j, z, at] for j in sorted(used)}
            keep = gain[step, z, at]
            for k in range(own):
                value = stencil(
                    c, lambda dz, dy: v[k, z + 1 + dz, pl.ds(PAD + tile * TILE + dy, TILE)], reach
                )
                if 0 in reach:
                    value += mu[k, z, at] * keep
                part[k, z, at] = value
    if part_edges is not None:
        for k in range(own):
            part_edges[0, k] = part[k, 0]
            part_edges[1, k] = part[k, depth - 1]


def taker(total, own, rows_x):
    lanes = lax.broadcasted_iota(jnp.int32, (1, rows_x), 1)
    slots = lax.broadcasted_iota(jnp.int32, (own, total.shape[1]), 1)

    def take(r, x, row):
        value = jnp.sum(jnp.where(lanes == x, row, 0.0), axis=-1, keepdims=True)
        total[...] += jnp.where(slots == r, value, 0.0)

    return take


def collect(wanted, release, shape, total, own_row):
    cells, steps, inside = release
    own, depth, rows_y, rows_x = shape
    start = lax.axis_index("space") * (depth * rows_y * rows_x)
    take = taker(total, own, rows_x)

    def visit(i, carry):
        r = inside[i]
        _, z, y, x = spot(cells[r], start, rows_y, rows_x)

        @pl.when((steps[r] == wanted) & (z >= 0) & (z < depth))
        def _():
            take(r, x, own_row(z, y))

        return carry

    lax.fori_loop(0, inside[inside.shape[0] - 1], visit, 0)


def list_releases(cells, shape, inside):
    own, depth, rows_y, rows_x = shape
    plane = rows_y * rows_x
    start = lax.axis_index("space") * (depth * plane)

    def note(r, found):
        local = cells[r] - start
        inside[found] = r
        return found + jnp.where((local >= -plane) & (local < (depth + 1) * plane), 1, 0)

    inside[inside.shape[0] - 1] = lax.fori_loop(0, cells.shape[0], note, jnp.int32(0))


def rows_of(ref, *index):
    row = ref[(slice(None), *index, slice(None))]
    return row.reshape(row.shape[0], row.shape[-1])


def first_kernel(sensors, misfit, lam, coef, gain, scale, part, part_edges, v, mu):
    gather_field(True, lam, None, None, mu)
    add_misfit(STEPS - 1, sensors, misfit, mu)
    scale_field(scale, STEPS - 1, mu, v)
    spread_field(coef, gain, STEPS - 1, mu, v, part, part_edges)


def middle_kernel(
    sensors, misfit, cells, steps, lam, lam_a, lam_b, coef, gain, scale, base, part_edges, grad, inside, v, mu, part
):
    own, depth, rows_y, rows_x = mu.shape
    gather_field(False, lam, lam_a, lam_b, mu)
    grad[...] = jnp.zeros_like(grad)
    list_releases(cells, mu.shape, inside)
    release = (cells, steps, inside)
    collect(2, release, mu.shape, grad, lambda z, y: rows_of(mu, z, pl.ds(y, 1)))
    add_misfit(1, sensors, misfit, mu)
    scale_field(scale, 1, mu, v)
    spread_field(coef, gain, 1, mu, v, part, part_edges)

    void = jnp.zeros((rows_y, rows_x), jnp.float32)
    for k in range(own):
        mu[k, 0] = void
        mu[k, depth - 1] = void
        for z in range(1, depth - 1):
            mu[k, z] = part[k, z]
    collect(1, release, mu.shape, grad, lambda z, y: rows_of(mu, z, pl.ds(y, 1)))
    add_misfit(0, sensors, misfit, mu, 1)
    scale_field(scale, 0, mu, v)
    spread_field(coef, gain, 0, mu, v, base, skip=1)

    def own_row(z, y):
        at = pl.ds(y, 1)
        c = [coef[j, z, at] for j in range(PLANES)]
        spread = stencil(c, lambda dz, dy: rows_of(v, z + 1 + dz, pl.ds(PAD + y + dy, 1)))
        return rows_of(mu, z, at) * gain[0, z, at] + spread

    collect(0, release, mu.shape, grad, own_row)


def in_layer(c, here, up, down):
    width = here.shape[-1]
    value = c[0] * here + c[1] * up + c[2] * down
    right = c[3] * here + c[4] * up + c[5] * down
    left = c[6] * here + c[7] * up + c[8] * down
    return value + pltpu.roll(right, width - 1, axis=1) + pltpu.roll(left, 1, axis=1)


def front_kernel(
    cells, steps, inside, grad_in, lam_a, lam_b, sent_a, sent_b, coef, edge, corr, gain, scale, grads, total, ve
):
    own, rows_y, rows_x = lam_a.shape
    depth = coef.shape[1]
    start = lax.axis_index("space") * (depth * rows_y * rows_x)
    side_a = 1 - parity()
    blank = jnp.zeros((PAD, rows_x), jnp.float32)
    for k in range(own):
        for side in range(2):
            ve[side, k, pl.ds(0, PAD)] = blank
            ve[side, k, pl.ds(PAD + rows_y, PAD)] = blank
        ve[side_a, k, pl.ds(PAD, rows_y)] = sent_a[k]
        ve[1 - side_a, k, pl.ds(PAD, rows_y)] = sent_b[k]
    total[...] = grad_in[...]
    take = taker(total, own, rows_x)

    def visit(i, carry):
        r = inside[i]
        _, z, y, x = spot(cells[r], start, rows_y, rows_x)
        step = steps[r]
        at = pl.ds(y, 1)
        for lam, side in ((lam_a, side_a), (lam_b, 1 - side_a)):

            @pl.when((step == 1) & (z == side * (depth - 1)))
            def _(lam=lam):
                take(r, x, rows_of(lam, at))

        for side, names in ((0, LOW), (1, HIGH)):
            out = 2 * side - 1
            end = side * (depth - 1)

            def near(side=side):
                return [rows_of(ve.at[side], pl.ds(PAD + y + d, 1)) for d in (0, 1, -1)]

            @pl.when((step == 0) & (z == end))
            def _(side=side, end=end, near=near):
                here, up, down = near()
                value = in_layer([coef[j, end, at] for j in IN_LAYER], here, up, down)
                keep = gain[0, end, at] / scale[0, end, at] + corr[0, side, at]
                take(r, x, value + keep * here)

            @pl.when((step == 0) & (z == end - out))
            def _(end=end, out=out, names=names, near=near):
                take(r, x, from_met([coef[j, end - out, at] for j in names], *near()))

            @pl.when((step == 0) & (z == end + out))
            def _(side=side, near=near):
                here, up, down = near()
                value = edge[side, 0, at] * here
                value += edge[side, 1, pl.ds(jnp.maximum(y - 1, 0), 1)] * down
                value += edge[side, 2, pl.ds(jnp.minimum(y + 1, rows_y - 1), 1)] * up
                value += edge[side, 3, at] * pltpu.roll(here, 1, axis=1)
                value += edge[side, 4, at] * pltpu.roll(here, rows_x - 1, axis=1)
                take(r, x, value)

        return carry

    lax.fori_loop(0, inside[inside.shape[0] - 1], visit, 0)
    for i in range(grads.shape[0]):
        grads[i] = total[...]


def field_call(kernel, name, args, specs, outs, scratch, flops, listed=0):
    return pl.pallas_call(
        kernel,
        in_specs=specs,
        out_specs=[VMEM] * len(outs) + [SMEM] * (listed > 0),
        out_shape=outs + [jax.ShapeDtypeStruct((listed,), jnp.int32)] * (listed > 0),
        scratch_shapes=[pltpu.VMEM(o.shape, jnp.float32) for o in scratch],
        compiler_params=params(32),
        cost_estimate=cost(flops, 4_000_000),
        name=name,
    )(*args)


def met(got, k, tile, tiles):
    here = got[k, pl.ds(tile * TILE, TILE)]
    if tile == tiles - 1:
        up = pltpu.roll(here, TILE - 1, axis=0)
    else:
        up = got[k, pl.ds(tile * TILE + 1, TILE)]
    if tile == 0:
        down = pltpu.roll(here, 1, axis=0)
    else:
        down = got[k, pl.ds(tile * TILE - 1, TILE)]
    return here, up, down


def from_met(c, here, up, down):
    width = here.shape[-1]
    value = c[0] * here + c[1] * up + c[2] * down
    value += pltpu.roll(c[3] * here, width - 1, axis=1)
    return value + pltpu.roll(c[4] * here, 1, axis=1)


def rim_kernel(step, late, sensors, misfit, part_edges, got, sent, edge, corr, scale, lam, send):
    depth = scale.shape[1]
    own, rows_y, rows_x = got.shape
    tiles = rows_y // TILE
    side = parity() if late else 1 - parity()
    z = side * (depth - 1)
    for tile in range(tiles):
        at = pl.ds(tile * TILE, TILE)
        c = [edge[side, j, at] for j in range(5)]
        miss = corr[step, side, at]
        gain = scale[step - 1, z, at]
        for k in range(own):
            value = part_edges[side, k, at] + miss * sent[k, at]
            value += from_met(c, *met(got, k, tile, tiles))
            lam[k, at] = value
            send[k, at] = gain * value
    plane = rows_y * rows_x
    first = (lax.axis_index("space") * depth + z) * plane
    lanes = lax.broadcasted_iota(jnp.int32, (1, rows_x), 1)
    for k in range(own):
        local = sensors[k] - first

        @pl.when((local >= 0) & (local < plane))
        def _(k=k, local=local):
            y, x = lax.div(local, rows_x), lax.rem(local, rows_x)
            add = jnp.where(lanes == x, misfit[step - 1, k], 0.0)
            send[k, pl.ds(y, 1), :] += add * scale[step - 1, z, pl.ds(y, 1), :]


def rim(step, late, sensors, misfit, part_edges, got, sent, edge, corr, scale):
    return pl.pallas_call(
        functools.partial(rim_kernel, step, late),
        in_specs=[SMEM] * 2 + [VMEM] * 6,
        out_specs=[VMEM] * 2,
        out_shape=[f32(*got.shape)] * 2,
        compiler_params=params(16),
        cost_estimate=cost(2_000_000, 1_500_000),
        name=f"rim{step}{'b' if late else 'a'}",
    )(sensors, misfit, part_edges, got, sent, edge, corr, scale)


def last_kernel(base, sent_a, sent_b, tail, got_a, got_b, edge, out, part, sems):
    own, depth, rows_y, rows_x = base.shape
    tiles = rows_y // TILE
    copies = [
        pltpu.make_async_copy(base.at[:, z], out.at[:, z], sems.at[z]) for z in range(2, depth - 2)
    ]
    for c in copies:
        c.start()
    side_a = 1 - parity()
    pairs = ((got_b, sent_b, 1 - side_a), (got_a, sent_a, side_a))
    for turn, (got, sent, side) in enumerate(pairs):
        end = side * (depth - 1)
        inner = end + 1 - 2 * side
        for tile in range(tiles):
            at = pl.ds(tile * TILE, TILE)
            ce = [tail[side, j, at] for j in range(9)]
            ci = [tail[side, 9 + j, at] for j in range(5)]
            cm = [edge[side, j, at] for j in range(5)]
            keep = tail[side, 14, at]
            for k in range(own):
                here, up, down = met(sent, k, tile, tiles)
                value = base[k, end, at] + keep * here + in_layer(ce, here, up, down)
                part[k, end, at] = value + from_met(cm, *met(got, k, tile, tiles))
                part[k, inner, at] = base[k, inner, at] + from_met(ci, here, up, down)
        for z, sem in ((end, turn), (inner, depth - 1 - turn)):
            copies.append(pltpu.make_async_copy(part.at[:, z], out.at[:, z], sems.at[sem]))
            copies[-1].start()
    for c in copies:
        c.wait()


def last_call(base, sent_a, sent_b, tail, got_a, got_b, edge):
    return pl.pallas_call(
        last_kernel,
        in_specs=[VMEM] * 7,
        out_specs=ANY,
        out_shape=f32(*base.shape),
        scratch_shapes=[
            pltpu.VMEM(base.shape, jnp.float32),
            pltpu.SemaphoreType.DMA((base.shape[1],)),
        ],
        compiler_params=params(16),
        cost_estimate=cost(10_000_000, 6_000_000),
        name="step0",
    )(base, sent_a, sent_b, tail, got_a, got_b, edge)


def turned(array, axis):
    count = lax.axis_size(axis)
    return [array] + [
        lax.ppermute(array, axis, [(i, (i + k) % count) for i in range(count)])
        for k in range(1, count)
    ]


def body(
    adjoint_end,
    checkpoints,
    dispersion,
    owner_steps,
    sensor_cells,
    misfit,
    release_cells,
    release_steps,
):
    own, depth, rows_y, rows_x = adjoint_end.shape
    slabs = lax.axis_size("space")
    pairs_a = [(i, i ^ 1) for i in range(slabs)]
    pairs_b = [(i, ((i + 1) ^ 1) - 1) for i in range(1, slabs - 1)]
    misfit = misfit.T

    def swap_a(x):
        return lax.ppermute(x, "space", pairs_a)

    def swap_b(x):
        return lax.ppermute(x, "space", pairs_b)

    parts, states = turned(dispersion, "sens"), turned(checkpoints, "sens")
    sent_a, sent_b, small_a, small_b = pack(
        owner_steps, sensor_cells, misfit, adjoint_end, checkpoints, dispersion
    )
    small_a, small_b = swap_a(small_a), swap_b(small_b)
    parts, states, sent_a, sent_b = lax.optimization_barrier((parts, states, sent_a, sent_b))
    got_a, got_b = swap_a(sent_a), swap_b(sent_b)
    small_a, small_b, parts = lax.optimization_barrier((small_a, small_b, parts))
    small_a, small_b = turned(small_a, "sens"), turned(small_b, "sens")
    coef, gain, scale, ends = planes(owner_steps, parts, states)

    field = f32(own, depth, rows_y, rows_x)
    edges = f32(2, own, rows_y, rows_x)
    tall = f32(own, depth + 2, rows_y + 2 * PAD, rows_x)
    kept = f32(own, release_cells.shape[0])
    sensors = (sensor_cells, misfit)
    release = (release_cells, release_steps)

    part, part_edges = field_call(
        first_kernel,
        "step2",
        (*sensors, adjoint_end, coef, gain, scale),
        [SMEM] * 2 + [VMEM, VMEM, VMEM, VMEM],
        [field, edges],
        [tall, field],
        40_000_000,
    )
    small_a, small_b, part_edges = lax.optimization_barrier((small_a, small_b, part_edges))
    edge, edge_raw, corr, tail = ends_call(
        owner_steps, coef, gain, scale, ends, small_a, small_b, checkpoints.shape[0]
    )
    lam_b, send_b = rim(2, True, *sensors, part_edges, got_b, sent_b, edge_raw, corr, scale)
    got_b = swap_b(send_b)
    lam_a, send_a = rim(2, False, *sensors, part_edges, got_a, sent_a, edge_raw, corr, scale)
    got_a = swap_a(send_a)
    base, part_edges, grad, inside = field_call(
        middle_kernel,
        "step1",
        (*sensors, *release, part, lam_a, lam_b, coef, gain, scale),
        [SMEM] * 4 + [VMEM] * 6,
        [field, edges, kept],
        [tall, field, field],
        40_000_000,
        release_cells.shape[0] + 1,
    )
    sent_a, sent_b = send_a, send_b
    lam_b, send_b = rim(1, True, *sensors, part_edges, got_b, sent_b, edge, corr, scale)
    got_b = swap_b(send_b)
    lam_a, send_a = rim(1, False, *sensors, part_edges, got_a, sent_a, edge, corr, scale)
    got_a = swap_a(send_a)
    halo = f32(2, own, rows_y + 2 * PAD, rows_x)
    (grads,) = field_call(
        front_kernel,
        "front0",
        (*release, inside, grad, lam_a, lam_b, send_a, send_b, coef, edge, corr, gain, scale),
        [SMEM] * 3 + [VMEM] * 10,
        [f32(slabs, *kept.shape)],
        [kept, halo],
        10_000_000,
    )
    grads = lax.all_to_all(grads, "space", 0, 0, tiled=True)
    lam = last_call(base, send_a, send_b, tail, got_a, got_b, edge)
    lam, grads = lax.optimization_barrier((lam, grads))
    return lam, jnp.sum(grads, axis=0)


def solution(mesh):
    in_specs = (
        P("sens", "space", None, None),
        P("sens", "space", None, None),
        P(None, "space", "sens", None),
        P(),
        P("sens"),
        P("sens", None),
        P(),
        P(),
    )
    out_specs = (P("sens", "space", None, None), P("sens", None))
    return jax.shard_map(body, mesh=mesh, in_specs=in_specs, out_specs=out_specs, check_vma=False)
```

```python
import functools

import jax
import jax.numpy as jnp
from jax import lax
from jax.experimental import pallas as pl
from jax.experimental.pallas import tpu as pltpu
from jax.sharding import PartitionSpec as P

STEPS = 3
DT = 0.12
PAD = 8
TILE = 8
CENTRE, ZP, ZM, YP, YM, ZPYP, ZPYM, ZMYP, ZMYM = range(9)
XP, XPZP, XPZM, XPYP, XPYM, XM, XMZP, XMZM, XMYP, XMYM = range(9, 19)
PLANES = 19
LOW = (ZM, ZMYP, ZMYM, XPZM, XMZM)
HIGH = (ZP, ZPYP, ZPYM, XPZP, XMZP)
GROUPS = (
    (
        (CENTRE, 0, 0),
        (ZP, 1, 0),
        (ZM, -1, 0),
        (YP, 0, 1),
        (YM, 0, -1),
        (ZPYP, 1, 1),
        (ZPYM, 1, -1),
        (ZMYP, -1, 1),
        (ZMYM, -1, -1),
    ),
    ((XP, 0, 0), (XPZP, 1, 0), (XPZM, -1, 0), (XPYP, 0, 1), (XPYM, 0, -1)),
    ((XM, 0, 0), (XMZP, 1, 0), (XMZM, -1, 0), (XMYP, 0, 1), (XMYM, 0, -1)),
)
IN_LAYER = (CENTRE, YP, YM, XP, XPYP, XPYM, XM, XMYP, XMYM)

VMEM = pl.BlockSpec(memory_space=pltpu.VMEM)
SMEM = pl.BlockSpec(memory_space=pltpu.SMEM)
ANY = pl.BlockSpec(memory_space=pl.ANY)


def f32(*shape):
    return jax.ShapeDtypeStruct(shape, jnp.float32)


def params(mib):
    return pltpu.CompilerParams(vmem_limit_bytes=mib * 1024 * 1024)


def cost(flops, moved):
    return pl.CostEstimate(flops=flops, bytes_accessed=moved, transcendentals=0)


def owned(owner_ref, slots):
    me = lax.axis_index("sens")
    o0, o1, o2 = (owner_ref[i] for i in range(3))
    own0 = lax.div(o0, slots) == me
    own1 = lax.div(o1, slots) == me
    first = jnp.where(own0, o0, jnp.where(own1, o1, o2))
    second = jnp.where(own0 & own1, o1, o2)
    return lax.rem(first, slots), lax.rem(second, slots)


def parity():
    return lax.rem(lax.axis_index("space"), 2)


def spot(cell, start, rows_y, rows_x):
    local = cell - start
    lifted = local + rows_y * rows_x
    z = lax.div(lifted, rows_y * rows_x) - 1
    y = lax.div(lax.rem(lifted, rows_y * rows_x), rows_x)
    return lifted, z, y, lax.rem(lifted, rows_x)


def pack_kernel(
    owner, sensors, misfit, adj, ckpt, disp, lam_a, lam_b, small_a, small_b, sems
):
    own, depth, rows_y, rows_x = adj.shape
    rows = disp.shape[2]
    plane = rows_y * rows_x
    start = lax.axis_index("space") * (depth * plane)
    even = parity() == 0
    z_a = jnp.where(even, depth - 1, 0)
    z_b = jnp.where(even, 0, depth - 1)
    held = owned(owner, ckpt.shape[0])
    moves = [(adj.at[:, z_a], lam_a), (adj.at[:, z_b], lam_b)]
    for z, small in ((z_a, small_a), (z_b, small_b)):
        for j in range(2):
            moves.append((ckpt.at[held[j], z], small.at[pl.ds(j * rows_y, rows_y)]))
        for j, comp in enumerate((0, 3, 4)):
            moves.append((disp.at[comp, z], small.at[pl.ds(2 * rows_y + j * rows, rows)]))
    copies = [pltpu.make_async_copy(s, d, sems.at[i]) for i, (s, d) in enumerate(moves)]
    for c in copies:
        c.start()

    lanes = lax.broadcasted_iota(jnp.int32, (1, rows_x), 1)
    for c in copies[:2]:
        c.wait()
    for k in range(own):
        lifted, z, y, x = spot(sensors[k], start, rows_y, rows_x)
        mine = (lifted >= plane) & (lifted < (depth + 1) * plane)

        for edge, lam in ((z_a, lam_a), (z_b, lam_b)):

            @pl.when(mine & (z == edge))
            def _(k=k, y=y, x=x, lam=lam):
                lam[k, pl.ds(y, 1), :] += jnp.where(lanes == x, misfit[STEPS - 1, k], 0.0)

    for c in copies[2:]:
        c.wait()


def pack(owner, sensors, misfit, adj, ckpt, disp):
    own, depth, rows_y, rows_x = adj.shape
    rows = disp.shape[2]
    small = f32(2 * rows_y + 3 * rows, rows_x)
    return pl.pallas_call(
        pack_kernel,
        in_specs=[SMEM] * 3 + [ANY] * 3,
        out_specs=[VMEM] * 4,
        out_shape=[f32(own, rows_y, rows_x)] * 2 + [small, small],
        scratch_shapes=[pltpu.SemaphoreType.DMA((12,))],
        compiler_params=params(56),
        cost_estimate=cost(20_000_000_000, 60_000_000),
        name="pack",
    )(owner, sensors, misfit, adj, ckpt, disp)


def lane_masks(shape):
    lanes = lax.broadcasted_iota(jnp.int32, shape, len(shape) - 1)
    return lanes >= 1, lanes < shape[-1] - 1


def before(value, keep):
    return jnp.where(keep, pltpu.roll(value, 1, axis=value.ndim - 1), 0.0)


def after(value, keep):
    return jnp.where(keep, pltpu.roll(value, value.shape[-1] - 1, axis=value.ndim - 1), 0.0)


def planes_at(window, keep_b, keep_a):
    def yy(dy):
        return window(1, 0, dy)

    c = [None] * PLANES
    zz, zzp, zzm = window(0, 0, 0), window(0, 1, 0), window(0, -1, 0)
    xx = window(2, 0, 0)
    c[ZP], c[ZM] = 0.5 * (zz + zzp), 0.5 * (zz + zzm)
    c[YP], c[YM] = 0.5 * (yy(0) + yy(1)), 0.5 * (yy(0) + yy(-1))
    xx_b, xx_a = before(xx, keep_b), after(xx, keep_a)
    c[XP] = jnp.where(keep_b, 0.5 * (xx_b + xx), 0.0)
    c[XM] = jnp.where(keep_a, 0.5 * (xx_a + xx), 0.0)
    c[CENTRE] = -(c[ZP] + c[ZM] + c[YP] + c[YM] + (xx + 0.5 * (xx_a + xx_b)))
    zp, zm, yp, ym = window(3, 1, 0), window(3, -1, 0), window(3, 0, 1), window(3, 0, -1)
    c[ZPYP], c[ZPYM] = 0.25 * (zp + yp), -0.25 * (zp + ym)
    c[ZMYP], c[ZMYM] = -0.25 * (zm + yp), 0.25 * (zm + ym)
    for comp, plus, minus, names in (
        (4, window(4, 1, 0), window(4, -1, 0), (XPZP, XPZM, XMZP, XMZM)),
        (5, window(5, 0, 1), window(5, 0, -1), (XPYP, XPYM, XMYP, XMYM)),
    ):
        here = window(comp, 0, 0)
        c[names[0]] = jnp.where(keep_b, 0.25 * (before(plus, keep_b) + here), 0.0)
        c[names[1]] = jnp.where(keep_b, -0.25 * (before(minus, keep_b) + here), 0.0)
        c[names[2]] = jnp.where(keep_a, -0.25 * (after(plus, keep_a) + here), 0.0)
        c[names[3]] = jnp.where(keep_a, 0.25 * (after(minus, keep_a) + here), 0.0)
    return c


def stencil(c, u, reach=(-1, 0, 1)):
    near = {(dz, dy): u(dz, dy) for dz in reach for dy in (-1, 0, 1)}
    sums = []
    for group in GROUPS:
        value = None
        for j, dz, dy in group:
            if dz in reach:
                term = c[j] * near[dz, dy]
                value = term if value is None else value + term
        sums.append(value)
    here, right, left = sums
    width = here.shape[-1]
    return here + pltpu.roll(right, width - 1, axis=1) + pltpu.roll(left, 1, axis=1)


def scale_of(conc):
    root = jnp.sqrt(conc)
    return DT * root / (root + 0.5)


def slope_of(conc):
    root = jnp.sqrt(conc)
    return (0.25 * DT) / (root * (root + 0.5) * (root + 0.5))


def planes_kernel(count, *refs):
    owner = refs[0]
    parts, states = refs[1 : 1 + count], refs[1 + count : 1 + 2 * count]
    coef, gain, scale, ends, full, conc = refs[1 + 2 * count :]
    depth, rows_y, rows_x = coef.shape[1:]
    rows = rows_y // count
    slots = states[0].shape[0]
    me = lax.axis_index("sens")
    inner = pl.ds(PAD, rows_y)

    blank = jnp.zeros((PAD, rows_x), jnp.float32)
    void = jnp.zeros((rows_y + 2 * PAD, rows_x), jnp.float32)
    for ref in (full, conc):
        for i in range(ref.shape[0]):
            ref[i, 0] = void
            ref[i, depth + 1] = void
            for z in range(depth):
                ref[i, z + 1, pl.ds(0, PAD)] = blank
                ref[i, z + 1, pl.ds(PAD + rows_y, PAD)] = blank
    for k in range(count):
        who = lax.rem(me - k + count, count)
        span = pl.ds(pl.multiple_of(PAD + who * rows, PAD), rows)
        for comp in range(6):
            for z in range(depth):
                full[comp, z + 1, span] = parts[k][comp, z]
    for i in range(STEPS):
        turn = lax.rem(me - lax.div(owner[i], slots) + count, count)
        slot = lax.rem(owner[i], slots)
        for k in range(count):

            @pl.when(turn == k)
            def _(i=i, k=k, slot=slot):
                conc[i, pl.ds(1, depth), inner] = states[k][slot]

        for side in range(2):
            ends[i, side] = conc[i, 1 + side * (depth - 1), inner]

    keep_b, keep_a = lane_masks((TILE, rows_x))

    def layer(z, carry):
        for tile in range(rows_y // TILE):
            at = pl.ds(tile * TILE, TILE)

            def window(comp, dz, dy):
                return full[comp, z + 1 + dz, pl.ds(PAD + tile * TILE + dy, TILE)]

            c = planes_at(window, keep_b, keep_a)
            for j in range(PLANES):
                coef[j, z, at] = c[j]
            for i in range(STEPS):
                here = conc[i, z + 1, pl.ds(PAD + tile * TILE, TILE)]
                spread = stencil(
                    c, lambda dz, dy: conc[i, z + 1 + dz, pl.ds(PAD + tile * TILE + dy, TILE)]
                )
                scale[i, z, at] = scale_of(here)
                gain[i, z, at] = 1.0 + slope_of(here) * spread
        return carry

    lax.fori_loop(0, depth, layer, 0)


def planes(owner, parts, states):
    count = len(parts)
    depth, rows_y, rows_x = states[0].shape[1:]
    grown = rows_y + 2 * PAD
    return pl.pallas_call(
        functools.partial(planes_kernel, count),
        in_specs=[SMEM] + [VMEM] * (2 * count),
        out_specs=[VMEM] * 4,
        out_shape=[
            f32(PLANES, depth, rows_y, rows_x),
            f32(STEPS, depth, rows_y, rows_x),
            f32(STEPS, depth, rows_y, rows_x),
            f32(STEPS, 2, rows_y, rows_x),
        ],
        scratch_shapes=[
            pltpu.VMEM((6, depth + 2, grown, rows_x), jnp.float32),
            pltpu.VMEM((STEPS, depth + 2, grown, rows_x), jnp.float32),
        ],
        compiler_params=params(24),
        cost_estimate=cost(2_000_000_000, 60_000_000),
        name="planes",
    )(owner, *parts, *states)


def ends_kernel(count, slots, *refs):
    owner, coef, gains, scales, ends = refs[:5]
    small = refs[5 : 5 + count], refs[5 + count : 5 + 2 * count]
    edge, edge_raw, corr, tail, tensor, conc = refs[5 + 2 * count :]
    depth, rows_y, rows_x = coef.shape[1:]
    rows = rows_y // count
    me = lax.axis_index("sens")
    side_a = 1 - parity()
    inner = pl.ds(PAD, rows_y)
    blank = jnp.zeros((PAD, rows_x), jnp.float32)
    for side in range(2):
        for i in range(STEPS):
            conc[side, i, pl.ds(0, PAD)] = blank
            conc[side, i, pl.ds(PAD + rows_y, PAD)] = blank
    for k in range(count):
        who = lax.rem(me - k + count, count)
        span = pl.ds(pl.multiple_of(who * rows, PAD), rows)
        for j in range(3):
            here = pl.ds(2 * rows_y + j * rows, rows)
            tensor[side_a, j, span] = small[0][k][here]
            tensor[1 - side_a, j, span] = small[1][k][here]
    holders = [lax.div(owner[i], slots) for i in range(STEPS)]
    for i in range(STEPS):
        slot = jnp.int32(0)
        for j in range(i):
            slot += jnp.where(holders[j] == holders[i], 1, 0)
        slot = jnp.minimum(slot, 1)
        turn = lax.rem(me - holders[i] + count, count)
        for k in range(count):

            @pl.when(turn == k)
            def _(i=i, k=k, slot=slot):
                span = pl.ds(pl.multiple_of(slot * rows_y, PAD), rows_y)
                conc[side_a, i, inner] = small[0][k][span]
                conc[1 - side_a, i, inner] = small[1][k][span]

    keep_b, keep_a = lane_masks((TILE, rows_x))
    ys = lax.broadcasted_iota(jnp.int32, (TILE, rows_x), 0)
    for side, z, names in ((0, 0, LOW), (1, depth - 1, HIGH)):
        sign = 2 * side - 1
        for tile in range(rows_y // TILE):
            at = pl.ds(tile * TILE, TILE)
            zz, zy, zx = (tensor[side, j, at] for j in range(3))
            e = [coef[names[j], z, at] for j in range(5)]
            e[0] += 0.5 * zz
            e[1] += (0.25 * sign) * zy
            e[2] -= (0.25 * sign) * zy
            e[3] += (0.25 * sign) * before(zx, keep_b)
            e[4] -= (0.25 * sign) * after(zx, keep_a)
            if tile == rows_y // TILE - 1:
                e[1] = jnp.where(ys < TILE - 1, e[1], 0.0)
            if tile == 0:
                e[2] = jnp.where(ys > 0, e[2], 0.0)
            near = [
                [conc[side, i, pl.ds(PAD + tile * TILE + d, TILE)] for d in (0, 1, -1)]
                for i in range(STEPS)
            ]
            for j in range(5):
                edge[side, j, at] = e[j]
                edge_raw[side, j, at] = e[j] * scale_of(near[STEPS - 1][(0, 1, 2, 0, 0)[j]])
            for i in range(STEPS):
                here, up, down = near[i]
                own = ends[i, side, at]
                spread = e[0] * here + e[1] * up + e[2] * down - 0.5 * zz * own
                spread += pltpu.roll(e[3] * here, rows_x - 1, axis=1)
                spread += pltpu.roll(e[4] * here, 1, axis=1)
                gain, scale = slope_of(own) * spread, scale_of(own)
                if i == STEPS - 1:
                    corr[i, side, at] = gain - 0.5 * zz * scale
                else:
                    corr[i, side, at] = gain / scale - 0.5 * zz
                    if i == 0:
                        keep = gains[0, z, at] / scales[0, z, at]
                        tail[side, 14, at] = keep + (gain / scale - 0.5 * zz)
            rows_in = [(name, z) for name in IN_LAYER] + [(name, z - sign) for name in names]
            for j, (name, layer) in enumerate(rows_in):
                value = coef[name, layer, at]
                if tile == rows_y // TILE - 1 and j in (1, 4, 7, 10):
                    value = jnp.where(ys < TILE - 1, value, 0.0)
                if tile == 0 and j in (2, 5, 8, 11):
                    value = jnp.where(ys > 0, value, 0.0)
                tail[side, j, at] = value


def ends_call(owner, coef, gain, scale, ends, small_a, small_b, slots):
    count = len(small_a)
    _, _, rows_y, rows_x = coef.shape
    return pl.pallas_call(
        functools.partial(ends_kernel, count, slots),
        in_specs=[SMEM] + [VMEM] * (4 + 2 * count),
        out_specs=[VMEM] * 4,
        out_shape=[
            f32(2, 5, rows_y, rows_x),
            f32(2, 5, rows_y, rows_x),
            f32(STEPS, 2, rows_y, rows_x),
            f32(2, 15, rows_y, rows_x),
        ],
        scratch_shapes=[
            pltpu.VMEM((2, 3, rows_y, rows_x), jnp.float32),
            pltpu.VMEM((2, STEPS, rows_y + 2 * PAD, rows_x), jnp.float32),
        ],
        compiler_params=params(16),
        cost_estimate=cost(1_000_000, 1_000_000),
        name="ends",
    )(owner, coef, gain, scale, ends, *small_a, *small_b)


def gather_field(first, lam, lam_a, lam_b, mu):
    own, depth = mu.shape[:2]
    for k in range(own):
        for z in range(depth):
            if first or 0 < z < depth - 1:
                mu[k, z] = lam[k, z]
    if not first:
        z_a = jnp.where(parity() == 0, depth - 1, 0)
        for k in range(own):
            mu[k, z_a] = lam_a[k]
            mu[k, depth - 1 - z_a] = lam_b[k]


def add_misfit(step, sensors, misfit, mu, skip=0):
    own, depth, rows_y, rows_x = mu.shape
    plane = rows_y * rows_x
    start = lax.axis_index("space") * (depth * plane)
    lanes = lax.broadcasted_iota(jnp.int32, (1, rows_x), 1)
    for k in range(own):
        lifted, z, y, x = spot(sensors[k], start, rows_y, rows_x)

        @pl.when((lifted >= (1 + skip) * plane) & (lifted < (depth + 1 - skip) * plane))
        def _(k=k, z=z, y=y, x=x):
            mu[k, z, pl.ds(y, 1), :] += jnp.where(lanes == x, misfit[step, k], 0.0)


def scale_field(scale, step, mu, v):
    own, depth, rows_y, rows_x = mu.shape
    blank = jnp.zeros((PAD, rows_x), jnp.float32)
    void = jnp.zeros((rows_y + 2 * PAD, rows_x), jnp.float32)
    for k in range(own):
        v[k, 0] = void
        v[k, depth + 1] = void
        for z in range(depth):
            v[k, z + 1, pl.ds(0, PAD)] = blank
            v[k, z + 1, pl.ds(PAD + rows_y, PAD)] = blank
            v[k, z + 1, pl.ds(PAD, rows_y)] = scale[step, z] * mu[k, z]


def spread_field(coef, gain, step, mu, v, part, part_edges=None, skip=0):
    own, depth, rows_y, rows_x = mu.shape
    for z in range(depth):
        reach = [dz for dz in (-1, 0, 1) if skip <= z + dz < depth - skip]
        used = {j for group in GROUPS for j, dz, _ in group if dz in reach}
        for tile in range(rows_y // TILE):
            at = pl.ds(tile * TILE, TILE)
            c = {j: coef[j, z, at] for j in sorted(used)}
            keep = gain[step, z, at]
            for k in range(own):
                value = stencil(
                    c, lambda dz, dy: v[k, z + 1 + dz, pl.ds(PAD + tile * TILE + dy, TILE)], reach
                )
                if 0 in reach:
                    value += mu[k, z, at] * keep
                part[k, z, at] = value
    if part_edges is not None:
        for k in range(own):
            part_edges[0, k] = part[k, 0]
            part_edges[1, k] = part[k, depth - 1]


def taker(total, own, rows_x):
    lanes = lax.broadcasted_iota(jnp.int32, (1, rows_x), 1)
    slots = lax.broadcasted_iota(jnp.int32, (own, total.shape[1]), 1)

    def take(r, x, row):
        value = jnp.sum(jnp.where(lanes == x, row, 0.0), axis=-1, keepdims=True)
        total[...] += jnp.where(slots == r, value, 0.0)

    return take


def collect(wanted, release, shape, total, own_row):
    cells, steps, inside = release
    own, depth, rows_y, rows_x = shape
    start = lax.axis_index("space") * (depth * rows_y * rows_x)
    take = taker(total, own, rows_x)

    def visit(i, carry):
        r = inside[i]
        _, z, y, x = spot(cells[r], start, rows_y, rows_x)

        @pl.when((steps[r] == wanted) & (z >= 0) & (z < depth))
        def _():
            take(r, x, own_row(z, y))

        return carry

    lax.fori_loop(0, inside[inside.shape[0] - 1], visit, 0)


def list_releases(cells, shape, inside):
    own, depth, rows_y, rows_x = shape
    plane = rows_y * rows_x
    start = lax.axis_index("space") * (depth * plane)

    count = cells.shape[0]
    many = 8 if count % 8 == 0 else 1

    def note(i, found):
        for j in range(many):
            r = i * many + j
            local = cells[r] - start
            inside[found] = r
            found += jnp.where((local >= -plane) & (local < (depth + 1) * plane), 1, 0)
        return found

    inside[count] = lax.fori_loop(0, count // many, note, jnp.int32(0))


def rows_of(ref, *index):
    row = ref[(slice(None), *index, slice(None))]
    return row.reshape(row.shape[0], row.shape[-1])


def first_kernel(sensors, misfit, lam, coef, gain, scale, part, part_edges, v, mu):
    gather_field(True, lam, None, None, mu)
    add_misfit(STEPS - 1, sensors, misfit, mu)
    scale_field(scale, STEPS - 1, mu, v)
    spread_field(coef, gain, STEPS - 1, mu, v, part, part_edges)


def middle_kernel(
    sensors, misfit, cells, steps, lam, lam_a, lam_b, coef, gain, scale, base, part_edges, grad, inside, v, mu, part
):
    own, depth, rows_y, rows_x = mu.shape
    gather_field(False, lam, lam_a, lam_b, mu)
    grad[...] = jnp.zeros_like(grad)
    list_releases(cells, mu.shape, inside)
    release = (cells, steps, inside)
    collect(2, release, mu.shape, grad, lambda z, y: rows_of(mu, z, pl.ds(y, 1)))
    add_misfit(1, sensors, misfit, mu)
    scale_field(scale, 1, mu, v)
    spread_field(coef, gain, 1, mu, v, part, part_edges)

    void = jnp.zeros((rows_y, rows_x), jnp.float32)
    for k in range(own):
        mu[k, 0] = void
        mu[k, depth - 1] = void
        for z in range(1, depth - 1):
            mu[k, z] = part[k, z]
    collect(1, release, mu.shape, grad, lambda z, y: rows_of(mu, z, pl.ds(y, 1)))
    add_misfit(0, sensors, misfit, mu, 1)
    scale_field(scale, 0, mu, v)
    spread_field(coef, gain, 0, mu, v, base, skip=1)

    def own_row(z, y):
        at = pl.ds(y, 1)
        c = [coef[j, z, at] for j in range(PLANES)]
        spread = stencil(c, lambda dz, dy: rows_of(v, z + 1 + dz, pl.ds(PAD + y + dy, 1)))
        return rows_of(mu, z, at) * gain[0, z, at] + spread

    collect(0, release, mu.shape, grad, own_row)


def in_layer(c, here, up, down):
    width = here.shape[-1]
    value = c[0] * here + c[1] * up + c[2] * down
    right = c[3] * here + c[4] * up + c[5] * down
    left = c[6] * here + c[7] * up + c[8] * down
    return value + pltpu.roll(right, width - 1, axis=1) + pltpu.roll(left, 1, axis=1)


def front_kernel(
    cells, steps, inside, grad_in, lam_a, lam_b, sent_a, sent_b, coef, edge, corr, gain, scale, grads, total, ve
):
    own, rows_y, rows_x = lam_a.shape
    depth = coef.shape[1]
    start = lax.axis_index("space") * (depth * rows_y * rows_x)
    side_a = 1 - parity()
    blank = jnp.zeros((PAD, rows_x), jnp.float32)
    for k in range(own):
        for side in range(2):
            ve[side, k, pl.ds(0, PAD)] = blank
            ve[side, k, pl.ds(PAD + rows_y, PAD)] = blank
        ve[side_a, k, pl.ds(PAD, rows_y)] = sent_a[k]
        ve[1 - side_a, k, pl.ds(PAD, rows_y)] = sent_b[k]
    total[...] = grad_in[...]
    take = taker(total, own, rows_x)

    def visit(i, carry):
        r = inside[i]
        _, z, y, x = spot(cells[r], start, rows_y, rows_x)
        step = steps[r]
        at = pl.ds(y, 1)
        for lam, side in ((lam_a, side_a), (lam_b, 1 - side_a)):

            @pl.when((step == 1) & (z == side * (depth - 1)))
            def _(lam=lam):
                take(r, x, rows_of(lam, at))

        for side, names in ((0, LOW), (1, HIGH)):
            out = 2 * side - 1
            end = side * (depth - 1)

            def near(side=side):
                return [rows_of(ve.at[side], pl.ds(PAD + y + d, 1)) for d in (0, 1, -1)]

            @pl.when((step == 0) & (z == end))
            def _(side=side, end=end, near=near):
                here, up, down = near()
                value = in_layer([coef[j, end, at] for j in IN_LAYER], here, up, down)
                keep = gain[0, end, at] / scale[0, end, at] + corr[0, side, at]
                take(r, x, value + keep * here)

            @pl.when((step == 0) & (z == end - out))
            def _(end=end, out=out, names=names, near=near):
                take(r, x, from_met([coef[j, end - out, at] for j in names], *near()))

            @pl.when((step == 0) & (z == end + out))
            def _(side=side, near=near):
                here, up, down = near()
                value = edge[side, 0, at] * here
                value += edge[side, 1, pl.ds(jnp.maximum(y - 1, 0), 1)] * down
                value += edge[side, 2, pl.ds(jnp.minimum(y + 1, rows_y - 1), 1)] * up
                value += edge[side, 3, at] * pltpu.roll(here, 1, axis=1)
                value += edge[side, 4, at] * pltpu.roll(here, rows_x - 1, axis=1)
                take(r, x, value)

        return carry

    lax.fori_loop(0, inside[inside.shape[0] - 1], visit, 0)
    for i in range(grads.shape[0]):
        grads[i] = total[...]


def field_call(kernel, name, args, specs, outs, scratch, flops, listed=0):
    return pl.pallas_call(
        kernel,
        in_specs=specs,
        out_specs=[VMEM] * len(outs) + [SMEM] * (listed > 0),
        out_shape=outs + [jax.ShapeDtypeStruct((listed,), jnp.int32)] * (listed > 0),
        scratch_shapes=[pltpu.VMEM(o.shape, jnp.float32) for o in scratch],
        compiler_params=params(32),
        cost_estimate=cost(flops, 4_000_000),
        name=name,
    )(*args)


def met(got, k, tile, tiles):
    here = got[k, pl.ds(tile * TILE, TILE)]
    if tile == tiles - 1:
        up = pltpu.roll(here, TILE - 1, axis=0)
    else:
        up = got[k, pl.ds(tile * TILE + 1, TILE)]
    if tile == 0:
        down = pltpu.roll(here, 1, axis=0)
    else:
        down = got[k, pl.ds(tile * TILE - 1, TILE)]
    return here, up, down


def from_met(c, here, up, down):
    width = here.shape[-1]
    value = c[0] * here + c[1] * up + c[2] * down
    value += pltpu.roll(c[3] * here, width - 1, axis=1)
    return value + pltpu.roll(c[4] * here, 1, axis=1)


def rim_kernel(step, late, sensors, misfit, part_edges, got, sent, edge, corr, scale, lam, send):
    depth = scale.shape[1]
    own, rows_y, rows_x = got.shape
    tiles = rows_y // TILE
    side = parity() if late else 1 - parity()
    z = side * (depth - 1)
    for tile in range(tiles):
        at = pl.ds(tile * TILE, TILE)
        c = [edge[side, j, at] for j in range(5)]
        miss = corr[step, side, at]
        gain = scale[step - 1, z, at]
        for k in range(own):
            value = part_edges[side, k, at] + miss * sent[k, at]
            value += from_met(c, *met(got, k, tile, tiles))
            lam[k, at] = value
            send[k, at] = gain * value
    plane = rows_y * rows_x
    first = (lax.axis_index("space") * depth + z) * plane
    lanes = lax.broadcasted_iota(jnp.int32, (1, rows_x), 1)
    for k in range(own):
        local = sensors[k] - first

        @pl.when((local >= 0) & (local < plane))
        def _(k=k, local=local):
            y, x = lax.div(local, rows_x), lax.rem(local, rows_x)
            add = jnp.where(lanes == x, misfit[step - 1, k], 0.0)
            send[k, pl.ds(y, 1), :] += add * scale[step - 1, z, pl.ds(y, 1), :]


def rim(step, late, sensors, misfit, part_edges, got, sent, edge, corr, scale):
    return pl.pallas_call(
        functools.partial(rim_kernel, step, late),
        in_specs=[SMEM] * 2 + [VMEM] * 6,
        out_specs=[VMEM] * 2,
        out_shape=[f32(*got.shape)] * 2,
        compiler_params=params(16),
        cost_estimate=cost(2_000_000, 1_500_000),
        name=f"rim{step}{'b' if late else 'a'}",
    )(sensors, misfit, part_edges, got, sent, edge, corr, scale)


def last_kernel(base, sent_a, sent_b, tail, got_a, got_b, edge, out, part, sems):
    own, depth, rows_y, rows_x = base.shape
    tiles = rows_y // TILE
    copies = [
        pltpu.make_async_copy(base.at[:, z], out.at[:, z], sems.at[z]) for z in range(2, depth - 2)
    ]
    for c in copies:
        c.start()
    side_a = 1 - parity()
    pairs = ((got_b, sent_b, 1 - side_a), (got_a, sent_a, side_a))
    for turn, (got, sent, side) in enumerate(pairs):
        end = side * (depth - 1)
        inner = end + 1 - 2 * side
        for tile in range(tiles):
            at = pl.ds(tile * TILE, TILE)
            ce = [tail[side, j, at] for j in range(9)]
            ci = [tail[side, 9 + j, at] for j in range(5)]
            cm = [edge[side, j, at] for j in range(5)]
            keep = tail[side, 14, at]
            for k in range(own):
                here, up, down = met(sent, k, tile, tiles)
                value = base[k, end, at] + keep * here + in_layer(ce, here, up, down)
                part[k, end, at] = value + from_met(cm, *met(got, k, tile, tiles))
                part[k, inner, at] = base[k, inner, at] + from_met(ci, here, up, down)
        for z, sem in ((end, turn), (inner, depth - 1 - turn)):
            copies.append(pltpu.make_async_copy(part.at[:, z], out.at[:, z], sems.at[sem]))
            copies[-1].start()
    for c in copies:
        c.wait()


def last_call(base, sent_a, sent_b, tail, got_a, got_b, edge):
    return pl.pallas_call(
        last_kernel,
        in_specs=[VMEM] * 7,
        out_specs=ANY,
        out_shape=f32(*base.shape),
        scratch_shapes=[
            pltpu.VMEM(base.shape, jnp.float32),
            pltpu.SemaphoreType.DMA((base.shape[1],)),
        ],
        compiler_params=params(16),
        cost_estimate=cost(10_000_000, 6_000_000),
        name="step0",
    )(base, sent_a, sent_b, tail, got_a, got_b, edge)


def turned(array, axis):
    count = lax.axis_size(axis)
    return [array] + [
        lax.ppermute(array, axis, [(i, (i + k) % count) for i in range(count)])
        for k in range(1, count)
    ]


def body(
    adjoint_end,
    checkpoints,
    dispersion,
    owner_steps,
    sensor_cells,
    misfit,
    release_cells,
    release_steps,
):
    own, depth, rows_y, rows_x = adjoint_end.shape
    slabs = lax.axis_size("space")
    pairs_a = [(i, i ^ 1) for i in range(slabs)]
    pairs_b = [(i, ((i + 1) ^ 1) - 1) for i in range(1, slabs - 1)]
    misfit = misfit.T

    def swap_a(x):
        return lax.ppermute(x, "space", pairs_a)

    def swap_b(x):
        return lax.ppermute(x, "space", pairs_b)

    parts, states = turned(dispersion, "sens"), turned(checkpoints, "sens")
    sent_a, sent_b, small_a, small_b = pack(
        owner_steps, sensor_cells, misfit, adjoint_end, checkpoints, dispersion
    )
    small_a, small_b = swap_a(small_a), swap_b(small_b)
    parts, states, sent_a, sent_b = lax.optimization_barrier((parts, states, sent_a, sent_b))
    got_a, got_b = swap_a(sent_a), swap_b(sent_b)
    small_a, small_b, parts = lax.optimization_barrier((small_a, small_b, parts))
    small_a, small_b = turned(small_a, "sens"), turned(small_b, "sens")
    coef, gain, scale, ends = planes(owner_steps, parts, states)

    field = f32(own, depth, rows_y, rows_x)
    edges = f32(2, own, rows_y, rows_x)
    tall = f32(own, depth + 2, rows_y + 2 * PAD, rows_x)
    kept = f32(own, release_cells.shape[0])
    sensors = (sensor_cells, misfit)
    release = (release_cells, release_steps)

    part, part_edges = field_call(
        first_kernel,
        "step2",
        (*sensors, adjoint_end, coef, gain, scale),
        [SMEM] * 2 + [VMEM, VMEM, VMEM, VMEM],
        [field, edges],
        [tall, field],
        40_000_000,
    )
    small_a, small_b, part_edges = lax.optimization_barrier((small_a, small_b, part_edges))
    edge, edge_raw, corr, tail = ends_call(
        owner_steps, coef, gain, scale, ends, small_a, small_b, checkpoints.shape[0]
    )
    lam_b, send_b = rim(2, True, *sensors, part_edges, got_b, sent_b, edge_raw, corr, scale)
    got_b = swap_b(send_b)
    lam_a, send_a = rim(2, False, *sensors, part_edges, got_a, sent_a, edge_raw, corr, scale)
    got_a = swap_a(send_a)
    base, part_edges, grad, inside = field_call(
        middle_kernel,
        "step1",
        (*sensors, *release, part, lam_a, lam_b, coef, gain, scale),
        [SMEM] * 4 + [VMEM] * 6,
        [field, edges, kept],
        [tall, field, field],
        40_000_000,
        release_cells.shape[0] + 1,
    )
    sent_a, sent_b = send_a, send_b
    lam_b, send_b = rim(1, True, *sensors, part_edges, got_b, sent_b, edge, corr, scale)
    got_b = swap_b(send_b)
    lam_a, send_a = rim(1, False, *sensors, part_edges, got_a, sent_a, edge, corr, scale)
    got_a = swap_a(send_a)
    halo = f32(2, own, rows_y + 2 * PAD, rows_x)
    (grads,) = field_call(
        front_kernel,
        "front0",
        (*release, inside, grad, lam_a, lam_b, send_a, send_b, coef, edge, corr, gain, scale),
        [SMEM] * 3 + [VMEM] * 10,
        [f32(slabs, *kept.shape)],
        [kept, halo],
        10_000_000,
    )
    grads = lax.all_to_all(grads, "space", 0, 0, tiled=True)
    lam = last_call(base, send_a, send_b, tail, got_a, got_b, edge)
    lam, grads = lax.optimization_barrier((lam, grads))
    return lam, jnp.sum(grads, axis=0)


def solution(mesh):
    in_specs = (
        P("sens", "space", None, None),
        P("sens", "space", None, None),
        P(None, "space", "sens", None),
        P(),
        P("sens"),
        P("sens", None),
        P(),
        P(),
    )
    out_specs = (P("sens", "space", None, None), P("sens", None))
    return jax.shard_map(body, mesh=mesh, in_specs=in_specs, out_specs=out_specs, check_vma=False)
```
